32 devices in a mesh: group: 4 (over y, core), dev: 8 (over z, x).
Axes of the slice: x: 2, y: 2, z: 4, core: 2. Of those that a mesh axis runs over, the one named last changes fastest.
Arguments:
- hidden: bfloat16 [8192, 8192], P('group', 'dev'), may hold values from -6 to 6
- base_in_projection: bfloat16 [8192, 8192], P('group', 'dev'), may hold values from -6 to 6
- state_input_matrix: bfloat16 [8192, 128], P(('group', 'dev')), may hold values from -0.625 to 0.625
- state_output_matrix: bfloat16 [8192, 128], P(('group', 'dev')), may hold values from -1.75 to 1.75
- head_step_size: float32 [128, 8192], P('dev', 'group'), may hold values from 0.3 to 20, as said below
- head_decay_rate: float32 [128], P('dev'), may hold values from 0.0005 to 0.05
- head_skip_scale: float32 [128], P('dev'), may hold values from 0.5 to 1.5
- convolution_weight: float32 [4, 8192], P(None, 'dev'), may hold values from -3 to 3
- convolution_bias: float32 [8192], P('dev'), may hold values from -0.5 to 0.5
- adapter_down_weight: bfloat16 [32, 64, 8192], P('group', None, 'dev'), may hold values from -0.0625 to 0.0625
- adapter_up_weight: bfloat16 [32, 64, 8192], P('group', None, 'dev'), may hold values from -0.75 to 0.75
- adapter_home_group: int32 [32, 1], replicated, may hold values from 0 to 3; in each aligned block of 8 rows (0 to 7, 8 to 15, ...) at most 4 rows name the same one
- adapter_group_index: int32 [32], replicated, may hold values from 0 to 7
- state_space_cache: bfloat16 [128, 128, 64, 128], P(('group', 'dev')), may hold values from -1.75 to 1.75
- convolution_cache: bfloat16 [128, 3, 8192], P(('group', 'dev')), may hold values from -6 to 6
- prefix_holder_device: int32 [32, 1], replicated, may hold values from 0 to 7; in each aligned block of 8 rows (0 to 7, 8 to 15, ...) at most 2 rows name the same one
- prefix_cache_slot: int32 [32], replicated, may hold values from 0 to 3
- prefix_block_count: int32 [32], replicated, may hold values from 0 to 8
Outputs:
- mixer_out: bfloat16 [8192, 8192], P('group', 'dev')
- final_state: bfloat16 [32, 128, 64, 128], P('group', 'dev')
The draws below stay inside these ranges and needn't reach their ends.
Inputs may be any that keep to these rules, and one draw needn't show every extreme that they name: `prefix_holder_device`: in each aligned block of 8 rows (one group's requests) no device index is named by more than 2 rows. `adapter_home_group`: in each aligned block of 8 rows (one group's requests) no group is named by more than 4 rows. `prefix_block_count`: 0 means that the request has no cached prefix. `head_step_size`: positive.
All inputs are finite; a program needn't handle non-finite values.
Results may differ from the reference program's by a relative error of at most 0.006.
Values may be sent and summed in bfloat16 or wider, within the bound.
No kernel may reach another device: no remote copies, remote signals or barrier semaphores. Data moves between devices by JAX's collectives and lax.ppermute only.
A program may use at most 128 MiB of HBM per device.

```python
import math
import jax
import jax.numpy as jnp
import numpy as np
from jax import lax

MODEL_WIDTH = 8192
ADAPTER_RANK = 64
MIDWAY_ATTENDERS = 128
P_SIZE = 64
N = 128
K = 4
T_REQ = 256
AD_GRP = 8
CACHE_DEV = 4
CAP = 2
ACAP = 4
MAXB = 8
MIXER_CHANNELS = 8192
REQ_GRP = 8
REQUESTS = 32
SEQUENCE_LENGTH = 8192
ADAPTER_TOTAL = 32
SLOTS = 128
N_GROUP = 4
N_DEV = 8


def draw_head_step_size(key, part):
    first, latter_portion = jax.random.split(key, 2)
    spread = jax.random.uniform(first, (MIDWAY_ATTENDERS, SEQUENCE_LENGTH), jnp.float32, -0.7, 0.7)
    frozen_mapped_vector = jnp.exp(spread)
    position_run = jax.random.randint(latter_portion, (MIDWAY_ATTENDERS, SEQUENCE_LENGTH), 0, 64) == 0
    return jnp.where(position_run, frozen_mapped_vector * 8.0, frozen_mapped_vector)


def with_ends(values, rng, low, high):
    index_at = [jax.random.randint(jax.random.fold_in(rng, axis), (), 0, length) for axis, length in enumerate(values.shape)]
    main_axis = values.shape.index(max(values.shape))
    next_to = index_at[:main_axis] + [(index_at[main_axis] + 1) % values.shape[main_axis]] + index_at[main_axis + 1:]
    return values.at[tuple(index_at)].set(low).at[tuple(next_to)].set(high)


def levels(key, extent, shards, low, high):
    def one(dim, parts):
        draws = jax.random.uniform(jax.random.fold_in(jax.random.fold_in(key, 6), dim), (parts,), jnp.float32, low / len(shards), high / len(shards))
        return jnp.repeat(jnp.exp(draws), extent[dim] // parts).reshape((-1,) + (1,) * (len(extent) - dim - 1))

    gain = one(*shards[0])
    for cut in shards[1:]:
        gain = gain * one(*cut)
    return gain


def rank_bounds(amount, lean):
    weights = [(1 << 20) // math.isqrt(standing ** lean) + 1 for standing in range(1, amount + 1)]
    width = 1 + sum(weights) // (1 << 30)
    return np.cumsum(np.array([max(1, weight // width) for weight in weights]))


def skewed_ids(stream_key, dims, number_of, slope):
    table = rank_bounds(number_of, slope)
    pick = jax.random.randint(jax.random.fold_in(stream_key, 1), dims, 0, int(table[number_of - 1]))
    grade = jnp.searchsorted(jnp.asarray(table, jnp.int32), pick, side="right")
    return jax.random.permutation(jax.random.fold_in(stream_key, 2), number_of)[grade].astype(jnp.int32)


def shared_out(rng, own, number, rows, number_of, top, limit, slope):
    sequence = jax.random.permutation(rng, number_of)
    heavy_load, ordinary = load_shares(number_of, rows * top, limit, slope, True), load_shares(number_of, rows * top, limit, slope, False)
    places = jnp.arange(number_of)

    def named(sizes, offset_by):
        used = int((sizes > 0).sum())
        fixed = max(1, used // 4)
        moved = fixed + (places - fixed + offset_by * (used - fixed)) % max(1, number_of - fixed)
        return jnp.zeros((number_of,), jnp.int32).at[sequence[jnp.where(places < fixed, places, moved)]].set(jnp.asarray(sizes, jnp.int32))

    sizes = jnp.where(number % 4 == 0, named(heavy_load, number // 4), named(ordinary, number - number // 4 - 1))
    mixed = jax.random.permutation(jax.random.fold_in(own, 3), number_of)
    donor, sink = mixed[0:number_of // 2 * 2:2], mixed[1:number_of // 2 * 2:2]
    room = jnp.minimum(sizes[donor] - 1, limit - sizes[sink]) // 2
    room = jnp.where((donor == sequence[0]) | (sink == sequence[0]) | (sizes[sink] == 0), 0, jnp.maximum(room, 0))
    moved = jax.random.randint(jax.random.fold_in(own, 4), (number_of // 2,), 0, 1 << 20) % (room + 1)
    sizes = sizes.at[donor].add(-moved).at[sink].add(moved)
    members = jnp.searchsorted(jnp.cumsum(sizes), jnp.arange(rows * top), side="right").astype(jnp.int32)
    table = members.reshape(top, rows).T
    table = table[jax.random.permutation(jax.random.fold_in(own, 1), rows)]
    offset_by = jax.random.randint(jax.random.fold_in(own, 2), (rows, 1), 0, top)
    return jnp.take_along_axis(table, (jnp.arange(top)[None, :] + offset_by) % top, axis=1)


def load_shares(amount, total, bound, lean, full):
    loads = [(1 << 20) // math.isqrt(standing ** lean) + 1 for standing in range(1, amount + 1)]
    largest = bound if full else min(bound, max(-(-total // amount), total * loads[0] // sum(loads)))
    least = 1 if total - largest >= amount - 1 else 0
    given, surplus = [largest] + [least] * (amount - 1), total - largest - least * (amount - 1)
    while surplus > 0:
        movable = [i for i in range(1, amount) if given[i] < largest] or [i for i in range(1, amount) if given[i] < bound]
        mass, remaining = sum([loads[i] for i in movable]), surplus
        for i in movable:
            more = min(bound - given[i], max(1, remaining * loads[i] // mass), surplus)
            given[i] = given[i] + more
            surplus = surplus - more
    return np.array(given)


def normal_values(key, shape, width, reach, shards=(), kind=jnp.bfloat16):
    array = jax.random.normal(key, shape, jnp.float32) * width
    if len(shards) > 0:
        array = levels(key, shape, shards, -0.22, 0.18) * array
    return jnp.clip(array, min=-reach, max=reach).astype(kind)


def setup_inputs(seed: int = 0) -> dict:
    key_list = jax.random.split(jax.random.key(seed), 19)
    hidden = normal_values(key_list[0], (SEQUENCE_LENGTH, MODEL_WIDTH), 1.0, 6.0, ((0, 4), (1, 8)))
    base_in_projection = normal_values(key_list[1], (SEQUENCE_LENGTH, MIXER_CHANNELS), 1.0, 6.0, ((0, 4), (1, 8)))
    state_input_matrix = normal_values(key_list[2], (SEQUENCE_LENGTH, N), 0.1, 0.625, ((0, 32),))
    state_output_matrix = normal_values(key_list[3], (SEQUENCE_LENGTH, N), 0.3, 1.75, ((0, 32),))
    head_step_size = draw_head_step_size(jax.random.fold_in(key_list[18], 71), 0)
    head_decay_rate = jnp.clip(jnp.exp(math.log(0.05) - 4.6051702 * jax.random.uniform(key_list[5], (MIDWAY_ATTENDERS,), jnp.float32) ** levels(key_list[5], (MIDWAY_ATTENDERS,), ((0, 8),), -0.2, 0.2)), 0.0005, 0.05)
    head_skip_scale = jnp.clip(0.5 + 1.0 * jax.random.uniform(key_list[6], (MIDWAY_ATTENDERS,), jnp.float32) ** levels(key_list[6], (MIDWAY_ATTENDERS,), ((0, 8),), -0.2, 0.2), 0.5, 1.5)
    convolution_weight = normal_values(key_list[7], (K, MIXER_CHANNELS), K ** -0.5, 3.0, ((1, 8),), jnp.float32)
    convolution_bias = jnp.clip(jax.random.uniform(key_list[8], (MIXER_CHANNELS,), jnp.float32, -0.5, 0.5) * levels(key_list[8], (MIXER_CHANNELS,), ((0, 8),), -0.4, 0.0), -0.5, 0.5)
    adapter_down_weight = normal_values(key_list[9], (ADAPTER_TOTAL, ADAPTER_RANK, MODEL_WIDTH), MODEL_WIDTH ** -0.5, 0.0625, ((0, 4), (2, 8)))
    adapter_up_weight = normal_values(key_list[10], (ADAPTER_TOTAL, ADAPTER_RANK, MIXER_CHANNELS), ADAPTER_RANK ** -0.5, 0.75, ((0, 4), (2, 8)))
    adapter_home_group_keys = jax.random.split(jax.random.fold_in(key_list[11], 1), REQUESTS // REQ_GRP)
    adapter_home_group_turns = jax.random.permutation(jax.random.fold_in(key_list[11], 3), REQUESTS // REQ_GRP)
    adapter_home_group = jax.vmap(lambda own, number: shared_out(jax.random.fold_in(key_list[11], 2), own, number, REQ_GRP, N_GROUP, 1, ACAP, 2))(adapter_home_group_keys, adapter_home_group_turns).reshape((REQUESTS, 1))
    adapter_group_index = with_ends(skewed_ids(key_list[12], (REQUESTS,), AD_GRP, 2), jax.random.fold_in(key_list[12], 3), 0, AD_GRP - 1).astype(jnp.int32)
    state_space_cache = normal_values(key_list[13], (SLOTS, MIDWAY_ATTENDERS, P_SIZE, N), 0.3, 1.75, ((0, 32),))
    convolution_cache = normal_values(key_list[14], (SLOTS, K - 1, MIXER_CHANNELS), 1.0, 6.0, ((0, 32),))
    prefix_holder_device_keys = jax.random.split(jax.random.fold_in(key_list[15], 1), REQUESTS // REQ_GRP)
    prefix_holder_device_turns = jax.random.permutation(jax.random.fold_in(key_list[15], 3), REQUESTS // REQ_GRP)
    prefix_holder_device = jax.vmap(lambda own, number: shared_out(jax.random.fold_in(key_list[15], 2), own, number, REQ_GRP, N_DEV, 1, CAP, 2))(prefix_holder_device_keys, prefix_holder_device_turns).reshape((REQUESTS, 1))
    prefix_cache_slot = with_ends(jax.random.randint(key_list[16], (REQUESTS,), 0, CACHE_DEV), jax.random.fold_in(key_list[16], 1), 0, CACHE_DEV - 1).astype(jnp.int32)
    prefix_block_count = with_ends(jax.random.randint(key_list[17], (REQUESTS,), 0, MAXB + 1), jax.random.fold_in(key_list[17], 1), 0, MAXB).astype(jnp.int32)
    return {"hidden": hidden, "base_in_projection": base_in_projection, "state_input_matrix": state_input_matrix, "state_output_matrix": state_output_matrix, "head_step_size": head_step_size, "head_decay_rate": head_decay_rate, "head_skip_scale": head_skip_scale, "convolution_weight": convolution_weight, "convolution_bias": convolution_bias, "adapter_down_weight": adapter_down_weight, "adapter_up_weight": adapter_up_weight, "adapter_home_group": adapter_home_group, "adapter_group_index": adapter_group_index, "state_space_cache": state_space_cache, "convolution_cache": convolution_cache, "prefix_holder_device": prefix_holder_device, "prefix_cache_slot": prefix_cache_slot, "prefix_block_count": prefix_block_count}


def conv_activate(prev_conv, lifted_rows, convolution_weight, convolution_bias):
    tap_count = convolution_weight.shape[0]
    length = lifted_rows.shape[-2]
    extended = jnp.concatenate([prev_conv.astype(jnp.float32), lifted_rows], axis=-2)
    summed = convolution_bias.astype(jnp.float32)
    for offset in range(tap_count):
        summed = summed + convolution_weight[offset] * lax.slice_in_dim(extended, offset, offset + length, axis=extended.ndim - 2)
    return jax.nn.silu(summed)


def request_mixer(activated, step_rows, head_decay_rate, write_rows, read_rows, prev_state, head_skip_scale):
    length = activated.shape[0]
    decay_sum = jnp.cumsum(-head_decay_rate[:, None] * step_rows, axis=1)
    scores = jnp.einsum("tn,sn->ts", read_rows.astype(jnp.float32), write_rows.astype(jnp.float32))
    causal = (jnp.arange(length)[:, None] >= jnp.arange(length)[None, :])[None]
    exponent = jnp.where(causal, decay_sum[:, :, None] - decay_sum[:, None, :], 0.0)
    mixing = jnp.where(causal, scores[None] * jnp.exp(exponent), 0.0).astype(jnp.bfloat16)
    driven = (activated * step_rows.T[:, :, None]).astype(jnp.bfloat16)
    local_part = jnp.einsum("hts,shp->thp", mixing.astype(jnp.float32), driven.astype(jnp.float32))
    carried = jnp.einsum("tn,hpn->thp", read_rows.astype(jnp.float32), prev_state.astype(jnp.float32))
    result = local_part + carried * jnp.exp(decay_sum).T[:, :, None] + head_skip_scale[None, :, None] * activated
    to_end = jnp.exp(decay_sum[:, -1:] - decay_sum)
    factor_multiplied = (activated * (step_rows * to_end).T[:, :, None]).astype(jnp.bfloat16)
    state_new = jnp.einsum("thp,tn->hpn", factor_multiplied.astype(jnp.float32), write_rows.astype(jnp.float32))
    state_new = state_new + jnp.exp(decay_sum[:, -1])[:, None, None] * prev_state.astype(jnp.float32)
    return result.astype(jnp.bfloat16), state_new.astype(jnp.bfloat16)


def reference(hidden, base_in_projection, state_input_matrix, state_output_matrix, head_step_size, head_decay_rate, head_skip_scale, convolution_weight, convolution_bias, adapter_down_weight, adapter_up_weight, adapter_home_group, adapter_group_index, state_space_cache, convolution_cache, prefix_holder_device, prefix_cache_slot, prefix_block_count):
    requests = hidden.shape[0] // T_REQ
    owner = jnp.arange(requests, dtype=jnp.int32) // REQ_GRP
    adapter_row = (adapter_home_group[:, 0] * AD_GRP + adapter_group_index).astype(jnp.int32)
    stored_line = ((owner * N_DEV + prefix_holder_device[:, 0]) * CACHE_DEV + prefix_cache_slot).astype(jnp.int32)
    has_prefix = prefix_block_count > 0

    def per_request(fragments):
        incoming_tokens, base_token_rows, write_rows, read_rows, step_rows, single_adapter, cache_one, prefix_one = fragments
        shrunk_rows = jnp.dot(incoming_tokens, adapter_down_weight[single_adapter].T, preferred_element_type=jnp.float32).astype(jnp.bfloat16)
        lifted_rows = base_token_rows.astype(jnp.float32) + jnp.dot(shrunk_rows, adapter_up_weight[single_adapter], preferred_element_type=jnp.float32)
        conv_entry = convolution_cache[cache_one]
        prev_conv = jnp.where(prefix_one, conv_entry, jnp.zeros_like(conv_entry))
        activated = conv_activate(prev_conv, lifted_rows, convolution_weight, convolution_bias).reshape(T_REQ, MIDWAY_ATTENDERS, P_SIZE)
        state_entry = state_space_cache[cache_one]
        prev_state = jnp.where(prefix_one, state_entry, jnp.zeros_like(state_entry))
        outputs, state_new = request_mixer(activated, step_rows, head_decay_rate, write_rows, read_rows, prev_state, head_skip_scale)
        return outputs.reshape(T_REQ, MIDWAY_ATTENDERS * P_SIZE), state_new

    fragments = (
        hidden.reshape(requests, T_REQ, MODEL_WIDTH),
        base_in_projection.reshape(requests, T_REQ, MIXER_CHANNELS),
        state_input_matrix.reshape(requests, T_REQ, N),
        state_output_matrix.reshape(requests, T_REQ, N),
        head_step_size.reshape(MIDWAY_ATTENDERS, requests, T_REQ).transpose(1, 0, 2),
        adapter_row,
        stored_line,
        has_prefix,
    )
    outputs, states = lax.map(per_request, fragments)
    return outputs.reshape(requests * T_REQ, MIXER_CHANNELS), states
```

```python
import functools
import math

import jax
import jax.numpy as jnp
from jax import lax
from jax.experimental import pallas as pl
from jax.experimental.pallas import tpu as pltpu
from jax.sharding import PartitionSpec as P

T_REQ = 256
CAP = 2
ACAP = 4
HEADS_PER_PIECE = 4
LOG2E = math.log2(math.e)
NT = (((1,), (1,)), ((), ()))
TN = (((0,), (0,)), ((), ()))
VMEM_LIMIT = 48 * 1024 * 1024

HOME, ADAPTER_RANK_AMONG, HOLDER, HOLDER_RANK, PRESENT = range(5)


def cost(flops, nbytes, transcendentals=0):
    return pl.CostEstimate(
        flops=int(flops), bytes_accessed=int(nbytes), transcendentals=int(transcendentals)
    )


def hbm(count):
    return [pl.BlockSpec(memory_space=pl.ANY) for _ in range(count)]


def smem(count):
    return [pl.BlockSpec(memory_space=pltpu.SMEM) for _ in range(count)]


def count_before(ref, first, position, label):
    total = jnp.int32(0)
    for q in range(position):
        total = total + (ref[first + q] == label).astype(jnp.int32)
    return total


def pick_request(labels, first, count, wanted_label, wanted_rank):
    seen = jnp.int32(0)
    chosen = jnp.int32(0)
    for q in range(count):
        hit = labels[first + q] == wanted_label
        chosen = jnp.where(hit & (seen == wanted_rank), q, chosen)
        seen = seen + hit.astype(jnp.int32)
    return chosen


def pack_adapter_kernel(groups, per_group, home, index, table, out, sems):
    mine = lax.axis_index("group")
    copies = []
    for g in range(groups):
        seen = jnp.int32(0)
        chosen = [jnp.int32(0) for _ in range(ACAP)]
        for q in range(per_group):
            hit = home[g * per_group + q] == mine
            value = index[g * per_group + q]
            for c in range(ACAP):
                chosen[c] = jnp.where(hit & (seen == c), value, chosen[c])
            seen = seen + hit.astype(jnp.int32)
        for c in range(ACAP):
            copy = pltpu.make_async_copy(table.at[chosen[c]], out.at[g, c], sems.at[g, c])
            copy.start()
            copies.append(copy)
    for copy in copies:
        copy.wait()


def pack_adapter(home, index, table, groups, per_group):
    return pl.pallas_call(
        functools.partial(pack_adapter_kernel, groups, per_group),
        out_shape=jax.ShapeDtypeStruct((groups, ACAP) + table.shape[1:], table.dtype),
        in_specs=smem(2) + hbm(1),
        out_specs=pl.BlockSpec(memory_space=pl.ANY),
        scratch_shapes=[pltpu.SemaphoreType.DMA((groups, ACAP))],
        cost_estimate=cost(0, 2 * groups * ACAP * table.shape[1] * table.shape[2] * 2),
        name="pack_adapter",
    )(home, index, table)


def pack_small_kernel(
    devices, per_group, width, home, index, holder, slot, blocks,
    write_rows, read_rows, conv, meta, rows_out, conv_out, row_sems, conv_sems,
):
    my_group = lax.axis_index("group")
    mine = lax.axis_index("dev")
    first = my_group * per_group
    row_copies = [
        pltpu.make_async_copy(write_rows, rows_out.at[0], row_sems.at[0]),
        pltpu.make_async_copy(read_rows, rows_out.at[1], row_sems.at[1]),
    ]
    for copy in row_copies:
        copy.start()
    copies = []
    for c in range(CAP):
        chosen = slot[first + pick_request(holder, first, per_group, mine, c)]
        for d in range(devices):
            copy = pltpu.make_async_copy(
                conv.at[chosen, :, pl.ds(d * width, width)], conv_out.at[d, c], conv_sems.at[c, d]
            )
            copy.start()
            copies.append(copy)
    for q in range(per_group):
        meta[HOME, q] = home[first + q]
        meta[ADAPTER_RANK_AMONG, q] = count_before(home, first, q, home[first + q])
        meta[HOLDER, q] = holder[first + q]
        meta[HOLDER_RANK, q] = count_before(holder, first, q, holder[first + q])
        meta[PRESENT, q] = (blocks[first + q] > 0).astype(jnp.int32)
    for copy in row_copies + copies:
        copy.wait()


def pack_state_kernel(devices, per_group, pieces, holder, slot, cache, *rest):
    outs, sems = rest[:pieces], rest[pieces]
    first = lax.axis_index("group") * per_group
    mine = lax.axis_index("dev")
    copies = []
    for c in range(CAP):
        chosen = slot[first + pick_request(holder, first, per_group, mine, c)]
        for p in range(pieces):
            copy = pltpu.make_async_copy(
                cache.at[chosen, :, p], outs[p].at[:, c], sems.at[c, p]
            )
            copy.start()
            copies.append(copy)
    for copy in copies:
        copy.wait()


def shrink_kernel(meta, hidden, down, out):
    part = lax.dot_general(down[0, 0], hidden[...], NT, preferred_element_type=jnp.float32)
    out[0] = part.astype(out.dtype)


def sum_kernel(parts, out):
    total = parts[0].astype(jnp.float32)
    for k in range(1, parts.shape[0]):
        total = total + parts[k].astype(jnp.float32)
    total = total.astype(out.dtype)
    for k in range(out.shape[0]):
        out[k] = total


def prep_kernel(steps, rates, row_out, column_out):
    heads, length = steps.shape
    step = steps[...]
    x = step * (rates[...] * (-LOG2E))
    high = x.astype(jnp.bfloat16)
    rest = x - high.astype(jnp.float32)
    middle = rest.astype(jnp.bfloat16)
    low = (rest - middle.astype(jnp.float32)).astype(jnp.bfloat16)
    s = lax.broadcasted_iota(jnp.int32, (length, length), 0)
    t = lax.broadcasted_iota(jnp.int32, (length, length), 1)
    ones = (s <= t).astype(jnp.float32).astype(jnp.bfloat16)
    total = jnp.dot(low, ones, preferred_element_type=jnp.float32)
    total = total + jnp.dot(middle, ones, preferred_element_type=jnp.float32)
    total = total + jnp.dot(high, ones, preferred_element_type=jnp.float32)
    row_out[...] = total - jnp.log2(step)
    column_out[...] = total.T


def mix_kernel(
    piece, meta, base, shrunk, up, conv, conv_weight, conv_bias, skip, row_decay, column_decay,
    rows_in, state, *rest,
):
    out, state_out, extended, scores = rest[-4:]
    r = pl.program_id(0)
    length, width = base.shape
    half = length // 2
    heads = state.shape[2]
    size, depth = state.shape[3], state.shape[4]
    f32, bf16 = jnp.float32, jnp.bfloat16
    present = meta[PRESENT, r] > 0

    write, read = rows_in[0, 0], rows_in[0, 1]
    all_scores = lax.dot_general(read, write, NT, preferred_element_type=f32)
    t = lax.broadcasted_iota(jnp.int32, (length, length), 0)
    s = lax.broadcasted_iota(jnp.int32, (length, length), 1)
    scores[...] = jnp.where(s <= t, all_scores, 0.0)

    lifted = base[...].astype(f32) + lax.dot_general(
        shrunk[0], up[0, 0], TN, preferred_element_type=f32
    )
    taps = conv_weight.shape[0]
    extended[8:, :] = lifted
    before = conv[0, 0].astype(f32)
    extended[8 - (taps - 1):8, :] = jnp.where(present, before, 0.0)
    v = conv_bias[...] + conv_weight[taps - 1:taps, :] * lifted
    for k in range(taps - 1):
        begin = 8 - (taps - 1) + k
        v = v + conv_weight[k:k + 1, :] * extended[begin:begin + length, :]
    activated = v * (0.5 + 0.5 * jnp.tanh(0.5 * v))
    act16 = activated.astype(bf16)
    act16_t = act16.T

    row = row_decay[...]
    column = column_decay[...]
    lane = lax.broadcasted_iota(jnp.int32, (1, 2 * size), 1)
    for pair in range(heads // 2):
        lo, hi = pair * 2 * size, (pair + 1) * 2 * size
        a = act16[:, lo:hi]
        zero = jnp.zeros_like(a)
        a_sel = (jnp.where(lane < size, a, zero), jnp.where(lane < size, zero, a))
        upper, lower, decays = [], [], []
        for i in range(2):
            h = piece * heads + pair * 2 + i
            dt = jnp.broadcast_to(column[:, h:h + 1], (length, half))
            ds0, ds1 = row[h:h + 1, :half], row[h:h + 1, half:]
            m00 = jnp.exp2(jnp.minimum(dt[:half] - ds0, 126.0)) * scores[:half, :half]
            m10 = jnp.exp2(dt[half:] - ds0) * scores[half:, :half]
            m11 = jnp.exp2(jnp.minimum(dt[half:] - ds1, 126.0)) * scores[half:, half:]
            upper.append(m00.astype(bf16))
            lower.extend([m10.astype(bf16), m11.astype(bf16)])
            decays.append(dt)
            k = pair * 2 + i
            end = dt[length - 1:length, :]
            to_end = jnp.exp2(jnp.concatenate([end, end], axis=1) - row[h:h + 1, :])
            weighted = (act16_t[k * size:(k + 1) * size, :].astype(f32) * to_end).astype(bf16)
            fresh = jnp.dot(weighted, write, preferred_element_type=f32)
            before = jnp.where(present, state[0, 0, k].astype(f32), 0.0)
            state_out[0, k] = (fresh + before * jnp.exp2(end)).astype(state_out.dtype)
        y0 = jnp.dot(
            jnp.concatenate(upper, axis=1),
            jnp.concatenate([a_sel[0][:half], a_sel[1][:half]], axis=0),
            preferred_element_type=f32,
        )
        y1 = jnp.dot(
            jnp.concatenate(lower, axis=1),
            jnp.concatenate(a_sel, axis=0),
            preferred_element_type=f32,
        )
        states = state[0, 0, 2 * pair:2 * pair + 2].reshape(2 * size, depth)
        carried = lax.dot_general(read, states, NT, preferred_element_type=f32)
        grown = jnp.exp2(jnp.where(lane < size, decays[0], decays[1]))
        carried = jnp.where(present, carried * grown, 0.0)
        direct = skip[:, lo:hi] * activated[:, lo:hi]
        out[:, lo:hi] = (jnp.concatenate([y0, y1], axis=0) + carried + direct).astype(out.dtype)


def body(
    hidden, base_in_projection, state_input_matrix, state_output_matrix, head_step_size,
    head_decay_rate, head_skip_scale, convolution_weight, convolution_bias, adapter_down_weight,
    adapter_up_weight, adapter_home_group, adapter_group_index, state_space_cache,
    convolution_cache, prefix_holder_device, prefix_cache_slot, prefix_block_count,
):
    groups, devices = lax.axis_size("group"), lax.axis_size("dev")
    tokens, width = base_in_projection.shape
    per_group = tokens // T_REQ
    heads = head_step_size.shape[0]
    size, depth = state_space_cache.shape[2:]
    rank = adapter_down_weight.shape[1]
    taps = convolution_weight.shape[0]
    pieces = heads // HEADS_PER_PIECE
    piece_width = HEADS_PER_PIECE * size
    bf16, f32 = jnp.bfloat16, jnp.float32
    share = per_group // devices

    home = adapter_home_group.reshape(-1)
    holder = prefix_holder_device.reshape(-1)

    down_send = pack_adapter(home, adapter_group_index, adapter_down_weight, groups, per_group)
    down_got = lax.all_to_all(down_send, "group", split_axis=0, concat_axis=0, tiled=True)

    meta, rows_mine, conv_send = pl.pallas_call(
        functools.partial(pack_small_kernel, devices, per_group, width),
        out_shape=(
            jax.ShapeDtypeStruct((8, per_group), jnp.int32),
            jax.ShapeDtypeStruct((2,) + state_input_matrix.shape, bf16),
            jax.ShapeDtypeStruct((devices, CAP, taps - 1, width), bf16),
        ),
        in_specs=smem(5) + hbm(3),
        out_specs=tuple(smem(1) + hbm(2)),
        scratch_shapes=[pltpu.SemaphoreType.DMA((2,)), pltpu.SemaphoreType.DMA((CAP, devices))],
        cost_estimate=cost(0, 1 << 20),
        name="pack_small",
    )(
        home, adapter_group_index, holder, prefix_cache_slot, prefix_block_count,
        state_input_matrix, state_output_matrix, convolution_cache,
    )
    rows_all = lax.all_gather(rows_mine, "dev", axis=0, tiled=False)
    conv_got = lax.all_to_all(conv_send, "dev", split_axis=0, concat_axis=0, tiled=True)

    cache = state_space_cache.reshape(
        state_space_cache.shape[0], devices, pieces, HEADS_PER_PIECE, size, depth
    )
    state_sends = pl.pallas_call(
        functools.partial(pack_state_kernel, devices, per_group, pieces),
        out_shape=tuple(
            jax.ShapeDtypeStruct((devices, CAP, HEADS_PER_PIECE, size, depth), bf16)
            for _ in range(pieces)
        ),
        in_specs=smem(2) + hbm(1),
        out_specs=tuple(hbm(pieces)),
        scratch_shapes=[pltpu.SemaphoreType.DMA((CAP, pieces))],
        cost_estimate=cost(0, 8 << 20),
        name="pack_state",
    )(holder, prefix_cache_slot, cache)
    state_gots = [
        lax.all_to_all(x, "dev", split_axis=0, concat_axis=0, tiled=True) for x in state_sends
    ]

    up_send = pack_adapter(home, adapter_group_index, adapter_up_weight, groups, per_group)
    up_got = lax.all_to_all(up_send, "group", split_axis=0, concat_axis=0, tiled=True)

    row_decay, column_decay = pl.pallas_call(
        prep_kernel,
        grid=(per_group,),
        out_shape=(
            jax.ShapeDtypeStruct((heads, tokens), f32),
            jax.ShapeDtypeStruct((tokens, heads), f32),
        ),
        in_specs=[
            pl.BlockSpec((heads, T_REQ), lambda r: (0, r)),
            pl.BlockSpec((heads, 1), lambda r: (0, 0)),
        ],
        out_specs=(
            pl.BlockSpec((heads, T_REQ), lambda r: (0, r)),
            pl.BlockSpec((T_REQ, heads), lambda r: (r, 0)),
        ),
        cost_estimate=cost(0, 4 << 20),
        name="prep",
    )(head_step_size, head_decay_rate.reshape(heads, 1))

    partial_down = pl.pallas_call(
        shrink_kernel,
        grid_spec=pltpu.PrefetchScalarGridSpec(
            num_scalar_prefetch=1,
            grid=(per_group,),
            in_specs=[
                pl.BlockSpec((T_REQ, hidden.shape[1]), lambda r, meta: (r, 0)),
                pl.BlockSpec(
                    (1, 1, rank, hidden.shape[1]),
                    lambda r, meta: (meta[HOME, r], meta[ADAPTER_RANK_AMONG, r], 0, 0),
                ),
            ],
            out_specs=pl.BlockSpec((1, rank, T_REQ), lambda r, meta: (r, 0, 0)),
        ),
        out_shape=jax.ShapeDtypeStruct((per_group, rank, T_REQ), bf16),
        cost_estimate=cost(2 * tokens * hidden.shape[1] * rank, 6 << 20),
        compiler_params=pltpu.CompilerParams(vmem_limit_bytes=VMEM_LIMIT),
        name="shrink",
    )(meta, hidden, down_got)
    parts = lax.all_to_all(partial_down, "dev", split_axis=0, concat_axis=0, tiled=True)
    summed = pl.pallas_call(
        sum_kernel,
        out_shape=jax.ShapeDtypeStruct((devices, share, rank, T_REQ), bf16),
        cost_estimate=cost(0, 1 << 19),
        name="sum_parts",
    )(parts.reshape(devices, share, rank, T_REQ))
    shrunk = lax.all_to_all(summed, "dev", split_axis=0, concat_axis=0, tiled=True)
    shrunk = shrunk.reshape(per_group, rank, T_REQ)

    skip_row = jnp.repeat(head_skip_scale, size).reshape(1, width)
    bias_row = convolution_bias.reshape(1, width)
    outs = None
    for piece in range(pieces):
        in_specs = [
            pl.BlockSpec((T_REQ, piece_width), lambda r, meta, p=piece: (r, p)),
            pl.BlockSpec((1, rank, T_REQ), lambda r, meta: (r, 0, 0)),
            pl.BlockSpec(
                (1, 1, rank, piece_width),
                lambda r, meta, p=piece: (meta[HOME, r], meta[ADAPTER_RANK_AMONG, r], 0, p),
            ),
            pl.BlockSpec(
                (1, 1, taps - 1, piece_width),
                lambda r, meta, p=piece: (meta[HOLDER, r], meta[HOLDER_RANK, r], 0, p),
            ),
            pl.BlockSpec((taps, piece_width), lambda r, meta, p=piece: (0, p)),
            pl.BlockSpec((1, piece_width), lambda r, meta, p=piece: (0, p)),
            pl.BlockSpec((1, piece_width), lambda r, meta, p=piece: (0, p)),
            pl.BlockSpec((heads, T_REQ), lambda r, meta: (0, r)),
            pl.BlockSpec((T_REQ, heads), lambda r, meta: (r, 0)),
            pl.BlockSpec((1, 2, T_REQ, depth), lambda r, meta: (r, 0, 0, 0)),
            pl.BlockSpec(
                (1, 1, HEADS_PER_PIECE, size, depth),
                lambda r, meta: (meta[HOLDER, r], meta[HOLDER_RANK, r], 0, 0, 0),
            ),
        ]
        operands = [
            meta, base_in_projection, shrunk, up_got, conv_got, convolution_weight, bias_row,
            skip_row, row_decay, column_decay, rows_all, state_gots[piece],
        ]
        aliases = {}
        if outs is not None:
            aliases = {len(operands): 0, len(operands) + 1: 1}
            operands += list(outs)
            in_specs += hbm(2)
        outs = pl.pallas_call(
            functools.partial(mix_kernel, piece),
            grid_spec=pltpu.PrefetchScalarGridSpec(
                num_scalar_prefetch=1,
                grid=(per_group,),
                in_specs=in_specs,
                out_specs=(
                    pl.BlockSpec((T_REQ, piece_width), lambda r, meta, p=piece: (r, p)),
                    pl.BlockSpec(
                        (1, HEADS_PER_PIECE, size, depth), lambda r, meta, p=piece: (r, p, 0, 0)
                    ),
                ),
                scratch_shapes=[
                    pltpu.VMEM((T_REQ + 8, piece_width), f32),
                    pltpu.VMEM((T_REQ, T_REQ), f32),
                ],
            ),
            out_shape=(
                jax.ShapeDtypeStruct((tokens, width), bf16),
                jax.ShapeDtypeStruct((per_group, heads, size, depth), bf16),
            ),
            input_output_aliases=aliases,
            cost_estimate=cost(1 << 30, 6 << 20, 8 << 20),
            compiler_params=pltpu.CompilerParams(vmem_limit_bytes=VMEM_LIMIT),
            name=f"mix_{piece}",
        )(*operands)
    return outs


def solution(mesh):
    placed = (
        P("group", "dev"),
        P("group", "dev"),
        P(("group", "dev"), None),
        P(("group", "dev"), None),
        P("dev", "group"),
        P("dev"),
        P("dev"),
        P(None, "dev"),
        P("dev"),
        P("group", None, "dev"),
        P("group", None, "dev"),
        P(),
        P(),
        P(("group", "dev"), None, None, None),
        P(("group", "dev"), None, None),
        P(),
        P(),
        P(),
    )
    return jax.shard_map(
        body,
        mesh=mesh,
        in_specs=placed,
        out_specs=(P("group", "dev"), P("group", "dev", None, None)),
        check_vma=False,
    )
```

```python
import functools
import math

import jax
import jax.numpy as jnp
from jax import lax
from jax.experimental import pallas as pl
from jax.experimental.pallas import tpu as pltpu
from jax.sharding import PartitionSpec as P

T_REQ = 256
CAP = 2
ACAP = 4
CONV_ROWS = 16
LOG2E = math.log2(math.e)
NT = (((1,), (1,)), ((), ()))
TN = (((0,), (0,)), ((), ()))
VMEM_LIMIT = 48 * 1024 * 1024

DIST, ARANK, AINDEX, HOLDER, HRANK, PRESENT, REQ_OF, OVER, OSLOT, OHOLDER, MISC, SEND = range(12)
COUNT, MOST, ME, SLOT, SLOT_TOO = range(5)
META_SHAPE = (16, 64)


def cost(flops, nbytes, transcendentals=0):
    return pl.CostEstimate(
        flops=int(flops), bytes_accessed=int(nbytes), transcendentals=int(transcendentals)
    )


def params():
    return pltpu.CompilerParams(vmem_limit_bytes=VMEM_LIMIT)


def smem(count):
    return [pl.BlockSpec(memory_space=pltpu.SMEM) for _ in range(count)]


def as_int(flag):
    return flag.astype(jnp.int32)


def ranks_of(labels):
    ranks = []
    for q, label in enumerate(labels):
        total = jnp.int32(0)
        for other in labels[:q]:
            total = total + as_int(other == label)
        ranks.append(total)
    return ranks


def plan_kernel(groups, devices, per_group, home, index, holder, slot, blocks, meta):
    my_group = lax.axis_index("group")
    me = lax.axis_index("dev")
    first = my_group * per_group
    for j in range(per_group):
        meta[OVER, j] = jnp.int32(0)
        meta[OSLOT, j] = jnp.int32(0)
        meta[OHOLDER, j] = jnp.int32(0)

    homes = [home[first + q] for q in range(per_group)]
    for q, rank in enumerate(ranks_of(homes)):
        own = homes[q] == my_group
        meta[DIST, q] = lax.bitwise_xor(homes[q], my_group)
        meta[ARANK, q] = jnp.where(own, 0, rank)
        meta[AINDEX, q] = jnp.where(own, index[first + q], 0)
        meta[PRESENT, q] = as_int(blocks[first + q] > 0)
    for k in range(1, groups):
        theirs = lax.bitwise_xor(my_group, k) * per_group
        seen = jnp.int32(0)
        chosen = [jnp.int32(0) for _ in range(ACAP)]
        for q in range(per_group):
            hit = home[theirs + q] == my_group
            value = index[theirs + q]
            for c in range(ACAP):
                chosen[c] = jnp.where(hit & (seen == c), value, chosen[c])
            seen = seen + as_int(hit)
        for c in range(ACAP):
            meta[SEND, (k - 1) * ACAP + c] = chosen[c]

    holders = [holder[first + q] for q in range(per_group)]
    ranks = ranks_of(holders)
    count = jnp.int32(0)
    my_slots = [jnp.int32(0) for _ in range(CAP)]
    for q in range(per_group):
        meta[HOLDER, q] = holders[q]
        meta[HRANK, q] = ranks[q]
        for c in range(CAP):
            hit = (holders[q] == me) & (ranks[q] == c)
            my_slots[c] = jnp.where(hit, slot[first + q], my_slots[c])

        @pl.when(ranks[q] > 0)
        def _():
            meta[OVER, count] = jnp.int32(q)
            meta[OSLOT, count] = slot[first + q]
            meta[OHOLDER, count] = holders[q]

        count = count + as_int(ranks[q] > 0)
    empties = jnp.int32(0)
    for d in range(devices):
        source = lax.bitwise_xor(me, d)
        request = jnp.int32(-1)
        for q in range(per_group):
            request = jnp.where((holders[q] == source) & (ranks[q] == 0), q, request)
        missing = request < 0
        meta[REQ_OF, d] = jnp.where(missing, meta[OVER, empties], request)
        empties = empties + as_int(missing)
    most = jnp.int32(0)
    for g in range(groups):
        labels = [holder[g * per_group + q] for q in range(per_group)]
        total = jnp.int32(0)
        for rank in ranks_of(labels):
            total = total + as_int(rank > 0)
        most = jnp.maximum(most, total)
    meta[MISC, COUNT] = count
    meta[MISC, MOST] = most
    meta[MISC, ME] = me
    meta[MISC, SLOT] = my_slots[0]
    meta[MISC, SLOT_TOO] = my_slots[1]


def pack_adapter_kernel(groups, meta, table, *rest):
    outs, sems = rest[:-1], rest[-1]
    copies = []
    for k in range(1, groups):
        for c in range(ACAP):
            chosen = meta[SEND, (k - 1) * ACAP + c]
            copy = pltpu.make_async_copy(
                table.at[chosen], outs[k - 1].at[c], sems.at[(k - 1) * ACAP + c]
            )
            copy.start()
            copies.append(copy)
    for copy in copies:
        copy.wait()


def swap_adapters(meta, table, groups, name):
    packed = pl.pallas_call(
        functools.partial(pack_adapter_kernel, groups),
        out_shape=tuple(
            jax.ShapeDtypeStruct((ACAP,) + table.shape[1:], table.dtype) for _ in range(groups - 1)
        ),
        in_specs=smem(1) + [pl.BlockSpec(memory_space=pltpu.HBM)],
        out_specs=tuple(pl.BlockSpec(memory_space=pltpu.VMEM) for _ in range(groups - 1)),
        scratch_shapes=[pltpu.SemaphoreType.DMA(((groups - 1) * ACAP,))],
        cost_estimate=cost(0, 2 * (groups - 1) * ACAP * table.shape[1] * table.shape[2] * 2),
        compiler_params=params(),
        name=name,
    )(meta, table)
    return [
        lax.ppermute(packed[k - 1], "group", [(g, g ^ k) for g in range(groups)])
        for k in range(1, groups)
    ]


def pack_state_kernel(devices, meta, cache, *rest):
    outs, sems = rest[:-1], rest[-1]
    me = meta[MISC, ME]
    copies = []
    for d in range(1, devices):
        target = lax.bitwise_xor(me, d)
        copy = pltpu.make_async_copy(
            cache.at[meta[MISC, SLOT], target // 2, target % 2], outs[d - 1], sems.at[d - 1]
        )
        copy.start()
        copies.append(copy)
    for copy in copies:
        copy.wait()


def pack_conv_kernel(devices, width, meta, conv, out):
    half = width // 2
    for c in range(CAP):
        rows = conv[meta[MISC, (SLOT, SLOT_TOO)[c]]]
        for d in range(devices):
            for k in range(rows.shape[0]):
                for part in range(2):
                    at = c * 2 * rows.shape[0] + 2 * k + part
                    begin = d * width + part * half
                    out[d, at:at + 1, :] = rows[k:k + 1, begin:begin + half]


def copy_kernel(j, meta, source, out):
    out[0] = source[0, 0, 0]


def pick_kernel(step, lines, j, meta, own_r, over_r, own_l, over_l, *rest):
    out_r, out_l = rest[-2:]
    me = meta[MISC, ME]
    source = meta[OHOLDER, j[0]]
    same = source // 2 == me // 2
    mine = same & (source % 2 == me % 2)
    across = same & (source % 2 != me % 2)

    @pl.when(mine)
    def _():
        out_r[...] = own_r[0, 0, 0]
        out_l[...] = own_l[0, 0, 0]

    @pl.when(across)
    def _():
        out_r[...] = over_r[0]
        out_l[...] = over_l[0]

    @pl.when(jnp.logical_not(same))
    def _():
        if step > 1:
            out_r[...] = rest[0][...]
            out_l[...] = rest[1][...]
        else:
            out_r[...] = jnp.zeros_like(out_r)
            out_l[...] = jnp.zeros_like(out_l)


def right_block(meta, step, lines):
    return jnp.clip(lines + meta[MISC, ME] // 2 - step, 0, lines - 1)


def left_block(meta, step, lines):
    return jnp.clip(meta[MISC, ME] // 2 + step - lines, 0, lines - 1)


def spread_entry(j, meta, cache, devices):
    lines = devices // 2
    shape = cache.shape[3:]
    full = (1, 1, 1) + shape
    send = pl.pallas_call(
        copy_kernel,
        grid_spec=pltpu.PrefetchScalarGridSpec(
            num_scalar_prefetch=2,
            grid=(lines,),
            in_specs=[
                pl.BlockSpec(
                    full,
                    lambda m, j, meta: (
                        meta[OSLOT, j[0]], m, 1 - meta[MISC, ME] % 2, 0, 0, 0
                    ),
                )
            ],
            out_specs=pl.BlockSpec((1,) + shape, lambda m, j, meta: (m, 0, 0, 0)),
        ),
        out_shape=jax.ShapeDtypeStruct((lines,) + shape, cache.dtype),
        cost_estimate=cost(0, 2 << 20),
        compiler_params=params(),
        name="pack_across",
    )(j, meta, cache)
    across = lax.ppermute(send, "dev", [(d, d ^ 1) for d in range(devices)])
    from_left = from_right = None
    whole = pl.BlockSpec(shape, lambda g, j, meta: (0, 0, 0))
    for step in range(1, lines):
        def at_right(j, meta, step=step):
            return right_block(meta, step, lines)

        def at_left(j, meta, step=step):
            return left_block(meta, step, lines)

        operands = [cache, across, cache, across]
        in_specs = [
            pl.BlockSpec(
                full, lambda g, j, meta, at=at: (
                    meta[OSLOT, j[0]], at(j, meta), meta[MISC, ME] % 2, 0, 0, 0
                )
            ) if is_own else pl.BlockSpec(
                (1,) + shape, lambda g, j, meta, at=at: (at(j, meta), 0, 0, 0)
            )
            for at in (at_right, at_left) for is_own in (True, False)
        ]
        if step > 1:
            operands += [from_left, from_right]
            in_specs += [whole, whole]
        to_right, to_left = pl.pallas_call(
            functools.partial(pick_kernel, step, lines),
            grid_spec=pltpu.PrefetchScalarGridSpec(
                num_scalar_prefetch=2, grid=(1,), in_specs=in_specs, out_specs=(whole, whole)
            ),
            out_shape=tuple(jax.ShapeDtypeStruct(shape, cache.dtype) for _ in range(2)),
            cost_estimate=cost(0, 2 << 20),
            compiler_params=params(),
            name=f"pick_{step}",
        )(j, meta, *operands)
        from_left = lax.ppermute(
            to_right, "dev",
            [(2 * i + x, 2 * i + 2 + x) for i in range(step) for x in range(2)],
        )
        from_right = lax.ppermute(
            to_left, "dev",
            [(devices - 1 - (2 * i + x), devices - 3 - (2 * i + x))
             for i in range(step) for x in range(2)],
        )
    return across, from_left, from_right


def final_specs(shape, request):
    full = (1, 1, 1) + shape
    return [
        pl.BlockSpec(
            full, lambda g, j, meta: (
                request(g, j, meta), meta[MISC, ME] // 2, meta[MISC, ME] % 2, 0, 0, 0
            )
        ),
        pl.BlockSpec((1,) + shape, lambda g, j, meta: (meta[MISC, ME] // 2, 0, 0, 0)),
        pl.BlockSpec(shape, lambda g, j, meta: (0, 0, 0)),
        pl.BlockSpec(shape, lambda g, j, meta: (0, 0, 0)),
    ]


def which_candidate(meta, source):
    me = meta[MISC, ME]
    same = source // 2 == me // 2
    mine = same & (source % 2 == me % 2)
    return jnp.where(mine, 0, jnp.where(same, 1, jnp.where(source // 2 < me // 2, 2, 3)))


def final_kernel(j, meta, own, across, from_left, from_right, out):
    which = which_candidate(meta, meta[OHOLDER, j[0]])
    picks = (own.at[0, 0, 0], across.at[0], from_left, from_right)
    for k, pick in enumerate(picks):
        @pl.when(which == k)
        def _(pick=pick):
            out[...] = pick[...]


def spread_rest(meta, cache, devices, limit):
    shape = cache.shape[3:]

    def one(j, held):
        jj = j.reshape(1)
        got = spread_entry(jj, meta, cache, devices)
        block = pl.pallas_call(
            final_kernel,
            grid_spec=pltpu.PrefetchScalarGridSpec(
                num_scalar_prefetch=2,
                grid=(1,),
                in_specs=final_specs(shape, lambda g, j, meta: meta[OSLOT, j[0]]),
                out_specs=pl.BlockSpec(shape, lambda g, j, meta: (0, 0, 0)),
            ),
            out_shape=jax.ShapeDtypeStruct(shape, cache.dtype),
            compiler_params=params(),
            name="final_pick",
        )(jj, meta, cache, *got)
        return lax.dynamic_update_slice_in_dim(held, block[None], j - 1, 0)

    held = jnp.zeros((limit - 1,) + shape, cache.dtype)
    return lax.fori_loop(jnp.int32(1), meta[MISC, MOST], one, held)


def shrink_kernel(groups, meta, hidden, *rest):
    tables, out = rest[:groups], rest[groups]
    dist = meta[DIST, pl.program_id(0)]
    for k in range(groups):
        @pl.when(dist == k)
        def _(k=k):
            part = lax.dot_general(
                tables[k][0], hidden[...], NT, preferred_element_type=jnp.float32
            )
            out[0] = part.astype(out.dtype)


def sum_kernel(parts, out):
    total = parts[0].astype(jnp.float32)
    for k in range(1, parts.shape[0]):
        total = total + parts[k].astype(jnp.float32)
    total = total.astype(out.dtype)
    for k in range(out.shape[0]):
        out[k] = total


def prep_kernel(steps, rates, row_out, column_out):
    heads, length = steps.shape
    step = steps[...]
    x = step * (rates[...] * (-LOG2E))
    high = x.astype(jnp.bfloat16)
    rest = x - high.astype(jnp.float32)
    middle = rest.astype(jnp.bfloat16)
    low = (rest - middle.astype(jnp.float32)).astype(jnp.bfloat16)
    s = lax.broadcasted_iota(jnp.int32, (length, length), 0)
    t = lax.broadcasted_iota(jnp.int32, (length, length), 1)
    ones = (s <= t).astype(jnp.float32).astype(jnp.bfloat16)
    total = jnp.dot(low, ones, preferred_element_type=jnp.float32)
    total = total + jnp.dot(middle, ones, preferred_element_type=jnp.float32)
    total = total + jnp.dot(high, ones, preferred_element_type=jnp.float32)
    row_out[...] = total - jnp.log2(step)
    column_out[...] = total.T


def mix_kernel(groups, taps, meta, base, shrunk, *rest):
    tables, (conv, channel, row_decay, column_decay, rows_in, partial, fresh, extended, scores) = (
        rest[:groups], rest[groups:]
    )
    r = pl.program_id(0)
    length, width = base.shape
    half = length // 2
    heads, size, depth = fresh.shape[1:]
    f32, bf16 = jnp.float32, jnp.bfloat16
    dist = meta[DIST, r]
    for k in range(groups):
        @pl.when(dist == k)
        def _(k=k):
            extended[8:, :] = base[...].astype(f32) + lax.dot_general(
                shrunk[0], tables[k][0], TN, preferred_element_type=f32
            )

    write, read = rows_in[:, :depth], rows_in[:, depth:]
    all_scores = lax.dot_general(read, write, NT, preferred_element_type=f32)
    t = lax.broadcasted_iota(jnp.int32, (length, length), 0)
    s = lax.broadcasted_iota(jnp.int32, (length, length), 1)
    scores[...] = jnp.where(s <= t, all_scores, 0.0)

    present = meta[PRESENT, r] > 0
    second = meta[HRANK, r] > 0
    few = taps - 1
    carry = jnp.where(second, conv[0, 2 * few:4 * few, :], conv[0, :2 * few, :]).astype(f32)
    carry = jnp.where(present, carry, 0.0)
    for k in range(few):
        at = 8 - few + k
        extended[at:at + 1, :width // 2] = carry[2 * k:2 * k + 1, :]
        extended[at:at + 1, width // 2:] = carry[2 * k + 1:2 * k + 2, :]

    row = row_decay[...]
    column = column_decay[...]
    lane = lax.broadcasted_iota(jnp.int32, (1, 2 * size), 1)
    for pair in range(heads // 2):
        lo, hi = pair * 2 * size, (pair + 1) * 2 * size
        v = channel[taps:taps + 1, lo:hi]
        for k in range(taps):
            begin = 8 - few + k
            v = v + channel[k:k + 1, lo:hi] * extended[begin:begin + length, lo:hi]
        activated = v * (0.5 + 0.5 * jnp.tanh(0.5 * v))
        a = activated.astype(bf16)
        a_t = a.T
        zero = jnp.zeros_like(a)
        a_sel = (jnp.where(lane < size, a, zero), jnp.where(lane < size, zero, a))
        upper, lower = [], []
        for i in range(2):
            h = pair * 2 + i
            dt = jnp.broadcast_to(column[:, h:h + 1], (length, half))
            ds0, ds1 = row[h:h + 1, :half], row[h:h + 1, half:]
            m00 = jnp.exp2(jnp.minimum(dt[:half] - ds0, 126.0)) * scores[:half, :half]
            m10 = jnp.exp2(dt[half:] - ds0) * scores[half:, :half]
            m11 = jnp.exp2(jnp.minimum(dt[half:] - ds1, 126.0)) * scores[half:, half:]
            upper.append(m00.astype(bf16))
            lower.extend([m10.astype(bf16), m11.astype(bf16)])
            end = dt[length - 1:length, :]
            to_end = jnp.exp2(jnp.concatenate([end, end], axis=1) - row[h:h + 1, :])
            weighted = (a_t[i * size:(i + 1) * size, :].astype(f32) * to_end).astype(bf16)
            fresh[0, h] = jnp.dot(weighted, write, preferred_element_type=f32)
        y0 = jnp.dot(
            jnp.concatenate(upper, axis=1),
            jnp.concatenate([a_sel[0][:half], a_sel[1][:half]], axis=0),
            preferred_element_type=f32,
        )
        y1 = jnp.dot(
            jnp.concatenate(lower, axis=1),
            jnp.concatenate(a_sel, axis=0),
            preferred_element_type=f32,
        )
        direct = channel[taps + 1:taps + 2, lo:hi] * activated
        partial[:half, lo:hi] = y0 + direct[:half]
        partial[half:, lo:hi] = y1 + direct[half:]


def add_state(present, state, partial, fresh, read, column, out, final):
    heads, size, depth = state.shape
    length = partial.shape[0]
    f32 = jnp.float32
    lane = lax.broadcasted_iota(jnp.int32, (1, 2 * size), 1)
    for pair in range(heads // 2):
        lo, hi = pair * 2 * size, (pair + 1) * 2 * size
        states = state[2 * pair:2 * pair + 2]
        carried = lax.dot_general(
            read, states.reshape(2 * size, depth), NT, preferred_element_type=f32
        )
        decays = [
            jnp.broadcast_to(column[:, h:h + 1], (length, 2 * size))
            for h in (2 * pair, 2 * pair + 1)
        ]
        grown = jnp.exp2(jnp.where(lane < size, decays[0], decays[1]))
        carried = jnp.where(present, carried * grown, 0.0)
        out[:, lo:hi] = (partial[:, lo:hi] + carried).astype(out.dtype)
        for i in range(2):
            h = 2 * pair + i
            kept = states[i].astype(f32) * jnp.exp2(decays[i][length - 1:length, :depth])
            kept = jnp.where(present, kept, 0.0)
            final[0, h] = (fresh[0, h] + kept).astype(final.dtype)


def finish(begin, states, cache, j, meta, partial, fresh, rows_all, column_decay, outs):
    tokens, width = partial.shape
    per_group, heads, size, depth = fresh.shape
    shape = (heads, size, depth)
    count = len(states)
    if begin == 0:
        state_specs = [
            pl.BlockSpec(
                (1, 1, 1) + shape, lambda g, j, meta: (
                    meta[MISC, SLOT], meta[MISC, ME] // 2, meta[MISC, ME] % 2, 0, 0, 0
                )
            )
        ]
    else:
        state_specs = [pl.BlockSpec(shape, lambda g, j, meta: (0, 0, 0))]
    state_specs += [pl.BlockSpec(shape, lambda g, j, meta: (0, 0, 0))] * (count - 1)

    def kernel(j, meta, partial, fresh, rows_in, column, *rest):
        out, final = rest[-2:]
        g = pl.program_id(0)
        present = meta[PRESENT, meta[REQ_OF, begin + g]] > 0
        for k in range(count):
            state = rest[0].at[0, 0, 0] if begin == 0 and k == 0 else rest[k]

            @pl.when(g == k)
            def _(state=state):
                add_state(
                    present, state, partial, fresh, rows_in[:, depth:], column[...], out, final
                )

    return finish_call(
        kernel, count, lambda g, j, meta: meta[REQ_OF, begin + g], states, state_specs, j, meta,
        partial, fresh, rows_all, column_decay, outs, f"finish_{begin}",
    )


def finish_call(
    kernel, count, request, states, state_specs, j, meta, partial, fresh, rows_all, column_decay,
    outs, name,
):
    tokens, width = partial.shape
    per_group, heads, size, depth = fresh.shape
    in_specs = [
        pl.BlockSpec((T_REQ, width), lambda g, j, meta: (request(g, j, meta), 0)),
        pl.BlockSpec((1, heads, size, depth), lambda g, j, meta: (request(g, j, meta), 0, 0, 0)),
        pl.BlockSpec((T_REQ, 2 * depth), lambda g, j, meta: (request(g, j, meta), 0)),
        pl.BlockSpec((T_REQ, heads), lambda g, j, meta: (request(g, j, meta), 0)),
    ] + state_specs
    operands = [j, meta, partial, fresh, rows_all, column_decay] + list(states)
    aliases = {}
    if outs is not None:
        aliases = {len(operands): 0, len(operands) + 1: 1}
        operands += list(outs)
        in_specs += [pl.BlockSpec(memory_space=pl.ANY) for _ in range(2)]
    return pl.pallas_call(
        kernel,
        grid_spec=pltpu.PrefetchScalarGridSpec(
            num_scalar_prefetch=2,
            grid=(count,),
            in_specs=in_specs,
            out_specs=(
                pl.BlockSpec((T_REQ, width), lambda g, j, meta: (request(g, j, meta), 0)),
                pl.BlockSpec(
                    (1, heads, size, depth), lambda g, j, meta: (request(g, j, meta), 0, 0, 0)
                ),
            ),
        ),
        out_shape=(
            jax.ShapeDtypeStruct((tokens, width), jnp.bfloat16),
            jax.ShapeDtypeStruct((per_group, heads, size, depth), jnp.bfloat16),
        ),
        input_output_aliases=aliases,
        cost_estimate=cost(count << 26, count * (3 << 20)),
        compiler_params=params(),
        name=name,
    )(*operands)


def finish_spread(
    first, others, limit, cache, j, meta, partial, fresh, rows_all, column_decay, outs
):
    shape = fresh.shape[1:]
    depth = shape[2]

    def place(g, meta):
        return jnp.maximum(jnp.minimum(g, meta[MISC, COUNT] - 1), 0)

    def request(g, j, meta):
        return jnp.where(
            meta[MISC, COUNT] > 0, meta[OVER, place(g, meta)], meta[REQ_OF, 0]
        )

    def own_slot(g, j, meta):
        return jnp.where(meta[MISC, COUNT] > 0, meta[OSLOT, 0], meta[MISC, SLOT])

    state_specs = final_specs(shape, own_slot) + [
        pl.BlockSpec(
            (1,) + shape, lambda g, j, meta: (jnp.maximum(place(g, meta) - 1, 0), 0, 0, 0)
        )
    ]

    def kernel(j, meta, partial, fresh, rows_in, column, *rest):
        out, final = rest[-2:]
        own, across, from_left, from_right, later = rest[:5]
        g = pl.program_id(0)
        count = meta[MISC, COUNT]
        present = meta[PRESENT, request(g, j, meta)] > 0
        which = jnp.where(count > 0, which_candidate(meta, meta[OHOLDER, 0]), 0)
        which = jnp.where(g > 0, jnp.where(g < count, 4, 5), which)
        picks = (own.at[0, 0, 0], across.at[0], from_left, from_right, later.at[0])
        for k, state in enumerate(picks):
            @pl.when(which == k)
            def _(state=state):
                add_state(
                    present, state, partial, fresh, rows_in[:, depth:], column[...], out, final
                )

    return finish_call(
        kernel, limit, request, [cache, *first, others], state_specs, j, meta, partial, fresh,
        rows_all, column_decay, outs, "finish_spread",
    )


def body(
    hidden, base_in_projection, state_input_matrix, state_output_matrix, head_step_size,
    head_decay_rate, head_skip_scale, convolution_weight, convolution_bias, adapter_down_weight,
    adapter_up_weight, adapter_home_group, adapter_group_index, state_space_cache,
    convolution_cache, prefix_holder_device, prefix_cache_slot, prefix_block_count,
):
    groups, devices = lax.axis_size("group"), lax.axis_size("dev")
    tokens, width = base_in_projection.shape
    per_group = tokens // T_REQ
    assert per_group == devices and devices & (devices - 1) == 0 == groups & (groups - 1)
    heads = head_step_size.shape[0]
    size, depth = state_space_cache.shape[2:]
    rank = adapter_down_weight.shape[1]
    taps = convolution_weight.shape[0]
    bf16, f32 = jnp.bfloat16, jnp.float32
    share = per_group // devices
    shape = (heads, size, depth)

    rows_all = lax.all_gather(
        jnp.concatenate([state_input_matrix, state_output_matrix], axis=1), "dev", axis=0,
        tiled=True,
    )
    meta = pl.pallas_call(
        functools.partial(plan_kernel, groups, devices, per_group),
        out_shape=jax.ShapeDtypeStruct(META_SHAPE, jnp.int32),
        in_specs=smem(5),
        out_specs=smem(1)[0],
        cost_estimate=cost(0, 1 << 16),
        name="plan",
    )(
        adapter_home_group.reshape(-1), adapter_group_index, prefix_holder_device.reshape(-1),
        prefix_cache_slot, prefix_block_count,
    )
    zero = jnp.zeros((1,), jnp.int32)

    down_got = swap_adapters(meta, adapter_down_weight, groups, "pack_down")

    cache = state_space_cache.reshape((state_space_cache.shape[0], devices // 2, 2) + shape)
    state_sends = pl.pallas_call(
        functools.partial(pack_state_kernel, devices),
        out_shape=tuple(jax.ShapeDtypeStruct(shape, bf16) for _ in range(devices - 1)),
        in_specs=smem(1) + [pl.BlockSpec(memory_space=pltpu.HBM)],
        out_specs=tuple(pl.BlockSpec(memory_space=pltpu.VMEM) for _ in range(devices - 1)),
        scratch_shapes=[pltpu.SemaphoreType.DMA((devices - 1,))],
        cost_estimate=cost(0, 4 << 20),
        compiler_params=params(),
        name="pack_state",
    )(meta, cache)
    state_gots = [
        lax.ppermute(x, "dev", [(s, s ^ (k + 1)) for s in range(devices)])
        for k, x in enumerate(state_sends)
    ]

    conv_send = pl.pallas_call(
        functools.partial(pack_conv_kernel, devices, width),
        out_shape=jax.ShapeDtypeStruct((devices, CONV_ROWS, width // 2), bf16),
        in_specs=smem(1) + [pl.BlockSpec(memory_space=pltpu.VMEM)],
        out_specs=pl.BlockSpec(memory_space=pltpu.VMEM),
        cost_estimate=cost(0, 1 << 19),
        name="pack_conv",
    )(meta, convolution_cache)
    conv_got = lax.all_to_all(conv_send, "dev", split_axis=0, concat_axis=0, tiled=True)

    spread = spread_entry(zero, meta, cache, devices)
    limit = per_group // 2
    spread_others = spread_rest(meta, cache, devices, limit)

    row_decay, column_decay = pl.pallas_call(
        prep_kernel,
        grid=(per_group,),
        out_shape=(
            jax.ShapeDtypeStruct((heads, tokens), f32),
            jax.ShapeDtypeStruct((tokens, heads), f32),
        ),
        in_specs=[
            pl.BlockSpec((heads, T_REQ), lambda r: (0, r)),
            pl.BlockSpec((heads, 1), lambda r: (0, 0)),
        ],
        out_specs=(
            pl.BlockSpec((heads, T_REQ), lambda r: (0, r)),
            pl.BlockSpec((T_REQ, heads), lambda r: (r, 0)),
        ),
        cost_estimate=cost(0, 4 << 20),
        name="prep",
    )(head_step_size, head_decay_rate.reshape(heads, 1))

    def table_specs(table):
        return [
            pl.BlockSpec((1,) + table.shape[1:], lambda r, meta: (meta[AINDEX, r], 0, 0))
        ] + [
            pl.BlockSpec(
                (1,) + table.shape[1:],
                lambda r, meta, k=k: (jnp.where(meta[DIST, r] == k, meta[ARANK, r], 0), 0, 0),
            )
            for k in range(1, groups)
        ]

    partial_down = pl.pallas_call(
        functools.partial(shrink_kernel, groups),
        grid_spec=pltpu.PrefetchScalarGridSpec(
            num_scalar_prefetch=1,
            grid=(per_group,),
            in_specs=[pl.BlockSpec((T_REQ, hidden.shape[1]), lambda r, meta: (r, 0))]
            + table_specs(adapter_down_weight),
            out_specs=pl.BlockSpec((1, rank, T_REQ), lambda r, meta: (r, 0, 0)),
        ),
        out_shape=jax.ShapeDtypeStruct((per_group, rank, T_REQ), bf16),
        cost_estimate=cost(2 * tokens * hidden.shape[1] * rank, 6 << 20),
        compiler_params=params(),
        name="shrink",
    )(meta, hidden, adapter_down_weight, *down_got)

    meta_late, _ = lax.optimization_barrier((meta, partial_down))
    up_got = swap_adapters(meta_late, adapter_up_weight, groups, "pack_up")

    parts = lax.all_to_all(partial_down, "dev", split_axis=0, concat_axis=0, tiled=True)
    summed = pl.pallas_call(
        sum_kernel,
        out_shape=jax.ShapeDtypeStruct((devices, share, rank, T_REQ), bf16),
        cost_estimate=cost(0, 1 << 19),
        name="sum_parts",
    )(parts.reshape(devices, share, rank, T_REQ))
    shrunk = lax.all_to_all(summed, "dev", split_axis=0, concat_axis=0, tiled=True)
    shrunk = shrunk.reshape(per_group, rank, T_REQ)

    channel = jnp.concatenate(
        [
            convolution_weight,
            convolution_bias.reshape(1, width),
            jnp.repeat(head_skip_scale, size).reshape(1, width),
            jnp.zeros((8 - taps - 2, width), f32),
        ],
        axis=0,
    )
    partial, fresh = pl.pallas_call(
        functools.partial(mix_kernel, groups, taps),
        grid_spec=pltpu.PrefetchScalarGridSpec(
            num_scalar_prefetch=1,
            grid=(per_group,),
            in_specs=[
                pl.BlockSpec((T_REQ, width), lambda r, meta: (r, 0)),
                pl.BlockSpec((1, rank, T_REQ), lambda r, meta: (r, 0, 0)),
            ] + table_specs(adapter_up_weight) + [
                pl.BlockSpec(
                    (1, CONV_ROWS, width // 2), lambda r, meta: (meta[HOLDER, r], 0, 0)
                ),
                pl.BlockSpec((8, width), lambda r, meta: (0, 0)),
                pl.BlockSpec((heads, T_REQ), lambda r, meta: (0, r)),
                pl.BlockSpec((T_REQ, heads), lambda r, meta: (r, 0)),
                pl.BlockSpec((T_REQ, 2 * depth), lambda r, meta: (r, 0)),
            ],
            out_specs=(
                pl.BlockSpec((T_REQ, width), lambda r, meta: (r, 0)),
                pl.BlockSpec((1,) + shape, lambda r, meta: (r, 0, 0, 0)),
            ),
            scratch_shapes=[
                pltpu.VMEM((T_REQ + 8, width), f32),
                pltpu.VMEM((T_REQ, T_REQ), f32),
            ],
        ),
        out_shape=(
            jax.ShapeDtypeStruct((tokens, width), f32),
            jax.ShapeDtypeStruct((per_group,) + shape, f32),
        ),
        cost_estimate=cost(4 << 30, 24 << 20, 16 << 20),
        compiler_params=params(),
        name="mix",
    )(
        meta, base_in_projection, shrunk, adapter_up_weight, *up_got, conv_got, channel,
        row_decay, column_decay, rows_all,
    )

    outs = None
    half = devices // 2
    for begin, states in (
        (0, [cache] + state_gots[:half - 1]),
        (half, state_gots[half - 1:half + 1]),
        (half + 2, state_gots[half + 1:]),
    ):
        outs = finish(
            begin, states, cache, zero, meta, partial, fresh, rows_all, column_decay, outs
        )
    return finish_spread(
        spread, spread_others, limit, cache, zero, meta, partial, fresh, rows_all, column_decay,
        outs,
    )


def solution(mesh):
    placed = (
        P("group", "dev"),
        P("group", "dev"),
        P(("group", "dev"), None),
        P(("group", "dev"), None),
        P("dev", "group"),
        P("dev"),
        P("dev"),
        P(None, "dev"),
        P("dev"),
        P("group", None, "dev"),
        P("group", None, "dev"),
        P(),
        P(),
        P(("group", "dev"), None, None, None),
        P(("group", "dev"), None, None),
        P(),
        P(),
        P(),
    )
    return jax.shard_map(
        body,
        mesh=mesh,
        in_specs=placed,
        out_specs=(P("group", "dev"), P("group", "dev", None, None)),
        check_vma=False,
    )
```

```python
import functools
import math

import jax
import jax.numpy as jnp
from jax import lax
from jax.experimental import pallas as pl
from jax.experimental.pallas import tpu as pltpu
from jax.sharding import PartitionSpec as P

T_REQ = 256
CAP = 2
ACAP = 4
LOG2E = math.log2(math.e)
NT = (((1,), (1,)), ((), ()))
TN = (((0,), (0,)), ((), ()))
VMEM_LIMIT = 48 * 1024 * 1024

DIST, ARANK, AINDEX, PRESENT, POS_REQ, POS_VALID, OSLOT, OHOLDER, MISC, SEND = range(10)
MOST, ME, SLOT = range(3)
META_SHAPE = (16, 64)


def cost(flops, nbytes, transcendentals=0):
    return pl.CostEstimate(
        flops=int(flops), bytes_accessed=int(nbytes), transcendentals=int(transcendentals)
    )


def params():
    return pltpu.CompilerParams(vmem_limit_bytes=VMEM_LIMIT)


def smem(count):
    return [pl.BlockSpec(memory_space=pltpu.SMEM) for _ in range(count)]


def anywhere(count):
    return [pl.BlockSpec(memory_space=pl.ANY) for _ in range(count)]


def as_int(flag):
    return flag.astype(jnp.int32)


def ranks_of(labels):
    ranks = []
    for q, label in enumerate(labels):
        total = jnp.int32(0)
        for other in labels[:q]:
            total = total + as_int(other == label)
        ranks.append(total)
    return ranks


def plan_kernel(groups, devices, per_group, home, index, holder, slot, blocks, meta):
    my_group = lax.axis_index("group")
    me = lax.axis_index("dev")
    first = my_group * per_group
    limit = per_group // 2
    for j in range(limit):
        meta[POS_REQ, devices + j] = jnp.int32(-1)
        meta[POS_VALID, devices + j] = jnp.int32(0)
        meta[OSLOT, j] = jnp.int32(0)
        meta[OHOLDER, j] = jnp.int32(0)

    homes = [home[first + q] for q in range(per_group)]
    for q, rank in enumerate(ranks_of(homes)):
        own = homes[q] == my_group
        meta[DIST, q] = lax.bitwise_xor(homes[q], my_group)
        meta[ARANK, q] = jnp.where(own, 0, rank)
        meta[AINDEX, q] = jnp.where(own, index[first + q], 0)
        meta[PRESENT, q] = as_int(blocks[first + q] > 0)
    for k in range(1, groups):
        theirs = lax.bitwise_xor(my_group, k) * per_group
        seen = jnp.int32(0)
        chosen = [jnp.int32(0) for _ in range(ACAP)]
        for q in range(per_group):
            hit = home[theirs + q] == my_group
            value = index[theirs + q]
            for c in range(ACAP):
                chosen[c] = jnp.where(hit & (seen == c), value, chosen[c])
            seen = seen + as_int(hit)
        for c in range(ACAP):
            meta[SEND, (k - 1) * ACAP + c] = chosen[c]

    holders = [holder[first + q] for q in range(per_group)]
    ranks = ranks_of(holders)
    count = jnp.int32(0)
    my_slot = jnp.int32(0)
    for q in range(per_group):
        my_slot = jnp.where((holders[q] == me) & (ranks[q] == 0), slot[first + q], my_slot)

        @pl.when(ranks[q] > 0)
        def _():
            meta[POS_REQ, devices + count] = jnp.int32(q)
            meta[POS_VALID, devices + count] = jnp.int32(1)
            meta[OSLOT, count] = slot[first + q]
            meta[OHOLDER, count] = holders[q]

        count = count + as_int(ranks[q] > 0)
    spread = meta[POS_REQ, devices]
    requests = []
    for d in range(devices):
        source = lax.bitwise_xor(me, d)
        request = jnp.int32(-1)
        for q in range(per_group):
            request = jnp.where((holders[q] == source) & (ranks[q] == 0), q, request)
        meta[POS_VALID, d] = as_int(request >= 0)
        requests.append(request)
    requests += [meta[POS_REQ, devices + j] for j in range(limit)]
    for begin, end in ((0, devices // 2), (devices // 2, devices + limit)):
        last = jnp.int32(-1)
        filled = []
        for p in range(begin, end):
            last = jnp.where(requests[p] >= 0, requests[p], last)
            filled.append(last)
        following = jnp.maximum(spread, 0)
        for p in reversed(range(begin, end)):
            following = jnp.where(filled[p - begin] >= 0, filled[p - begin], following)
            meta[POS_REQ, p] = following
    most = jnp.int32(0)
    for g in range(groups):
        labels = [holder[g * per_group + q] for q in range(per_group)]
        total = jnp.int32(0)
        for rank in ranks_of(labels):
            total = total + as_int(rank > 0)
        most = jnp.maximum(most, total)
    meta[MISC, MOST] = most
    meta[MISC, ME] = me
    meta[MISC, SLOT] = my_slot


def pack_adapter_kernel(groups, meta, table, *rest):
    outs, sems = rest[-groups:-1], rest[-1]
    copies = []
    for k in range(1, groups):
        for c in range(ACAP):
            chosen = meta[SEND, (k - 1) * ACAP + c]
            copy = pltpu.make_async_copy(
                table.at[chosen], outs[k - 1].at[c], sems.at[(k - 1) * ACAP + c]
            )
            copy.start()
            copies.append(copy)
    for copy in copies:
        copy.wait()


def pack_adapters(meta, table, groups, name, after=()):
    return pl.pallas_call(
        functools.partial(pack_adapter_kernel, groups),
        out_shape=tuple(
            jax.ShapeDtypeStruct((ACAP,) + table.shape[1:], table.dtype) for _ in range(groups - 1)
        ),
        in_specs=smem(1) + [pl.BlockSpec(memory_space=pltpu.HBM)] + anywhere(len(after)),
        out_specs=tuple(pl.BlockSpec(memory_space=pltpu.VMEM) for _ in range(groups - 1)),
        scratch_shapes=[pltpu.SemaphoreType.DMA(((groups - 1) * ACAP,))],
        cost_estimate=cost(0, 2 * (groups - 1) * ACAP * table.shape[1] * table.shape[2] * 2),
        compiler_params=params(),
        name=name,
    )(meta, table, *after)


def swap(packed, groups):
    return [
        lax.ppermute(packed[k - 1], "group", [(g, g ^ k) for g in range(groups)])
        for k in range(1, groups)
    ]


def copy_conv(conv, slot, target, width, out, at):
    parts = width // 128
    for k in range(conv.shape[1]):
        for part in range(parts):
            begin = pl.multiple_of(target * width + part * 128, 128)
            out[at + k * parts + part:at + k * parts + part + 1, :] = (
                conv[slot, k:k + 1, pl.ds(begin, 128)]
            )


def pack_state_kernel(devices, width, meta, cache, conv, *rest):
    outs, sems = rest[-devices - 1:-1], rest[-1]
    me, slot = meta[MISC, ME], meta[MISC, SLOT]
    state_rows = cache.shape[3]
    copies = []
    for d in reversed(range(devices)):
        target = lax.bitwise_xor(me, d)
        copy = pltpu.make_async_copy(
            cache.at[slot, target // 2, target % 2], outs[d].at[pl.ds(0, state_rows)], sems.at[d]
        )
        copy.start()
        copies.append(copy)
    for d in range(devices):
        copy_conv(conv, slot, lax.bitwise_xor(me, d), width, outs[d], state_rows)
    for copy in copies:
        copy.wait()


def pack_across_kernel(lines, width, j, meta, cache, conv, *rest):
    across, own, sems = rest[-3:]
    x, slot = meta[MISC, ME] % 2, meta[OSLOT, j[0]]
    state_rows = cache.shape[3]
    copies = []
    for k, (out, place) in enumerate(((across, 1 - x), (own, x))):
        copy = pltpu.make_async_copy(
            cache.at[slot, :, place], out.at[:, pl.ds(0, state_rows)], sems.at[k]
        )
        copy.start()
        copies.append(copy)
    for out, place in ((across, 1 - x), (own, x)):
        for m in range(lines):
            copy_conv(conv, slot, 2 * m + place, width, out.at[m], state_rows)
    for copy in copies:
        copy.wait()


def pick_kernel(step, lines, j, meta, own_r, over_r, own_l, over_l, *rest):
    out_r, out_l = rest[-2:]
    me = meta[MISC, ME]
    source = meta[OHOLDER, j[0]]
    same = source // 2 == me // 2
    mine = same & (source % 2 == me % 2)
    across = same & (source % 2 != me % 2)

    @pl.when(mine)
    def _():
        out_r[...] = own_r[0]
        out_l[...] = own_l[0]

    @pl.when(across)
    def _():
        out_r[...] = over_r[0]
        out_l[...] = over_l[0]

    @pl.when(jnp.logical_not(same))
    def _():
        if step > 1:
            out_r[...] = rest[0][...]
            out_l[...] = rest[1][...]
        else:
            out_r[...] = jnp.zeros_like(out_r)
            out_l[...] = jnp.zeros_like(out_l)


def right_block(meta, step, lines):
    return jnp.clip(lines + meta[MISC, ME] // 2 - step, 0, lines - 1)


def left_block(meta, step, lines):
    return jnp.clip(meta[MISC, ME] // 2 + step - lines, 0, lines - 1)


def pack_across(j, meta, cache, conv, devices, width, after=()):
    lines = devices // 2
    shape = chunk_shape(cache, conv, width)
    return pl.pallas_call(
        functools.partial(pack_across_kernel, lines, width),
        out_shape=tuple(jax.ShapeDtypeStruct((lines,) + shape, cache.dtype) for _ in range(2)),
        in_specs=smem(2) + [
            pl.BlockSpec(memory_space=pltpu.HBM), pl.BlockSpec(memory_space=pltpu.VMEM)
        ] + anywhere(len(after)),
        out_specs=tuple(pl.BlockSpec(memory_space=pltpu.VMEM) for _ in range(2)),
        scratch_shapes=[pltpu.SemaphoreType.DMA((2,))],
        cost_estimate=cost(0, 4 << 20),
        compiler_params=params(),
        name="pack_across",
    )(j, meta, cache, conv, *after)


def spread_entry(j, meta, packed, devices):
    lines = devices // 2
    send, own = packed
    shape = own.shape[1:]
    across = lax.ppermute(send, "dev", [(d, d ^ 1) for d in range(devices)])
    from_left = from_right = None
    whole = pl.BlockSpec(shape, lambda g, j, meta: (0, 0))
    for step in range(1, lines):
        blocks = [
            pl.BlockSpec(
                (1,) + shape, lambda g, j, meta, at=at, step=step: (at(meta, step, lines), 0, 0)
            )
            for at in (right_block, left_block)
        ]
        operands = [own, across, own, across]
        in_specs = [blocks[0], blocks[0], blocks[1], blocks[1]]
        if step > 1:
            operands += [from_left, from_right]
            in_specs += [whole, whole]
        to_right, to_left = pl.pallas_call(
            functools.partial(pick_kernel, step, lines),
            grid_spec=pltpu.PrefetchScalarGridSpec(
                num_scalar_prefetch=2, grid=(1,), in_specs=in_specs, out_specs=(whole, whole)
            ),
            out_shape=tuple(jax.ShapeDtypeStruct(shape, own.dtype) for _ in range(2)),
            cost_estimate=cost(0, 2 << 20),
            compiler_params=params(),
            name=f"pick_{step}",
        )(j, meta, *operands)
        from_left = lax.ppermute(
            to_right, "dev",
            [(2 * i + x, 2 * i + 2 + x) for i in range(step) for x in range(2)],
        )
        from_right = lax.ppermute(
            to_left, "dev",
            [(devices - 1 - (2 * i + x), devices - 3 - (2 * i + x))
             for i in range(step) for x in range(2)],
        )
    return own, across, from_left, from_right


def final_specs(shape):
    line = pl.BlockSpec((1,) + shape, lambda g, j, meta: (meta[MISC, ME] // 2, 0, 0))
    whole = pl.BlockSpec(shape, lambda g, j, meta: (0, 0))
    return [line, line, whole, whole]


def which_candidate(meta, source):
    me = meta[MISC, ME]
    same = source // 2 == me // 2
    mine = same & (source % 2 == me % 2)
    return jnp.where(mine, 0, jnp.where(same, 1, jnp.where(source // 2 < me // 2, 2, 3)))


def final_kernel(j, meta, own, across, from_left, from_right, out):
    which = which_candidate(meta, meta[OHOLDER, j[0]])
    picks = (own.at[0], across.at[0], from_left, from_right)
    for k, pick in enumerate(picks):
        @pl.when(which == k)
        def _(pick=pick):
            out[...] = pick[...]


def spread_rest(meta, cache, conv, devices, width, limit):
    shape = chunk_shape(cache, conv, width)

    def one(j, held):
        jj = j.reshape(1)
        packed = pack_across(jj, meta, cache, conv, devices, width)
        got = spread_entry(jj, meta, packed, devices)
        block = pl.pallas_call(
            final_kernel,
            grid_spec=pltpu.PrefetchScalarGridSpec(
                num_scalar_prefetch=2,
                grid=(1,),
                in_specs=final_specs(shape),
                out_specs=pl.BlockSpec(shape, lambda g, j, meta: (0, 0)),
            ),
            out_shape=jax.ShapeDtypeStruct(shape, cache.dtype),
            compiler_params=params(),
            name="final_pick",
        )(jj, meta, *got)
        return lax.dynamic_update_slice_in_dim(held, block[None], j - 1, 0)

    held = jnp.zeros((limit - 1,) + shape, cache.dtype)
    return lax.fori_loop(jnp.int32(1), meta[MISC, MOST], one, held)


def shrink_kernel(groups, meta, hidden, *rest):
    tables, out = rest[:groups], rest[-1]
    dist = meta[DIST, pl.program_id(0)]
    for k in range(groups):
        @pl.when(dist == k)
        def _(k=k):
            part = lax.dot_general(
                hidden[...], tables[k][0], NT, preferred_element_type=jnp.float32
            )
            out[0] = part.T.astype(out.dtype)


def sum_kernel(parts, out):
    total = parts[0].astype(jnp.float32)
    for k in range(1, parts.shape[0]):
        total = total + parts[k].astype(jnp.float32)
    total = total.astype(out.dtype)
    for k in range(out.shape[0]):
        out[k] = total


def prep_kernel(per_group, rates, skips, steps, taps_in, bias, rows_out, column_out, channel):
    heads, tokens = steps.shape
    length = tokens // per_group
    rate = jnp.zeros((heads, length), jnp.float32)
    place = lax.broadcasted_iota(jnp.int32, rate.shape, 0)
    for h in range(heads):
        rate = jnp.where(place == h, rates[h] * (-LOG2E), rate)
    step = [steps[:, r * length:(r + 1) * length] for r in range(per_group)]
    x = jnp.concatenate([part * rate for part in step], axis=0)
    high = x.astype(jnp.bfloat16)
    rest = x - high.astype(jnp.float32)
    middle = rest.astype(jnp.bfloat16)
    low = (rest - middle.astype(jnp.float32)).astype(jnp.bfloat16)
    s = lax.broadcasted_iota(jnp.int32, (length, length), 0)
    t = lax.broadcasted_iota(jnp.int32, (length, length), 1)
    ones = (s <= t).astype(jnp.float32).astype(jnp.bfloat16)
    total = jnp.dot(low, ones, preferred_element_type=jnp.float32)
    total = total + jnp.dot(middle, ones, preferred_element_type=jnp.float32)
    total = total + jnp.dot(high, ones, preferred_element_type=jnp.float32)
    shifted = total - jnp.log2(jnp.concatenate(step, axis=0))
    columns = shifted.T
    for r in range(per_group):
        rows_out[:heads, r * length:(r + 1) * length] = total[r * heads:(r + 1) * heads]
        rows_out[heads:, r * length:(r + 1) * length] = shifted[r * heads:(r + 1) * heads]
        column_out[r] = columns[:, r * heads:(r + 1) * heads]
    taps, width = taps_in.shape
    head_of = lax.broadcasted_iota(jnp.int32, (1, width), 1) // (width // heads)
    skip = jnp.zeros((1, width), jnp.float32)
    for h in range(heads):
        skip = jnp.where(head_of == h, skips[h], skip)
    channel[:taps] = taps_in[...]
    channel[taps:taps + 1] = bias[...]
    channel[taps + 1:taps + 2] = skip


def mix_kernel(
    groups, taps, begin, direct, spread, size, meta, base, shrunk, *rest
):
    tables, rest = rest[:groups], rest[groups:]
    channel, rows_decay, column, rows_in = rest[:4]
    chunks = rest[4:4 + direct + (5 if spread else 0)]
    out, final, extended, scores, cur, carried, weighted = rest[-7:]
    g = pl.program_id(0)
    position = begin + g
    r = meta[POS_REQ, position]
    length, width = base.shape
    half = length // 2
    heads = width // size
    depth = cur.shape[1]
    few = taps - 1
    parts = width // 128
    f32, bf16 = jnp.float32, jnp.bfloat16

    which = g
    picks = list(chunks[:direct])
    if spread:
        j = g - direct
        late = jnp.where(j == 0, direct + which_candidate(meta, meta[OHOLDER, 0]), direct + 4)
        which = jnp.where(j >= 0, late, which)
        own, across, from_left, from_right, others = chunks[direct:]
        picks += [own.at[0], across.at[0], from_left, from_right, others.at[0]]

    @pl.when(meta[POS_VALID, position] > 0)
    def _():
        present = meta[PRESENT, r] > 0
        for k, pick in enumerate(picks):
            @pl.when(which == k)
            def _(pick=pick):
                cur[...] = jnp.where(present, pick[...], jnp.zeros_like(cur))

        dist = meta[DIST, r]
        for k in range(groups):
            @pl.when(dist == k)
            def _(k=k):
                extended[8:, :] = base[...].astype(f32) + lax.dot_general(
                    shrunk[0], tables[k][0], TN, preferred_element_type=f32
                )

        before = cur[width:, :].astype(f32)
        for k in range(few):
            for part in range(parts):
                extended[8 - few + k:9 - few + k, part * 128:(part + 1) * 128] = (
                    before[k * parts + part:k * parts + part + 1, :]
                )

        write, read = rows_in[:, :depth], rows_in[:, depth:]
        all_scores = lax.dot_general(write, read, NT, preferred_element_type=f32)
        s = lax.broadcasted_iota(jnp.int32, (length, length), 0)
        t = lax.broadcasted_iota(jnp.int32, (length, length), 1)
        scores[...] = jnp.where(s <= t, all_scores, 0.0)
        carried[...] = lax.dot_general(cur[:width, :], read, NT, preferred_element_type=f32)

        to_here, from_here = rows_decay[:heads, :], rows_decay[heads:, :]
        end = jnp.broadcast_to(to_here[:, length - 1:length], (heads, length))
        grown = jnp.exp2(to_here)
        to_end = jnp.exp2(end - from_here)
        kept = jnp.exp2(end[:, :depth])
        corner = jnp.zeros((half, half), bf16)
        for pair in range(heads // 2):
            lo, hi = pair * 2 * size, (pair + 1) * 2 * size
            v = channel[taps:taps + 1, lo:hi]
            for k in range(taps):
                first = 8 - few + k
                v = v + channel[k:k + 1, lo:hi] * extended[first:first + length, lo:hi]
            activated = v * (0.5 + 0.5 * jnp.tanh(0.5 * v))
            act = activated.astype(bf16).T
            sums = []
            for i in range(2):
                h = 2 * pair + i
                a = act[i * size:(i + 1) * size, :]
                ds = jnp.broadcast_to(column[0, :, h:h + 1], (length, half))
                dt0, dt1 = to_here[h:h + 1, :half], to_here[h:h + 1, half:]
                m00 = jnp.exp2(jnp.minimum(dt0 - ds[:half], 126.0)) * scores[:half, :half]
                m01 = jnp.exp2(dt1 - ds[:half]) * scores[:half, half:]
                m11 = jnp.exp2(jnp.minimum(dt1 - ds[half:], 126.0)) * scores[half:, half:]
                mixing = jnp.concatenate(
                    [
                        jnp.concatenate([m00.astype(bf16), m01.astype(bf16)], axis=1),
                        jnp.concatenate([corner, m11.astype(bf16)], axis=1),
                    ],
                    axis=0,
                )
                total = jnp.dot(a, mixing, preferred_element_type=f32)
                begin_h = h * size
                sums.append(total + carried[begin_h:begin_h + size, :] * grown[h:h + 1, :])
                weighted[begin_h:begin_h + size, :] = (
                    a.astype(f32) * to_end[h:h + 1, :]
                ).astype(bf16)
            skipped = channel[taps + 1:taps + 2, lo:hi] * activated
            out[:, lo:hi] = (jnp.concatenate(sums, axis=0).T + skipped).astype(out.dtype)
        fresh = jnp.dot(weighted[...], write, preferred_element_type=f32)
        for h in range(heads):
            rows = slice(h * size, (h + 1) * size)
            old = cur[rows, :].astype(f32) * kept[h:h + 1, :]
            final[0, rows, :] = (fresh[rows, :] + old).astype(final.dtype)


def chunk_shape(cache, conv, width):
    conv_rows = conv.shape[1] * (width // 128)
    return (cache.shape[3] + -(-conv_rows // 16) * 16, cache.shape[4])


def body(
    hidden, base_in_projection, state_input_matrix, state_output_matrix, head_step_size,
    head_decay_rate, head_skip_scale, convolution_weight, convolution_bias, adapter_down_weight,
    adapter_up_weight, adapter_home_group, adapter_group_index, state_space_cache,
    convolution_cache, prefix_holder_device, prefix_cache_slot, prefix_block_count,
):
    groups, devices = lax.axis_size("group"), lax.axis_size("dev")
    tokens, width = base_in_projection.shape
    per_group = tokens // T_REQ
    assert per_group == devices and devices & (devices - 1) == 0 == groups & (groups - 1)
    heads = head_step_size.shape[0]
    size, depth = state_space_cache.shape[2:]
    rank = adapter_down_weight.shape[1]
    taps = convolution_weight.shape[0]
    bf16, f32 = jnp.bfloat16, jnp.float32
    limit = per_group // 2
    lines = devices // 2

    rows_all = lax.all_gather(
        jnp.concatenate([state_input_matrix, state_output_matrix], axis=1), "dev", axis=0,
        tiled=True,
    )
    meta = pl.pallas_call(
        functools.partial(plan_kernel, groups, devices, per_group),
        out_shape=jax.ShapeDtypeStruct(META_SHAPE, jnp.int32),
        in_specs=smem(5),
        out_specs=smem(1)[0],
        cost_estimate=cost(0, 1 << 16),
        name="plan",
    )(
        adapter_home_group.reshape(-1), adapter_group_index, prefix_holder_device.reshape(-1),
        prefix_cache_slot, prefix_block_count,
    )
    zero = jnp.zeros((1,), jnp.int32)

    down_send = pack_adapters(meta, adapter_down_weight, groups, "pack_down")
    down_got = swap(down_send, groups)

    cache = state_space_cache.reshape(
        state_space_cache.shape[0], lines, 2, heads * size, depth
    )
    conv = convolution_cache
    shape = chunk_shape(cache, conv, width)
    chunks = pl.pallas_call(
        functools.partial(pack_state_kernel, devices, width),
        out_shape=tuple(jax.ShapeDtypeStruct(shape, bf16) for _ in range(devices)),
        in_specs=smem(1) + [
            pl.BlockSpec(memory_space=pltpu.HBM), pl.BlockSpec(memory_space=pltpu.VMEM)
        ] + anywhere(1),
        out_specs=tuple(pl.BlockSpec(memory_space=pltpu.VMEM) for _ in range(devices)),
        scratch_shapes=[pltpu.SemaphoreType.DMA((devices,))],
        cost_estimate=cost(0, 4 << 20),
        compiler_params=params(),
        name="pack_state",
    )(meta, cache, conv, down_send[0])
    got = [chunks[0]] + [
        lax.ppermute(chunks[d], "dev", [(s, s ^ d) for s in range(devices)])
        for d in range(1, devices)
    ]

    up_send = pack_adapters(meta, adapter_up_weight, groups, "pack_up", (chunks[1],))
    up_got = swap(up_send, groups)

    across = pack_across(zero, meta, cache, conv, devices, width, (up_send[0],))
    spread = spread_entry(zero, meta, across, devices)
    spread_others = spread_rest(meta, cache, conv, devices, width, limit)

    rows_decay, column_decay, channel = pl.pallas_call(
        functools.partial(prep_kernel, per_group),
        out_shape=(
            jax.ShapeDtypeStruct((2 * heads, tokens), f32),
            jax.ShapeDtypeStruct((per_group, T_REQ, heads), f32),
            jax.ShapeDtypeStruct((8, width), f32),
        ),
        in_specs=smem(2) + [pl.BlockSpec(memory_space=pltpu.VMEM) for _ in range(3)],
        out_specs=tuple(pl.BlockSpec(memory_space=pltpu.VMEM) for _ in range(3)),
        cost_estimate=cost(0, 4 << 20),
        compiler_params=params(),
        name="prep",
    )(
        head_decay_rate, head_skip_scale, head_step_size, convolution_weight,
        convolution_bias.reshape(1, width),
    )

    def table_specs(table, request):
        return [
            pl.BlockSpec(
                (1,) + table.shape[1:], lambda g, meta: (meta[AINDEX, request(g, meta)], 0, 0)
            )
        ] + [
            pl.BlockSpec(
                (1,) + table.shape[1:],
                lambda g, meta, k=k: (
                    jnp.where(
                        meta[DIST, request(g, meta)] == k, meta[ARANK, request(g, meta)], 0
                    ), 0, 0,
                ),
            )
            for k in range(1, groups)
        ]

    partial_down = pl.pallas_call(
        functools.partial(shrink_kernel, groups),
        grid_spec=pltpu.PrefetchScalarGridSpec(
            num_scalar_prefetch=1,
            grid=(per_group,),
            in_specs=[pl.BlockSpec((T_REQ, hidden.shape[1]), lambda r, meta: (r, 0))]
            + table_specs(adapter_down_weight, lambda r, meta: r) + anywhere(2),
            out_specs=pl.BlockSpec((1, rank, T_REQ), lambda r, meta: (r, 0, 0)),
        ),
        out_shape=jax.ShapeDtypeStruct((per_group, rank, T_REQ), bf16),
        cost_estimate=cost(2 * tokens * hidden.shape[1] * rank, 6 << 20),
        compiler_params=params(),
        name="shrink",
    )(meta, hidden, adapter_down_weight, *down_got, across[0], channel)

    parts = lax.all_to_all(partial_down, "dev", split_axis=0, concat_axis=0, tiled=True)
    summed = pl.pallas_call(
        sum_kernel,
        out_shape=jax.ShapeDtypeStruct((devices, 1, rank, T_REQ), bf16),
        cost_estimate=cost(0, 1 << 19),
        name="sum_parts",
    )(parts.reshape(devices, 1, rank, T_REQ))
    shrunk = lax.all_to_all(summed, "dev", split_axis=0, concat_axis=0, tiled=True)
    shrunk = shrunk.reshape(per_group, rank, T_REQ)

    outs = None
    whole = pl.BlockSpec(shape, lambda g, meta: (0, 0))
    for begin, direct, late in ((0, lines, False), (lines, devices - lines, True)):
        steps = direct + (limit if late else 0)

        def request(g, meta, begin=begin):
            return meta[POS_REQ, begin + g]

        in_specs = [
            pl.BlockSpec((T_REQ, width), lambda g, meta: (request(g, meta), 0)),
            pl.BlockSpec((1, rank, T_REQ), lambda g, meta: (request(g, meta), 0, 0)),
        ] + table_specs(adapter_up_weight, request) + [
            pl.BlockSpec((8, width), lambda g, meta: (0, 0)),
            pl.BlockSpec((2 * heads, T_REQ), lambda g, meta: (0, request(g, meta))),
            pl.BlockSpec((1, T_REQ, heads), lambda g, meta: (request(g, meta), 0, 0)),
            pl.BlockSpec((T_REQ, 2 * depth), lambda g, meta: (request(g, meta), 0)),
        ] + [whole] * direct
        operands = [
            meta, base_in_projection, shrunk, adapter_up_weight, *up_got, channel, rows_decay,
            column_decay, rows_all, *got[begin:begin + direct],
        ]
        if late:
            line = pl.BlockSpec((1,) + shape, lambda g, meta: (meta[MISC, ME] // 2, 0, 0))
            in_specs += [
                line, line, whole, whole,
                pl.BlockSpec(
                    (1,) + shape,
                    lambda g, meta, d=direct: (jnp.clip(g - d - 1, 0, limit - 2), 0, 0),
                ),
            ]
            operands += [*spread, spread_others]
        aliases = {}
        if outs is not None:
            aliases = {len(operands): 0, len(operands) + 1: 1}
            operands += list(outs)
            in_specs += anywhere(2)
        outs = pl.pallas_call(
            functools.partial(mix_kernel, groups, taps, begin, direct, late, size),
            grid_spec=pltpu.PrefetchScalarGridSpec(
                num_scalar_prefetch=1,
                grid=(steps,),
                in_specs=in_specs,
                out_specs=(
                    pl.BlockSpec((T_REQ, width), lambda g, meta: (request(g, meta), 0)),
                    pl.BlockSpec(
                        (1, heads * size, depth), lambda g, meta: (request(g, meta), 0, 0)
                    ),
                ),
                scratch_shapes=[
                    pltpu.VMEM((T_REQ + 8, width), f32),
                    pltpu.VMEM((T_REQ, T_REQ), f32),
                    pltpu.VMEM(shape, bf16),
                    pltpu.VMEM((width, T_REQ), f32),
                    pltpu.VMEM((width, T_REQ), bf16),
                ],
            ),
            out_shape=(
                jax.ShapeDtypeStruct((tokens, width), bf16),
                jax.ShapeDtypeStruct((per_group, heads * size, depth), bf16),
            ),
            input_output_aliases=aliases,
            cost_estimate=cost(2 << 30, 12 << 20, 8 << 20),
            compiler_params=params(),
            name=f"mix_{begin}",
        )(*operands)
    return outs[0], outs[1].reshape(per_group, heads, size, depth)


def solution(mesh):
    placed = (
        P("group", "dev"),
        P("group", "dev"),
        P(("group", "dev"), None),
        P(("group", "dev"), None),
        P("dev", "group"),
        P("dev"),
        P("dev"),
        P(None, "dev"),
        P("dev"),
        P("group", None, "dev"),
        P("group", None, "dev"),
        P(),
        P(),
        P(("group", "dev"), None, None, None),
        P(("group", "dev"), None, None),
        P(),
        P(),
        P(),
    )
    return jax.shard_map(
        body,
        mesh=mesh,
        in_specs=placed,
        out_specs=(P("group", "dev"), P("group", "dev", None, None)),
        check_vma=False,
    )
```

```python
import functools
import math

import jax
import jax.numpy as jnp
from jax import lax
from jax.experimental import pallas as pl
from jax.experimental.pallas import tpu as pltpu
from jax.sharding import PartitionSpec as P

T_REQ = 256
CAP = 2
ACAP = 4
LOG2E = math.log2(math.e)
NT = (((1,), (1,)), ((), ()))
TN = (((0,), (0,)), ((), ()))
VMEM_LIMIT = 48 * 1024 * 1024

DIST, ARANK, AINDEX, PRESENT, POS_REQ, POS_VALID, OSLOT, OHOLDER, MISC, SEND = range(10)
MOST, ME, SLOT, SPREAD = range(4)
META_SHAPE = (16, 64)


def cost():
    return pl.CostEstimate(flops=1, bytes_accessed=1, transcendentals=0)


def params():
    return pltpu.CompilerParams(vmem_limit_bytes=VMEM_LIMIT)


def smem(count):
    return [pl.BlockSpec(memory_space=pltpu.SMEM) for _ in range(count)]


def vmem(count):
    return [pl.BlockSpec(memory_space=pltpu.VMEM) for _ in range(count)]


def pinned(count):
    return [pl.BlockSpec(memory_space=pltpu.HBM) for _ in range(count)]


def anywhere(count):
    return [pl.BlockSpec(memory_space=pl.ANY) for _ in range(count)]


def as_int(flag):
    return flag.astype(jnp.int32)


def ranks_of(labels):
    ranks = []
    for q, label in enumerate(labels):
        total = jnp.int32(0)
        for other in labels[:q]:
            total = total + as_int(other == label)
        ranks.append(total)
    return ranks


def plan(groups, devices, per_group, home, index, holder, slot, blocks, meta):
    my_group = lax.axis_index("group")
    me = lax.axis_index("dev")
    first = my_group * per_group
    limit = per_group // 2
    for j in range(limit):
        meta[POS_REQ, devices + j] = jnp.int32(-1)
        meta[POS_VALID, devices + j] = jnp.int32(0)
        meta[OSLOT, j] = jnp.int32(0)
        meta[OHOLDER, j] = jnp.int32(0)

    homes = [home[first + q] for q in range(per_group)]
    for q, rank in enumerate(ranks_of(homes)):
        own = homes[q] == my_group
        meta[DIST, q] = lax.bitwise_xor(homes[q], my_group)
        meta[ARANK, q] = jnp.where(own, 0, rank)
        meta[AINDEX, q] = jnp.where(own, index[first + q], 0)
        meta[PRESENT, q] = as_int(blocks[first + q] > 0)
    for k in range(1, groups):
        theirs = lax.bitwise_xor(my_group, k) * per_group
        seen = jnp.int32(0)
        chosen = [jnp.int32(0) for _ in range(ACAP)]
        for q in range(per_group):
            hit = home[theirs + q] == my_group
            value = index[theirs + q]
            for c in range(ACAP):
                chosen[c] = jnp.where(hit & (seen == c), value, chosen[c])
            seen = seen + as_int(hit)
        for c in range(ACAP):
            meta[SEND, (k - 1) * ACAP + c] = chosen[c]

    holders = [holder[first + q] for q in range(per_group)]
    ranks = ranks_of(holders)
    count = jnp.int32(0)
    my_slot = jnp.int32(0)
    for q in range(per_group):
        my_slot = jnp.where((holders[q] == me) & (ranks[q] == 0), slot[first + q], my_slot)

        @pl.when(ranks[q] > 0)
        def _():
            meta[POS_REQ, devices + count] = jnp.int32(q)
            meta[POS_VALID, devices + count] = jnp.int32(1)
            meta[OSLOT, count] = slot[first + q]
            meta[OHOLDER, count] = holders[q]

        count = count + as_int(ranks[q] > 0)
    spread = meta[POS_REQ, devices]
    requests = []
    for d in range(devices):
        source = lax.bitwise_xor(me, d)
        request = jnp.int32(-1)
        for q in range(per_group):
            request = jnp.where((holders[q] == source) & (ranks[q] == 0), q, request)
        meta[POS_VALID, d] = as_int(request >= 0)
        requests.append(request)
    requests += [meta[POS_REQ, devices + j] for j in range(limit)]
    for begin, end in ((0, devices // 2), (devices // 2, devices)):
        last = jnp.int32(-1)
        filled = []
        for p in range(begin, end):
            last = jnp.where(requests[p] >= 0, requests[p], last)
            filled.append(last)
        following = jnp.maximum(spread, 0)
        for p in reversed(range(begin, end)):
            following = jnp.where(filled[p - begin] >= 0, filled[p - begin], following)
            meta[POS_REQ, p] = following
    meta[MISC, SPREAD] = as_int(count > 0)
    meta[POS_VALID, devices] = jnp.int32(1)
    for j in range(limit):
        meta[POS_REQ, devices + j] = jnp.where(
            j < count, requests[devices + j],
            jnp.where(count > 0, meta[POS_REQ, devices + max(j - 1, 0)], requests[0]),
        )
    most = jnp.int32(0)
    for g in range(groups):
        labels = [holder[g * per_group + q] for q in range(per_group)]
        total = jnp.int32(0)
        for rank in ranks_of(labels):
            total = total + as_int(rank > 0)
        most = jnp.maximum(most, total)
    meta[MISC, MOST] = most
    meta[MISC, ME] = me
    meta[MISC, SLOT] = my_slot


def start_adapters(groups, meta, table, outs, sems):
    copies = []
    for k in reversed(range(1, groups)):
        for c in range(ACAP):
            chosen = meta[SEND, (k - 1) * ACAP + c]
            copy = pltpu.make_async_copy(
                table.at[chosen], outs[k - 1].at[c], sems.at[(k - 1) * ACAP + c]
            )
            copy.start()
            copies.append(copy)
    return copies


def swap(packed, groups):
    return [
        lax.ppermute(packed[k - 1], "group", [(g, g ^ k) for g in range(groups)])
        for k in range(1, groups)
    ]


def copy_conv(conv, slot, target, width, out, at):
    parts = width // 128
    begin = pl.multiple_of(target * width, 128)
    for k in range(conv.shape[0]):
        rows = conv[k, :, pl.ds(begin, width)]
        row = rows[:1, :]
        for c in range(1, conv.shape[1]):
            row = jnp.where(slot == c, rows[c:c + 1, :], row)
        for part in range(parts):
            place = at + k * parts + part
            out[place:place + 1, :] = row[:, part * 128:(part + 1) * 128]


def start_state(devices, meta, cache, outs, sems):
    copies = []
    for d in reversed(range(devices)):
        target = lax.bitwise_xor(meta[MISC, ME], d)
        copy = pltpu.make_async_copy(
            cache.at[meta[MISC, SLOT], target // 2, target % 2],
            outs[d].at[pl.ds(0, cache.shape[3])], sems.at[d],
        )
        copy.start()
        copies.append(copy)
    return copies


def start_across(j, meta, cache, across, own, sems):
    x = meta[MISC, ME] % 2
    copies = []
    for k, (out, place) in enumerate(((across, 1 - x), (own, x))):
        copy = pltpu.make_async_copy(
            cache.at[meta[OSLOT, j], :, place], out.at[:, pl.ds(0, cache.shape[3])], sems.at[k]
        )
        copy.start()
        copies.append(copy)
    return copies


def conv_across(lines, width, j, meta, conv, state_rows, across, own):
    x = meta[MISC, ME] % 2
    for out, place in ((across, 1 - x), (own, x)):
        for m in range(lines):
            copy_conv(conv, meta[OSLOT, j], 2 * m + place, width, out.at[m], state_rows)


def pack_kernel(
    groups, devices, per_group, width, home, index, holder, slot, blocks, down, up, cache, write,
    read, conv, meta, rows_out, *rest
):
    downs, rest = rest[:groups - 1], rest[groups - 1:]
    ups, rest = rest[:groups - 1], rest[groups - 1:]
    chunks, (across, own, down_sems, up_sems, chunk_sems, across_sems) = (
        rest[:devices], rest[devices:]
    )
    plan(groups, devices, per_group, home, index, holder, slot, blocks, meta)
    copies = start_adapters(groups, meta, down, downs, down_sems)
    copies += start_state(devices, meta, cache, chunks, chunk_sems)
    copies += start_across(0, meta, cache, across, own, across_sems)
    copies += start_adapters(groups, meta, up, ups, up_sems)
    depth = write.shape[1]
    rows_out[:, :depth] = write[...]
    rows_out[:, depth:] = read[...]
    state_rows = cache.shape[3]
    for d in range(devices):
        target = lax.bitwise_xor(meta[MISC, ME], d)
        copy_conv(conv, meta[MISC, SLOT], target, width, chunks[d], state_rows)
    conv_across(devices // 2, width, 0, meta, conv, state_rows, across, own)
    for copy in copies:
        copy.wait()


def pack_across_kernel(lines, width, j, meta, cache, conv, across, own, sems):
    copies = start_across(j[0], meta, cache, across, own, sems)
    conv_across(lines, width, j[0], meta, conv, cache.shape[3], across, own)
    for copy in copies:
        copy.wait()


def pick_kernel(step, lines, j, meta, own_r, over_r, own_l, over_l, *rest):
    out_r, out_l = rest[-2:]
    me = meta[MISC, ME]
    source = meta[OHOLDER, j[0]]
    same = source // 2 == me // 2
    mine = same & (source % 2 == me % 2)
    across = same & (source % 2 != me % 2)

    @pl.when(mine)
    def _():
        out_r[...] = own_r[0]
        out_l[...] = own_l[0]

    @pl.when(across)
    def _():
        out_r[...] = over_r[0]
        out_l[...] = over_l[0]

    @pl.when(jnp.logical_not(same))
    def _():
        if step > 1:
            out_r[...] = rest[0][...]
            out_l[...] = rest[1][...]
        else:
            out_r[...] = jnp.zeros_like(out_r)
            out_l[...] = jnp.zeros_like(out_l)


def right_block(meta, step, lines):
    return jnp.clip(lines + meta[MISC, ME] // 2 - step, 0, lines - 1)


def left_block(meta, step, lines):
    return jnp.clip(meta[MISC, ME] // 2 + step - lines, 0, lines - 1)


def pack_across(j, meta, cache, conv, devices, width):
    lines = devices // 2
    shape = chunk_shape(cache, conv, width)
    return pl.pallas_call(
        functools.partial(pack_across_kernel, lines, width),
        out_shape=tuple(jax.ShapeDtypeStruct((lines,) + shape, cache.dtype) for _ in range(2)),
        in_specs=smem(2) + pinned(1) + vmem(1),
        out_specs=tuple(vmem(2)),
        scratch_shapes=[pltpu.SemaphoreType.DMA((2,))],
        cost_estimate=cost(),
        compiler_params=params(),
        name="pack_across",
    )(j, meta, cache, conv)


def spread_steps(j, meta, packed, devices):
    lines = devices // 2
    send, own = packed
    shape = own.shape[1:]
    across = lax.ppermute(send, "dev", [(d, d ^ 1) for d in range(devices)])
    from_left = from_right = None
    after = yield across
    whole = pl.BlockSpec(shape, lambda g, j, meta: (0, 0))
    for step in range(1, lines):
        blocks = [
            pl.BlockSpec(
                (1,) + shape, lambda g, j, meta, at=at, step=step: (at(meta, step, lines), 0, 0)
            )
            for at in (right_block, left_block)
        ]
        operands = [own, across, own, across]
        in_specs = [blocks[0], blocks[0], blocks[1], blocks[1]]
        if step > 1:
            operands += [from_left, from_right]
            in_specs += [whole, whole]
        operands += after
        in_specs += anywhere(len(after))
        to_right, to_left = pl.pallas_call(
            functools.partial(pick_kernel, step, lines),
            grid_spec=pltpu.PrefetchScalarGridSpec(
                num_scalar_prefetch=2, grid=(1,), in_specs=in_specs, out_specs=(whole, whole)
            ),
            out_shape=tuple(jax.ShapeDtypeStruct(shape, own.dtype) for _ in range(2)),
            cost_estimate=cost(),
            compiler_params=params(),
            name=f"pick_{step}",
        )(j, meta, *operands)
        from_left = lax.ppermute(
            to_right, "dev",
            [(2 * i + x, 2 * i + 2 + x) for i in range(step) for x in range(2)],
        )
        from_right = lax.ppermute(
            to_left, "dev",
            [(devices - 1 - (2 * i + x), devices - 3 - (2 * i + x))
             for i in range(step) for x in range(2)],
        )
        after = yield to_right
    yield own, across, from_left, from_right


def final_specs(shape):
    line = pl.BlockSpec((1,) + shape, lambda g, j, meta: (meta[MISC, ME] // 2, 0, 0))
    whole = pl.BlockSpec(shape, lambda g, j, meta: (0, 0))
    return [line, line, whole, whole]


def which_candidate(meta, source):
    me = meta[MISC, ME]
    same = source // 2 == me // 2
    mine = same & (source % 2 == me % 2)
    return jnp.where(mine, 0, jnp.where(same, 1, jnp.where(source // 2 < me // 2, 2, 3)))


def final_kernel(j, meta, own, across, from_left, from_right, out):
    which = which_candidate(meta, meta[OHOLDER, j[0]])
    picks = (own.at[0], across.at[0], from_left, from_right)
    for k, pick in enumerate(picks):
        @pl.when(which == k)
        def _(pick=pick):
            out[...] = pick[...]


def spread_rest(meta, cache, conv, devices, width, limit):
    shape = chunk_shape(cache, conv, width)

    def one(j, held):
        jj = j.reshape(1)
        packed = pack_across(jj, meta, cache, conv, devices, width)
        steps = spread_steps(jj, meta, packed, devices)
        next(steps)
        for _ in range(devices // 2):
            got = steps.send([])
        block = pl.pallas_call(
            final_kernel,
            grid_spec=pltpu.PrefetchScalarGridSpec(
                num_scalar_prefetch=2,
                grid=(1,),
                in_specs=final_specs(shape),
                out_specs=pl.BlockSpec(shape, lambda g, j, meta: (0, 0)),
            ),
            out_shape=jax.ShapeDtypeStruct(shape, cache.dtype),
            compiler_params=params(),
            name="final_pick",
        )(jj, meta, *got)
        return lax.dynamic_update_slice_in_dim(held, block[None], j - 1, 0)

    held = jnp.zeros((limit - 1,) + shape, cache.dtype)
    return lax.fori_loop(jnp.int32(1), meta[MISC, MOST], one, held)


def fetch_table(groups, meta, r, tables, out, sem):
    dist = meta[DIST, r]
    for k in range(groups):
        row = meta[ARANK, r] if k else meta[AINDEX, r]

        @pl.when(dist == k)
        def _(k=k, row=row):
            pltpu.make_async_copy(tables[k].at[row], out, sem).start()


def shrink_kernel(groups, per_group, meta, hidden, *rest):
    tables, (out, picked, sems) = rest[:groups], rest[-3:]
    g = pl.program_id(0)
    each = out.shape[0]

    @pl.when(g == 0)
    def _():
        for r in range(per_group):
            fetch_table(groups, meta, r, tables, picked.at[r], sems.at[r])

    for i in range(each):
        r = g * each + i
        pltpu.make_async_copy(tables[0].at[0], picked.at[r], sems.at[r]).wait()
    for i in range(each):
        part = lax.dot_general(
            hidden[i * T_REQ:(i + 1) * T_REQ, :], picked[g * each + i], NT,
            preferred_element_type=jnp.float32,
        )
        out[i] = part.T.astype(out.dtype)


def sum_kernel(parts, *rest):
    out = rest[-1]
    total = parts[0].astype(jnp.float32)
    for k in range(1, parts.shape[0]):
        total = total + parts[k].astype(jnp.float32)
    total = total.astype(out.dtype)
    for k in range(out.shape[0]):
        out[k] = total


def prep_kernel(per_group, rates, skips, steps, taps_in, bias, *rest):
    rows_out, column_out, channel = rest[-3:]
    heads, tokens = steps.shape
    length = tokens // per_group
    rate = jnp.zeros((heads, length), jnp.float32)
    place = lax.broadcasted_iota(jnp.int32, rate.shape, 0)
    for h in range(heads):
        rate = jnp.where(place == h, rates[h] * (-LOG2E), rate)
    step = [steps[:, r * length:(r + 1) * length] for r in range(per_group)]
    x = jnp.concatenate([part * rate for part in step], axis=0)
    high = x.astype(jnp.bfloat16)
    rest = x - high.astype(jnp.float32)
    middle = rest.astype(jnp.bfloat16)
    low = (rest - middle.astype(jnp.float32)).astype(jnp.bfloat16)
    s = lax.broadcasted_iota(jnp.int32, (length, length), 0)
    t = lax.broadcasted_iota(jnp.int32, (length, length), 1)
    ones = (s <= t).astype(jnp.float32).astype(jnp.bfloat16)
    total = jnp.dot(low, ones, preferred_element_type=jnp.float32)
    total = total + jnp.dot(middle, ones, preferred_element_type=jnp.float32)
    total = total + jnp.dot(high, ones, preferred_element_type=jnp.float32)
    shifted = total - jnp.log2(jnp.concatenate(step, axis=0))
    columns = shifted.T
    for r in range(per_group):
        rows_out[:heads, r * length:(r + 1) * length] = total[r * heads:(r + 1) * heads]
        rows_out[heads:, r * length:(r + 1) * length] = shifted[r * heads:(r + 1) * heads]
        column_out[r] = columns[:, r * heads:(r + 1) * heads]
    taps, width = taps_in.shape
    head_of = lax.broadcasted_iota(jnp.int32, (1, width), 1) // (width // heads)
    skip = jnp.zeros((1, width), jnp.float32)
    for h in range(heads):
        skip = jnp.where(head_of == h, skips[h], skip)
    channel[:taps] = taps_in[...]
    channel[taps:taps + 1] = bias[...]
    channel[taps + 1:taps + 2] = skip


def mix_kernel(
    groups, taps, begin, steps, spread, size, meta, base, shrunk, channel, rows_decay, column,
    rows_in, *rest
):
    tables, chunks = rest[:groups], rest[groups:]
    out, final, done, extended, scores, carried, weighted, ups, curs, table_sems, chunk_sems = (
        rest[-11:]
    )
    g = pl.program_id(0)
    position = begin + g
    r = meta[POS_REQ, position]
    length, width = base.shape
    half = length // 2
    heads = width // size
    depth = curs.shape[2]
    few = taps - 1
    parts = width // 128
    f32, bf16 = jnp.float32, jnp.bfloat16

    done[...] = jnp.zeros_like(done)

    def fetch_chunk(source, i):
        pltpu.make_async_copy(source, curs.at[i], chunk_sems.at[i]).start()

    @pl.when(g == 0)
    def _():
        for i in range(steps):
            @pl.when(meta[POS_VALID, begin + i] > 0)
            def _(i=i):
                request = meta[POS_REQ, begin + i]
                fetch_table(groups, meta, request, tables, ups.at[i], table_sems.at[i])
                if not spread:
                    fetch_chunk(chunks[i], i)
                elif i > 0:
                    fetch_chunk(chunks[4].at[i - 1], i)
                else:
                    line = meta[MISC, ME] // 2
                    candidates = [
                        chunks[0].at[line], chunks[1].at[line], chunks[2], chunks[3], chunks[5]
                    ]
                    which = jnp.where(
                        meta[MISC, SPREAD] > 0, which_candidate(meta, meta[OHOLDER, 0]), 4
                    )
                    for k, candidate in enumerate(candidates):
                        @pl.when(which == k)
                        def _(candidate=candidate):
                            fetch_chunk(candidate, 0)

    @pl.when(meta[POS_VALID, position] > 0)
    def _():
        present = meta[PRESENT, r] > 0
        write, read = rows_in[:, :depth], rows_in[:, depth:]
        all_scores = lax.dot_general(write, read, NT, preferred_element_type=f32)
        s = lax.broadcasted_iota(jnp.int32, (half, half), 0)
        t = lax.broadcasted_iota(jnp.int32, (half, half), 1)
        scores[:half] = jnp.where(s <= t, all_scores[:half, :half], 0.0)
        scores[half:] = jnp.where(s <= t, all_scores[half:, half:], 0.0)
        late_scores = all_scores[:half, half:].astype(bf16)

        to_here, from_here = rows_decay[:heads, :], rows_decay[heads:, :]
        end = jnp.broadcast_to(to_here[:, length - 1:length], (heads, length))
        middle = jnp.broadcast_to(to_here[:, half - 1:half], (heads, half))
        grown = jnp.exp2(to_here)
        to_end = jnp.exp2(end - from_here)
        to_middle = jnp.exp2(middle - from_here[:, :half])
        past_middle = jnp.exp2(to_here[:, half:] - middle)
        kept = jnp.exp2(end[:, :depth])

        pltpu.make_async_copy(tables[0].at[0], ups.at[g], table_sems.at[g]).wait()
        extended[8:, :] = base[...].astype(f32) + lax.dot_general(
            shrunk[0], ups[g], TN, preferred_element_type=f32
        )
        pltpu.make_async_copy(curs.at[g], curs.at[g], chunk_sems.at[g]).wait()
        before = jnp.where(present, curs[g, width:, :].astype(f32), 0.0)
        for k in range(few):
            for part in range(parts):
                extended[8 - few + k:9 - few + k, part * 128:(part + 1) * 128] = (
                    before[k * parts + part:k * parts + part + 1, :]
                )
        from_state = lax.dot_general(curs[g, :width, :], read, NT, preferred_element_type=f32)
        carried[...] = jnp.where(present, from_state, 0.0)

        corner = jnp.zeros((half, half), bf16)
        for pair in range(heads // 2):
            lo, hi = pair * 2 * size, (pair + 1) * 2 * size
            v = channel[taps:taps + 1, lo:hi]
            for k in range(taps):
                first = 8 - few + k
                v = v + channel[k:k + 1, lo:hi] * extended[first:first + length, lo:hi]
            activated = v * (0.5 + 0.5 * jnp.tanh(0.5 * v))
            act = activated.astype(bf16).T
            wide = act.astype(f32)
            sums, early = [], []
            for i in range(2):
                h = 2 * pair + i
                a = act[i * size:(i + 1) * size, :]
                a32 = wide[i * size:(i + 1) * size, :]
                ds = jnp.broadcast_to(column[0, :, h:h + 1], (length, half))
                dt0, dt1 = to_here[h:h + 1, :half], to_here[h:h + 1, half:]
                m0 = jnp.exp2(jnp.minimum(dt0 - ds[:half], 126.0)) * scores[:half]
                m1 = jnp.exp2(jnp.minimum(dt1 - ds[half:], 126.0)) * scores[half:]
                mixing = jnp.concatenate(
                    [
                        jnp.concatenate([m0.astype(bf16), corner], axis=1),
                        jnp.concatenate([corner, m1.astype(bf16)], axis=1),
                    ],
                    axis=0,
                )
                total = jnp.dot(a, mixing, preferred_element_type=f32)
                sums.append(total + carried[h * size:(h + 1) * size, :] * grown[h:h + 1, :])
                weighted[h * size:(h + 1) * size, :] = (a32 * to_end[h:h + 1, :]).astype(bf16)
                early.append((a32[:, :half] * to_middle[h:h + 1, :]).astype(bf16))
            passed = jnp.dot(
                jnp.concatenate(early, axis=0), late_scores, preferred_element_type=f32
            )
            for i in range(2):
                h = 2 * pair + i
                late = passed[i * size:(i + 1) * size, :] * past_middle[h:h + 1, :]
                sums[i] = jnp.concatenate([sums[i][:, :half], sums[i][:, half:] + late], axis=1)
            skipped = channel[taps + 1:taps + 2, lo:hi] * activated
            out[:, lo:hi] = (jnp.concatenate(sums, axis=0).T + skipped).astype(out.dtype)
        fresh = jnp.dot(weighted[...], write, preferred_element_type=f32)
        for h in range(heads):
            rows = slice(h * size, (h + 1) * size)
            old = curs[g, rows, :].astype(f32) * kept[h:h + 1, :]
            old = jnp.where(present, old, 0.0)
            final[0, rows, :] = (fresh[rows, :] + old).astype(final.dtype)


def chunk_shape(cache, conv, width):
    conv_rows = conv.shape[0] * (width // 128)
    return (cache.shape[3] + -(-conv_rows // 16) * 16, cache.shape[4])


def body(
    hidden, base_in_projection, state_input_matrix, state_output_matrix, head_step_size,
    head_decay_rate, head_skip_scale, convolution_weight, convolution_bias, adapter_down_weight,
    adapter_up_weight, adapter_home_group, adapter_group_index, state_space_cache,
    convolution_cache, prefix_holder_device, prefix_cache_slot, prefix_block_count,
):
    groups, devices = lax.axis_size("group"), lax.axis_size("dev")
    tokens, width = base_in_projection.shape
    per_group = tokens // T_REQ
    assert per_group == devices and devices & (devices - 1) == 0 == groups & (groups - 1)
    heads = head_step_size.shape[0]
    size, depth = state_space_cache.shape[2:]
    rank = adapter_down_weight.shape[1]
    taps = convolution_weight.shape[0]
    bf16, f32 = jnp.bfloat16, jnp.float32
    limit = per_group // 2
    lines = devices // 2

    cache = state_space_cache.reshape(
        state_space_cache.shape[0], lines, 2, heads * size, depth
    )
    conv = convolution_cache.transpose(1, 0, 2)
    shape = chunk_shape(cache, conv, width)
    picks = [
        jax.ShapeDtypeStruct((ACAP,) + adapter_down_weight.shape[1:], bf16)
        for _ in range(groups - 1)
    ]
    packed = pl.pallas_call(
        functools.partial(pack_kernel, groups, devices, per_group, width),
        out_shape=(
            jax.ShapeDtypeStruct(META_SHAPE, jnp.int32),
            jax.ShapeDtypeStruct((state_input_matrix.shape[0], 2 * depth), bf16),
            *picks,
            *picks,
            *[jax.ShapeDtypeStruct(shape, bf16) for _ in range(devices)],
            *[jax.ShapeDtypeStruct((lines,) + shape, bf16) for _ in range(2)],
        ),
        in_specs=smem(5) + pinned(3) + vmem(3),
        out_specs=tuple(smem(1) + vmem(1 + 2 * len(picks) + devices + 2)),
        scratch_shapes=[
            pltpu.SemaphoreType.DMA((len(picks) * ACAP,)),
            pltpu.SemaphoreType.DMA((len(picks) * ACAP,)),
            pltpu.SemaphoreType.DMA((devices,)),
            pltpu.SemaphoreType.DMA((2,)),
        ],
        cost_estimate=cost(),
        compiler_params=params(),
        name="pack",
    )(
        adapter_home_group.reshape(-1), adapter_group_index, prefix_holder_device.reshape(-1),
        prefix_cache_slot, prefix_block_count, adapter_down_weight, adapter_up_weight, cache,
        state_input_matrix, state_output_matrix, conv,
    )
    meta, rows_mine, packed = packed[0], packed[1], packed[2:]
    down_got = swap(packed[:groups - 1], groups)
    up_got = swap(packed[groups - 1:2 * groups - 2], groups)
    chunks = packed[2 * groups - 2:-2]
    rows_all = lax.all_gather(rows_mine, "dev", axis=0, tiled=True)
    zero = jnp.zeros((1,), jnp.int32)
    got = [chunks[0]] + [
        lax.ppermute(chunks[d], "dev", [(s, s ^ d) for s in range(devices)])
        for d in range(1, devices)
    ]

    rows_decay, column_decay, channel = pl.pallas_call(
        functools.partial(prep_kernel, per_group),
        out_shape=(
            jax.ShapeDtypeStruct((2 * heads, tokens), f32),
            jax.ShapeDtypeStruct((per_group, T_REQ, heads), f32),
            jax.ShapeDtypeStruct((8, width), f32),
        ),
        in_specs=smem(2) + vmem(3) + anywhere(1),
        out_specs=tuple(pl.BlockSpec(memory_space=pltpu.VMEM) for _ in range(3)),
        cost_estimate=cost(),
        compiler_params=params(),
        name="prep",
    )(
        head_decay_rate, head_skip_scale, head_step_size, convolution_weight,
        convolution_bias.reshape(1, width), meta,
    )

    each = per_group // 2
    partial_down = pl.pallas_call(
        functools.partial(shrink_kernel, groups, per_group),
        grid_spec=pltpu.PrefetchScalarGridSpec(
            num_scalar_prefetch=1,
            grid=(per_group // each,),
            in_specs=[pl.BlockSpec((each * T_REQ, hidden.shape[1]), lambda g, meta: (g, 0))]
            + pinned(groups) + anywhere(3),
            out_specs=pl.BlockSpec((each, rank, T_REQ), lambda g, meta: (g, 0, 0)),
            scratch_shapes=[
                pltpu.VMEM((per_group,) + adapter_down_weight.shape[1:], bf16),
                pltpu.SemaphoreType.DMA((per_group,)),
            ],
        ),
        out_shape=jax.ShapeDtypeStruct((per_group, rank, T_REQ), bf16),
        cost_estimate=cost(),
        compiler_params=params(),
        name="shrink",
    )(meta, hidden, adapter_down_weight, *down_got, channel, got[lines], got[1])

    parts = lax.all_to_all(partial_down, "dev", split_axis=0, concat_axis=0, tiled=True)
    summed = pl.pallas_call(
        sum_kernel,
        out_shape=jax.ShapeDtypeStruct((devices, 1, rank, T_REQ), bf16),
        in_specs=vmem(1) + anywhere(2),
        out_specs=vmem(1)[0],
        cost_estimate=cost(),
        name="sum_parts",
    )(parts.reshape(devices, 1, rank, T_REQ), got[lines + 1], up_got[groups // 2 - 1])
    shrunk = lax.all_to_all(summed, "dev", split_axis=0, concat_axis=0, tiled=True)
    shrunk = shrunk.reshape(per_group, rank, T_REQ)

    spread = spread_steps(zero, meta, packed[-2:], devices)
    next(spread)
    sent = spread.send([summed, rows_all])
    for step in range(2, lines - 1):
        sent = spread.send([up_got[-1]] if step == lines - 2 else [])
    spread_others = spread_rest(meta, cache, conv, devices, width, limit)

    outs = None
    for begin, steps in ((0, lines), (lines, lines), (devices, limit)):
        if begin == 0:
            chunks, after = got[:lines], [sent, got[lines + 2]]
        elif begin == lines:
            chunks, after = got[lines:], [spread.send([outs[2]])]
        else:
            chunks, after = [*spread.send([]), spread_others, got[0]], []

        def request(g, meta, begin=begin):
            return meta[POS_REQ, begin + g]

        in_specs = [
            pl.BlockSpec((T_REQ, width), lambda g, meta: (request(g, meta), 0)),
            pl.BlockSpec((1, rank, T_REQ), lambda g, meta: (request(g, meta), 0, 0)),
            pl.BlockSpec((8, width), lambda g, meta: (0, 0)),
            pl.BlockSpec((2 * heads, T_REQ), lambda g, meta: (0, request(g, meta))),
            pl.BlockSpec((1, T_REQ, heads), lambda g, meta: (request(g, meta), 0, 0)),
            pl.BlockSpec((T_REQ, 2 * depth), lambda g, meta: (request(g, meta), 0)),
        ] + pinned(groups + len(chunks)) + anywhere(len(after))
        operands = [
            meta, base_in_projection, shrunk, channel, rows_decay, column_decay, rows_all,
            adapter_up_weight, *up_got, *chunks, *after,
        ]
        aliases = {}
        if outs is not None:
            aliases = {len(operands): 0, len(operands) + 1: 1}
            operands += list(outs[:2])
            in_specs += anywhere(2)
        outs = pl.pallas_call(
            functools.partial(mix_kernel, groups, taps, begin, steps, begin == devices, size),
            grid_spec=pltpu.PrefetchScalarGridSpec(
                num_scalar_prefetch=1,
                grid=(steps,),
                in_specs=in_specs,
                out_specs=(
                    pl.BlockSpec((T_REQ, width), lambda g, meta: (request(g, meta), 0)),
                    pl.BlockSpec(
                        (1, heads * size, depth), lambda g, meta: (request(g, meta), 0, 0)
                    ),
                    pl.BlockSpec((8, 128), lambda g, meta: (0, 0)),
                ),
                scratch_shapes=[
                    pltpu.VMEM((T_REQ + 8, width), f32),
                    pltpu.VMEM((T_REQ, T_REQ // 2), f32),
                    pltpu.VMEM((width, T_REQ), f32),
                    pltpu.VMEM((width, T_REQ), bf16),
                    pltpu.VMEM((steps,) + adapter_up_weight.shape[1:], bf16),
                    pltpu.VMEM((steps,) + shape, bf16),
                    pltpu.SemaphoreType.DMA((steps,)),
                    pltpu.SemaphoreType.DMA((steps,)),
                ],
            ),
            out_shape=(
                jax.ShapeDtypeStruct((tokens, width), bf16),
                jax.ShapeDtypeStruct((per_group, heads * size, depth), bf16),
                jax.ShapeDtypeStruct((8, 128), f32),
            ),
            input_output_aliases=aliases,
            cost_estimate=cost(),
            compiler_params=params(),
            name=f"mix_{begin}",
        )(*operands)
    return outs[0], outs[1].reshape(per_group, heads, size, depth)


def solution(mesh):
    placed = (
        P("group", "dev"),
        P("group", "dev"),
        P(("group", "dev"), None),
        P(("group", "dev"), None),
        P("dev", "group"),
        P("dev"),
        P("dev"),
        P(None, "dev"),
        P("dev"),
        P("group", None, "dev"),
        P("group", None, "dev"),
        P(),
        P(),
        P(("group", "dev"), None, None, None),
        P(("group", "dev"), None, None),
        P(),
        P(),
        P(),
    )
    return jax.shard_map(
        body,
        mesh=mesh,
        in_specs=placed,
        out_specs=(P("group", "dev"), P("group", "dev", None, None)),
        check_vma=False,
    )
```

```python
import functools
import math

import jax
import jax.numpy as jnp
from jax import lax
from jax.experimental import pallas as pl
from jax.experimental.pallas import tpu as pltpu
from jax.sharding import PartitionSpec as P

T_REQ = 256
CAP = 2
ACAP = 4
LOG2E = math.log2(math.e)
NT = (((1,), (1,)), ((), ()))
TN = (((0,), (0,)), ((), ()))
VMEM_LIMIT = 48 * 1024 * 1024

HOME, DIST, ARANK, AINDEX, PRESENT, POS_REQ, POS_VALID, OSLOT, OHOLDER, MISC, SEND = range(11)
MOST, ME, SLOT = range(3)
META_SHAPE = (16, 64)


def cost():
    return pl.CostEstimate(flops=0, bytes_accessed=1 << 16, transcendentals=0)


def params():
    return pltpu.CompilerParams(vmem_limit_bytes=VMEM_LIMIT)


def smem(count):
    return [pl.BlockSpec(memory_space=pltpu.SMEM) for _ in range(count)]


def vmem(count):
    return [pl.BlockSpec(memory_space=pltpu.VMEM) for _ in range(count)]


def pinned(count):
    return [pl.BlockSpec(memory_space=pltpu.HBM) for _ in range(count)]


def anywhere(count):
    return [pl.BlockSpec(memory_space=pl.ANY) for _ in range(count)]


def as_int(flag):
    return flag.astype(jnp.int32)


def ranks_of(labels):
    ranks = []
    for q, label in enumerate(labels):
        total = jnp.int32(0)
        for other in labels[:q]:
            total = total + as_int(other == label)
        ranks.append(total)
    return ranks


def plan(groups, devices, per_group, home, index, holder, slot, blocks, meta):
    my_group = lax.axis_index("group")
    me = lax.axis_index("dev")
    first = my_group * per_group
    limit = per_group // 2
    for j in range(limit):
        meta[POS_REQ, devices + j] = jnp.int32(-1)
        meta[POS_VALID, devices + j] = jnp.int32(0)
        meta[OSLOT, j] = jnp.int32(0)
        meta[OHOLDER, j] = jnp.int32(0)

    homes = [home[first + q] for q in range(per_group)]
    for q, rank in enumerate(ranks_of(homes)):
        meta[HOME, q] = homes[q]
        meta[DIST, q] = lax.bitwise_xor(homes[q], my_group)
        meta[ARANK, q] = rank
        meta[AINDEX, q] = index[first + q]
        meta[PRESENT, q] = as_int(blocks[first + q] > 0)
    for k in range(groups):
        theirs = lax.bitwise_xor(my_group, k) * per_group
        seen = jnp.int32(0)
        chosen = [jnp.int32(0) for _ in range(ACAP)]
        for q in range(per_group):
            hit = home[theirs + q] == my_group
            value = index[theirs + q]
            for c in range(ACAP):
                chosen[c] = jnp.where(hit & (seen == c), value, chosen[c])
            seen = seen + as_int(hit)
        for c in range(ACAP):
            meta[SEND, k * ACAP + c] = chosen[c]

    holders = [holder[first + q] for q in range(per_group)]
    ranks = ranks_of(holders)
    count = jnp.int32(0)
    my_slot = jnp.int32(0)
    for q in range(per_group):
        my_slot = jnp.where((holders[q] == me) & (ranks[q] == 0), slot[first + q], my_slot)

        @pl.when(ranks[q] > 0)
        def _():
            meta[POS_REQ, devices + count] = jnp.int32(q)
            meta[POS_VALID, devices + count] = jnp.int32(1)
            meta[OSLOT, count] = slot[first + q]
            meta[OHOLDER, count] = holders[q]

        count = count + as_int(ranks[q] > 0)
    spread = meta[POS_REQ, devices]
    requests = []
    for d in range(devices):
        source = lax.bitwise_xor(me, d)
        request = jnp.int32(-1)
        for q in range(per_group):
            request = jnp.where((holders[q] == source) & (ranks[q] == 0), q, request)
        meta[POS_VALID, d] = as_int(request >= 0)
        requests.append(request)
    requests += [meta[POS_REQ, devices + j] for j in range(limit)]
    for begin, end in ((0, devices // 2), (devices // 2, devices + limit)):
        last = jnp.int32(-1)
        filled = []
        for p in range(begin, end):
            last = jnp.where(requests[p] >= 0, requests[p], last)
            filled.append(last)
        following = jnp.maximum(spread, 0)
        for p in reversed(range(begin, end)):
            following = jnp.where(filled[p - begin] >= 0, filled[p - begin], following)
            meta[POS_REQ, p] = following
    most = jnp.int32(0)
    for g in range(groups):
        labels = [holder[g * per_group + q] for q in range(per_group)]
        total = jnp.int32(0)
        for rank in ranks_of(labels):
            total = total + as_int(rank > 0)
        most = jnp.maximum(most, total)
    meta[MISC, MOST] = most
    meta[MISC, ME] = me
    meta[MISC, SLOT] = my_slot


def start_adapters(groups, meta, table, outs, sems):
    copies = []
    for k in reversed(range(groups) if len(outs) == 1 else range(1, groups)):
        for c in range(ACAP):
            chosen = meta[SEND, k * ACAP + c]
            if len(outs) == 1:
                out = outs[0].at[lax.bitwise_xor(lax.axis_index("group"), k), c]
            else:
                out = outs[k - 1].at[c]
            copy = pltpu.make_async_copy(table.at[chosen], out, sems.at[k * ACAP + c])
            copy.start()
            copies.append(copy)
    return copies


def swap(packed, groups):
    return [
        lax.ppermute(packed[k - 1], "group", [(g, g ^ k) for g in range(groups)])
        for k in range(1, groups)
    ]


def copy_conv(conv, slot, target, width, out, at):
    parts = width // 128
    begin = pl.multiple_of(target * width, 128)
    for k in range(conv.shape[0]):
        rows = conv[k, :, pl.ds(begin, width)]
        row = rows[:1, :]
        for c in range(1, conv.shape[1]):
            row = jnp.where(slot == c, rows[c:c + 1, :], row)
        for part in range(parts):
            place = at + k * parts + part
            out[place:place + 1, :] = row[:, part * 128:(part + 1) * 128]


def start_state(devices, meta, cache, outs, sems):
    copies = []
    for d in reversed(range(devices)):
        target = lax.bitwise_xor(meta[MISC, ME], d)
        copy = pltpu.make_async_copy(
            cache.at[meta[MISC, SLOT], target // 2, target % 2],
            outs[d].at[pl.ds(0, cache.shape[3])], sems.at[d],
        )
        copy.start()
        copies.append(copy)
    return copies


def start_across(j, meta, cache, across, own, sems):
    x = meta[MISC, ME] % 2
    copies = []
    for k, (out, place) in enumerate(((across, 1 - x), (own, x))):
        copy = pltpu.make_async_copy(
            cache.at[meta[OSLOT, j], :, place], out.at[:, pl.ds(0, cache.shape[3])], sems.at[k]
        )
        copy.start()
        copies.append(copy)
    return copies


def conv_across(lines, width, j, meta, conv, state_rows, across, own):
    x = meta[MISC, ME] % 2
    for out, place in ((across, 1 - x), (own, x)):
        for m in range(lines):
            copy_conv(conv, meta[OSLOT, j], 2 * m + place, width, out.at[m], state_rows)


def pack_kernel(
    groups, devices, per_group, width, home, index, holder, slot, blocks, down, up, cache, write,
    read, conv, meta, rows_out, *rest
):
    downs, rest = rest[:1], rest[1:]
    ups, rest = rest[:groups - 1], rest[groups - 1:]
    chunks, (across, own, down_sems, up_sems, chunk_sems, across_sems) = (
        rest[:devices], rest[devices:]
    )
    plan(groups, devices, per_group, home, index, holder, slot, blocks, meta)
    copies = start_adapters(groups, meta, down, downs, down_sems)
    copies += start_state(devices, meta, cache, chunks, chunk_sems)
    copies += start_across(0, meta, cache, across, own, across_sems)
    copies += start_adapters(groups, meta, up, ups, up_sems)
    depth = write.shape[1]
    rows_out[:, :depth] = write[...]
    rows_out[:, depth:] = read[...]
    state_rows = cache.shape[3]
    for d in range(devices):
        target = lax.bitwise_xor(meta[MISC, ME], d)
        copy_conv(conv, meta[MISC, SLOT], target, width, chunks[d], state_rows)
    conv_across(devices // 2, width, 0, meta, conv, state_rows, across, own)
    for copy in copies:
        copy.wait()


def pack_across_kernel(lines, width, j, meta, cache, conv, across, own, sems):
    copies = start_across(j[0], meta, cache, across, own, sems)
    conv_across(lines, width, j[0], meta, conv, cache.shape[3], across, own)
    for copy in copies:
        copy.wait()


def pick_kernel(step, lines, j, meta, own_r, over_r, own_l, over_l, *rest):
    out_r, out_l = rest[-2:]
    me = meta[MISC, ME]
    source = meta[OHOLDER, j[0]]
    same = source // 2 == me // 2
    mine = same & (source % 2 == me % 2)
    across = same & (source % 2 != me % 2)

    @pl.when(mine)
    def _():
        out_r[...] = own_r[0]
        out_l[...] = own_l[0]

    @pl.when(across)
    def _():
        out_r[...] = over_r[0]
        out_l[...] = over_l[0]

    @pl.when(jnp.logical_not(same))
    def _():
        if step > 1:
            out_r[...] = rest[0][...]
            out_l[...] = rest[1][...]
        else:
            out_r[...] = jnp.zeros_like(out_r)
            out_l[...] = jnp.zeros_like(out_l)


def right_block(meta, step, lines):
    return jnp.clip(lines + meta[MISC, ME] // 2 - step, 0, lines - 1)


def left_block(meta, step, lines):
    return jnp.clip(meta[MISC, ME] // 2 + step - lines, 0, lines - 1)


def pack_across(j, meta, cache, conv, devices, width):
    lines = devices // 2
    shape = chunk_shape(cache, conv, width)
    return pl.pallas_call(
        functools.partial(pack_across_kernel, lines, width),
        out_shape=tuple(jax.ShapeDtypeStruct((lines,) + shape, cache.dtype) for _ in range(2)),
        in_specs=smem(2) + pinned(1) + vmem(1),
        out_specs=tuple(vmem(2)),
        scratch_shapes=[pltpu.SemaphoreType.DMA((2,))],
        cost_estimate=cost(),
        compiler_params=params(),
        name="pack_across",
    )(j, meta, cache, conv)


def spread_steps(j, meta, packed, devices):
    lines = devices // 2
    send, own = packed
    shape = own.shape[1:]
    across = lax.ppermute(send, "dev", [(d, d ^ 1) for d in range(devices)])
    from_left = from_right = None
    after = yield across
    whole = pl.BlockSpec(shape, lambda g, j, meta: (0, 0))
    for step in range(1, lines):
        blocks = [
            pl.BlockSpec(
                (1,) + shape, lambda g, j, meta, at=at, step=step: (at(meta, step, lines), 0, 0)
            )
            for at in (right_block, left_block)
        ]
        operands = [own, across, own, across]
        in_specs = [blocks[0], blocks[0], blocks[1], blocks[1]]
        if step > 1:
            operands += [from_left, from_right]
            in_specs += [whole, whole]
        operands += after
        in_specs += anywhere(len(after))
        to_right, to_left = pl.pallas_call(
            functools.partial(pick_kernel, step, lines),
            grid_spec=pltpu.PrefetchScalarGridSpec(
                num_scalar_prefetch=2, grid=(1,), in_specs=in_specs, out_specs=(whole, whole)
            ),
            out_shape=tuple(jax.ShapeDtypeStruct(shape, own.dtype) for _ in range(2)),
            cost_estimate=cost(),
            compiler_params=params(),
            name=f"pick_{step}",
        )(j, meta, *operands)
        from_left = lax.ppermute(
            to_right, "dev",
            [(2 * i + x, 2 * i + 2 + x) for i in range(step) for x in range(2)],
        )
        from_right = lax.ppermute(
            to_left, "dev",
            [(devices - 1 - (2 * i + x), devices - 3 - (2 * i + x))
             for i in range(step) for x in range(2)],
        )
        after = yield to_right
    yield own, across, from_left, from_right


def final_specs(shape):
    line = pl.BlockSpec((1,) + shape, lambda g, j, meta: (meta[MISC, ME] // 2, 0, 0))
    whole = pl.BlockSpec(shape, lambda g, j, meta: (0, 0))
    return [line, line, whole, whole]


def which_candidate(meta, source):
    me = meta[MISC, ME]
    same = source // 2 == me // 2
    mine = same & (source % 2 == me % 2)
    return jnp.where(mine, 0, jnp.where(same, 1, jnp.where(source // 2 < me // 2, 2, 3)))


def final_kernel(j, meta, own, across, from_left, from_right, out):
    which = which_candidate(meta, meta[OHOLDER, j[0]])
    picks = (own.at[0], across.at[0], from_left, from_right)
    for k, pick in enumerate(picks):
        @pl.when(which == k)
        def _(pick=pick):
            out[...] = pick[...]


def spread_rest(meta, cache, conv, devices, width, limit):
    shape = chunk_shape(cache, conv, width)

    def one(j, held):
        jj = j.reshape(1)
        packed = pack_across(jj, meta, cache, conv, devices, width)
        steps = spread_steps(jj, meta, packed, devices)
        next(steps)
        for _ in range(devices // 2):
            got = steps.send([])
        block = pl.pallas_call(
            final_kernel,
            grid_spec=pltpu.PrefetchScalarGridSpec(
                num_scalar_prefetch=2,
                grid=(1,),
                in_specs=final_specs(shape),
                out_specs=pl.BlockSpec(shape, lambda g, j, meta: (0, 0)),
            ),
            out_shape=jax.ShapeDtypeStruct(shape, cache.dtype),
            compiler_params=params(),
            name="final_pick",
        )(jj, meta, *got)
        return lax.dynamic_update_slice_in_dim(held, block[None], j - 1, 0)

    held = jnp.zeros((limit - 1,) + shape, cache.dtype)
    return lax.fori_loop(jnp.int32(1), meta[MISC, MOST], one, held)


def fetch_table(groups, meta, r, tables, out, sem):
    dist = meta[DIST, r]
    for k in range(groups):
        row = meta[ARANK, r] if k else meta[AINDEX, r]

        @pl.when(dist == k)
        def _(k=k, row=row):
            pltpu.make_async_copy(tables[k].at[row], out, sem).start()


def shrink_kernel(per_group, meta, hidden, table, *rest):
    out, picked, sems = rest[-3:]
    g = pl.program_id(0)
    each = out.shape[0]

    @pl.when(g == 0)
    def _():
        for r in range(per_group):
            pltpu.make_async_copy(
                table.at[meta[HOME, r], meta[ARANK, r]], picked.at[r], sems.at[r]
            ).start()

    for i in range(each):
        r = g * each + i
        pltpu.make_async_copy(table.at[0, 0], picked.at[r], sems.at[r]).wait()
    for i in range(each):
        part = lax.dot_general(
            hidden[i * T_REQ:(i + 1) * T_REQ, :], picked[g * each + i], NT,
            preferred_element_type=jnp.float32,
        )
        out[i] = part.T.astype(out.dtype)


def sum_kernel(parts, *rest):
    out = rest[-1]
    total = parts[0].astype(jnp.float32)
    for k in range(1, parts.shape[0]):
        total = total + parts[k].astype(jnp.float32)
    total = total.astype(out.dtype)
    for k in range(out.shape[0]):
        out[k] = total


def prep_kernel(per_group, rates, skips, steps, taps_in, bias, *rest):
    rows_out, column_out, channel = rest[-3:]
    heads, tokens = steps.shape
    length = tokens // per_group
    rate = jnp.zeros((heads, length), jnp.float32)
    place = lax.broadcasted_iota(jnp.int32, rate.shape, 0)
    for h in range(heads):
        rate = jnp.where(place == h, rates[h] * (-LOG2E), rate)
    step = [steps[:, r * length:(r + 1) * length] for r in range(per_group)]
    x = jnp.concatenate([part * rate for part in step], axis=0)
    high = x.astype(jnp.bfloat16)
    rest = x - high.astype(jnp.float32)
    middle = rest.astype(jnp.bfloat16)
    low = (rest - middle.astype(jnp.float32)).astype(jnp.bfloat16)
    s = lax.broadcasted_iota(jnp.int32, (length, length), 0)
    t = lax.broadcasted_iota(jnp.int32, (length, length), 1)
    ones = (s <= t).astype(jnp.float32).astype(jnp.bfloat16)
    total = jnp.dot(low, ones, preferred_element_type=jnp.float32)
    total = total + jnp.dot(middle, ones, preferred_element_type=jnp.float32)
    total = total + jnp.dot(high, ones, preferred_element_type=jnp.float32)
    shifted = total - jnp.log2(jnp.concatenate(step, axis=0))
    columns = shifted.T
    for r in range(per_group):
        rows_out[:heads, r * length:(r + 1) * length] = total[r * heads:(r + 1) * heads]
        rows_out[heads:, r * length:(r + 1) * length] = shifted[r * heads:(r + 1) * heads]
        column_out[r] = columns[:, r * heads:(r + 1) * heads]
    taps, width = taps_in.shape
    head_of = lax.broadcasted_iota(jnp.int32, (1, width), 1) // (width // heads)
    skip = jnp.zeros((1, width), jnp.float32)
    for h in range(heads):
        skip = jnp.where(head_of == h, skips[h], skip)
    channel[:taps] = taps_in[...]
    channel[taps:taps + 1] = bias[...]
    channel[taps + 1:taps + 2] = skip


def mix_kernel(
    groups, taps, begin, steps, direct, size, meta, base, shrunk, channel, rows_decay, column,
    rows_in, *rest
):
    tables, chunks = rest[:groups], rest[groups:]
    out, final, extended, scores, carried, weighted, ups, curs, table_sems, chunk_sems = (
        rest[-10:]
    )
    g = pl.program_id(0)
    position = begin + g
    r = meta[POS_REQ, position]
    length, width = base.shape
    half = length // 2
    heads = width // size
    depth = curs.shape[2]
    few = taps - 1
    parts = width // 128
    f32, bf16 = jnp.float32, jnp.bfloat16

    def fetch_chunk(source, i):
        pltpu.make_async_copy(source, curs.at[i], chunk_sems.at[i]).start()

    @pl.when(g == 0)
    def _():
        for i in range(steps):
            @pl.when(meta[POS_VALID, begin + i] > 0)
            def _(i=i):
                request = meta[POS_REQ, begin + i]
                fetch_table(groups, meta, request, tables, ups.at[i], table_sems.at[i])
                if i < direct:
                    fetch_chunk(chunks[i], i)
                elif i > direct:
                    fetch_chunk(chunks[direct + 4].at[i - direct - 1], i)
                else:
                    line = meta[MISC, ME] // 2
                    own, across, from_left, from_right = chunks[direct:direct + 4]
                    candidates = [own.at[line], across.at[line], from_left, from_right]
                    which = which_candidate(meta, meta[OHOLDER, 0])
                    for k, candidate in enumerate(candidates):
                        @pl.when(which == k)
                        def _(candidate=candidate):
                            fetch_chunk(candidate, direct)

    @pl.when(meta[POS_VALID, position] > 0)
    def _():
        present = meta[PRESENT, r] > 0
        write, read = rows_in[:, :depth], rows_in[:, depth:]
        all_scores = lax.dot_general(write, read, NT, preferred_element_type=f32)
        s = lax.broadcasted_iota(jnp.int32, (half, half), 0)
        t = lax.broadcasted_iota(jnp.int32, (half, half), 1)
        scores[:half] = jnp.where(s <= t, all_scores[:half, :half], 0.0)
        scores[half:] = jnp.where(s <= t, all_scores[half:, half:], 0.0)
        late_scores = all_scores[:half, half:].astype(bf16)

        to_here, from_here = rows_decay[:heads, :], rows_decay[heads:, :]
        end = jnp.broadcast_to(to_here[:, length - 1:length], (heads, length))
        middle = jnp.broadcast_to(to_here[:, half - 1:half], (heads, half))
        grown = jnp.exp2(to_here)
        to_end = jnp.exp2(end - from_here)
        to_middle = jnp.exp2(middle - from_here[:, :half])
        past_middle = jnp.exp2(to_here[:, half:] - middle)
        kept = jnp.exp2(end[:, :depth])

        pltpu.make_async_copy(tables[0].at[0], ups.at[g], table_sems.at[g]).wait()
        extended[8:, :] = base[...].astype(f32) + lax.dot_general(
            shrunk[0], ups[g], TN, preferred_element_type=f32
        )
        pltpu.make_async_copy(curs.at[g], curs.at[g], chunk_sems.at[g]).wait()
        before = jnp.where(present, curs[g, width:, :].astype(f32), 0.0)
        for k in range(few):
            for part in range(parts):
                extended[8 - few + k:9 - few + k, part * 128:(part + 1) * 128] = (
                    before[k * parts + part:k * parts + part + 1, :]
                )
        from_state = lax.dot_general(curs[g, :width, :], read, NT, preferred_element_type=f32)
        carried[...] = jnp.where(present, from_state, 0.0)

        corner = jnp.zeros((half, half), bf16)
        for pair in range(heads // 2):
            lo, hi = pair * 2 * size, (pair + 1) * 2 * size
            v = channel[taps:taps + 1, lo:hi]
            for k in range(taps):
                first = 8 - few + k
                v = v + channel[k:k + 1, lo:hi] * extended[first:first + length, lo:hi]
            activated = v * (0.5 + 0.5 * jnp.tanh(0.5 * v))
            act = activated.astype(bf16).T
            wide = act.astype(f32)
            sums, early = [], []
            for i in range(2):
                h = 2 * pair + i
                a = act[i * size:(i + 1) * size, :]
                a32 = wide[i * size:(i + 1) * size, :]
                ds = jnp.broadcast_to(column[0, :, h:h + 1], (length, half))
                dt0, dt1 = to_here[h:h + 1, :half], to_here[h:h + 1, half:]
                m0 = jnp.exp2(jnp.minimum(dt0 - ds[:half], 126.0)) * scores[:half]
                m1 = jnp.exp2(jnp.minimum(dt1 - ds[half:], 126.0)) * scores[half:]
                mixing = jnp.concatenate(
                    [
                        jnp.concatenate([m0.astype(bf16), corner], axis=1),
                        jnp.concatenate([corner, m1.astype(bf16)], axis=1),
                    ],
                    axis=0,
                )
                total = jnp.dot(a, mixing, preferred_element_type=f32)
                sums.append(total + carried[h * size:(h + 1) * size, :] * grown[h:h + 1, :])
                weighted[h * size:(h + 1) * size, :] = (a32 * to_end[h:h + 1, :]).astype(bf16)
                early.append((a32[:, :half] * to_middle[h:h + 1, :]).astype(bf16))
            passed = jnp.dot(
                jnp.concatenate(early, axis=0), late_scores, preferred_element_type=f32
            )
            for i in range(2):
                h = 2 * pair + i
                late = passed[i * size:(i + 1) * size, :] * past_middle[h:h + 1, :]
                sums[i] = jnp.concatenate([sums[i][:, :half], sums[i][:, half:] + late], axis=1)
            skipped = channel[taps + 1:taps + 2, lo:hi] * activated
            out[:, lo:hi] = (jnp.concatenate(sums, axis=0).T + skipped).astype(out.dtype)
        fresh = jnp.dot(weighted[...], write, preferred_element_type=f32)
        for h in range(heads):
            rows = slice(h * size, (h + 1) * size)
            old = curs[g, rows, :].astype(f32) * kept[h:h + 1, :]
            old = jnp.where(present, old, 0.0)
            final[0, rows, :] = (fresh[rows, :] + old).astype(final.dtype)


def chunk_shape(cache, conv, width):
    conv_rows = conv.shape[0] * (width // 128)
    return (cache.shape[3] + -(-conv_rows // 16) * 16, cache.shape[4])


def body(
    hidden, base_in_projection, state_input_matrix, state_output_matrix, head_step_size,
    head_decay_rate, head_skip_scale, convolution_weight, convolution_bias, adapter_down_weight,
    adapter_up_weight, adapter_home_group, adapter_group_index, state_space_cache,
    convolution_cache, prefix_holder_device, prefix_cache_slot, prefix_block_count,
):
    groups, devices = lax.axis_size("group"), lax.axis_size("dev")
    tokens, width = base_in_projection.shape
    per_group = tokens // T_REQ
    assert per_group == devices and devices & (devices - 1) == 0 == groups & (groups - 1)
    heads = head_step_size.shape[0]
    size, depth = state_space_cache.shape[2:]
    rank = adapter_down_weight.shape[1]
    taps = convolution_weight.shape[0]
    bf16, f32 = jnp.bfloat16, jnp.float32
    limit = per_group // 2
    lines = devices // 2

    cache = state_space_cache.reshape(
        state_space_cache.shape[0], lines, 2, heads * size, depth
    )
    conv = convolution_cache.transpose(1, 0, 2)
    shape = chunk_shape(cache, conv, width)
    picks = [
        jax.ShapeDtypeStruct((ACAP,) + adapter_down_weight.shape[1:], bf16)
        for _ in range(groups - 1)
    ]
    packed = pl.pallas_call(
        functools.partial(pack_kernel, groups, devices, per_group, width),
        out_shape=(
            jax.ShapeDtypeStruct(META_SHAPE, jnp.int32),
            jax.ShapeDtypeStruct((state_input_matrix.shape[0], 2 * depth), bf16),
            jax.ShapeDtypeStruct((groups, ACAP) + adapter_down_weight.shape[1:], bf16),
            *picks,
            *[jax.ShapeDtypeStruct(shape, bf16) for _ in range(devices)],
            *[jax.ShapeDtypeStruct((lines,) + shape, bf16) for _ in range(2)],
        ),
        in_specs=smem(5) + pinned(3) + vmem(3),
        out_specs=tuple(smem(1) + vmem(2 + len(picks) + devices + 2)),
        scratch_shapes=[
            pltpu.SemaphoreType.DMA((groups * ACAP,)),
            pltpu.SemaphoreType.DMA((groups * ACAP,)),
            pltpu.SemaphoreType.DMA((devices,)),
            pltpu.SemaphoreType.DMA((2,)),
        ],
        cost_estimate=cost(),
        compiler_params=params(),
        name="pack",
    )(
        adapter_home_group.reshape(-1), adapter_group_index, prefix_holder_device.reshape(-1),
        prefix_cache_slot, prefix_block_count, adapter_down_weight, adapter_up_weight, cache,
        state_input_matrix, state_output_matrix, conv,
    )
    meta, rows_mine, packed = packed[0], packed[1], packed[2:]
    down_got = lax.all_to_all(packed[0], "group", split_axis=0, concat_axis=0, tiled=True)
    chunks = packed[groups:-2]
    rows_all = lax.all_gather(rows_mine, "dev", axis=0, tiled=True)
    zero = jnp.zeros((1,), jnp.int32)
    got = [chunks[0]] + [
        lax.ppermute(chunks[d], "dev", [(s, s ^ d) for s in range(devices)])
        for d in range(1, devices)
    ]

    up_send, _ = lax.optimization_barrier((packed[1:groups], got[lines]))
    up_got = swap(up_send, groups)

    rows_decay, column_decay, channel = pl.pallas_call(
        functools.partial(prep_kernel, per_group),
        out_shape=(
            jax.ShapeDtypeStruct((2 * heads, tokens), f32),
            jax.ShapeDtypeStruct((per_group, T_REQ, heads), f32),
            jax.ShapeDtypeStruct((8, width), f32),
        ),
        in_specs=smem(2) + vmem(3) + anywhere(1),
        out_specs=tuple(pl.BlockSpec(memory_space=pltpu.VMEM) for _ in range(3)),
        cost_estimate=cost(),
        compiler_params=params(),
        name="prep",
    )(
        head_decay_rate, head_skip_scale, head_step_size, convolution_weight,
        convolution_bias.reshape(1, width), meta,
    )

    each = per_group // 2
    partial_down = pl.pallas_call(
        functools.partial(shrink_kernel, per_group),
        grid_spec=pltpu.PrefetchScalarGridSpec(
            num_scalar_prefetch=1,
            grid=(per_group // each,),
            in_specs=[pl.BlockSpec((each * T_REQ, hidden.shape[1]), lambda g, meta: (g, 0))]
            + anywhere(3),
            out_specs=pl.BlockSpec((each, rank, T_REQ), lambda g, meta: (g, 0, 0)),
            scratch_shapes=[
                pltpu.VMEM((per_group,) + adapter_down_weight.shape[1:], bf16),
                pltpu.SemaphoreType.DMA((per_group,)),
            ],
        ),
        out_shape=jax.ShapeDtypeStruct((per_group, rank, T_REQ), bf16),
        cost_estimate=cost(),
        compiler_params=params(),
        name="shrink",
    )(meta, hidden, down_got, channel, got[lines])

    parts = lax.all_to_all(partial_down, "dev", split_axis=0, concat_axis=0, tiled=True)
    summed = pl.pallas_call(
        sum_kernel,
        out_shape=jax.ShapeDtypeStruct((devices, 1, rank, T_REQ), bf16),
        in_specs=vmem(1) + anywhere(1),
        out_specs=vmem(1)[0],
        cost_estimate=cost(),
        name="sum_parts",
    )(parts.reshape(devices, 1, rank, T_REQ), got[lines + 1])
    shrunk = lax.all_to_all(summed, "dev", split_axis=0, concat_axis=0, tiled=True)
    shrunk = shrunk.reshape(per_group, rank, T_REQ)

    befores = [[partial_down], [summed, up_got[groups // 2 - 1]], [rows_all, up_got[-1]]]
    spread = spread_steps(zero, meta, packed[-2:], devices)
    next(spread)
    for step in range(1, lines):
        sent = spread.send(befores.pop(0) if befores else [])
    spread = spread.send([])
    spread_others = spread_rest(meta, cache, conv, devices, width, limit)

    outs = None
    for begin, steps in ((0, lines), (lines, devices - lines + limit)):
        if begin == 0:
            chunks, after = got[:lines], [sent, got[lines + 2]]
        else:
            chunks, after = [*got[lines:], *spread, spread_others], []

        def request(g, meta, begin=begin):
            return meta[POS_REQ, begin + g]

        in_specs = [
            pl.BlockSpec((T_REQ, width), lambda g, meta: (request(g, meta), 0)),
            pl.BlockSpec((1, rank, T_REQ), lambda g, meta: (request(g, meta), 0, 0)),
            pl.BlockSpec((8, width), lambda g, meta: (0, 0)),
            pl.BlockSpec((2 * heads, T_REQ), lambda g, meta: (0, request(g, meta))),
            pl.BlockSpec((1, T_REQ, heads), lambda g, meta: (request(g, meta), 0, 0)),
            pl.BlockSpec((T_REQ, 2 * depth), lambda g, meta: (request(g, meta), 0)),
        ] + anywhere(groups + len(chunks) + len(after))
        operands = [
            meta, base_in_projection, shrunk, channel, rows_decay, column_decay, rows_all,
            adapter_up_weight, *up_got, *chunks, *after,
        ]
        aliases = {}
        if outs is not None:
            aliases = {len(operands): 0, len(operands) + 1: 1}
            operands += list(outs)
            in_specs += anywhere(2)
        outs = pl.pallas_call(
            functools.partial(mix_kernel, groups, taps, begin, steps, lines, size),
            grid_spec=pltpu.PrefetchScalarGridSpec(
                num_scalar_prefetch=1,
                grid=(steps,),
                in_specs=in_specs,
                out_specs=(
                    pl.BlockSpec((T_REQ, width), lambda g, meta: (request(g, meta), 0)),
                    pl.BlockSpec(
                        (1, heads * size, depth), lambda g, meta: (request(g, meta), 0, 0)
                    ),
                ),
                scratch_shapes=[
                    pltpu.VMEM((T_REQ + 8, width), f32),
                    pltpu.VMEM((T_REQ, T_REQ // 2), f32),
                    pltpu.VMEM((width, T_REQ), f32),
                    pltpu.VMEM((width, T_REQ), bf16),
                    pltpu.VMEM((steps,) + adapter_up_weight.shape[1:], bf16),
                    pltpu.VMEM((steps,) + shape, bf16),
                    pltpu.SemaphoreType.DMA((steps,)),
                    pltpu.SemaphoreType.DMA((steps,)),
                ],
            ),
            out_shape=(
                jax.ShapeDtypeStruct((tokens, width), bf16),
                jax.ShapeDtypeStruct((per_group, heads * size, depth), bf16),
            ),
            input_output_aliases=aliases,
            cost_estimate=cost(),
            compiler_params=params(),
            name=f"mix_{begin}",
        )(*operands)
    return outs[0], outs[1].reshape(per_group, heads, size, depth)


def solution(mesh):
    placed = (
        P("group", "dev"),
        P("group", "dev"),
        P(("group", "dev"), None),
        P(("group", "dev"), None),
        P("dev", "group"),
        P("dev"),
        P("dev"),
        P(None, "dev"),
        P("dev"),
        P("group", None, "dev"),
        P("group", None, "dev"),
        P(),
        P(),
        P(("group", "dev"), None, None, None),
        P(("group", "dev"), None, None),
        P(),
        P(),
        P(),
    )
    return jax.shard_map(
        body,
        mesh=mesh,
        in_specs=placed,
        out_specs=(P("group", "dev"), P("group", "dev", None, None)),
        check_vma=False,
    )
```

```python
import functools
import math

import jax
import jax.numpy as jnp
from jax import lax
from jax.experimental import pallas as pl
from jax.experimental.pallas import tpu as pltpu
from jax.sharding import PartitionSpec as P

T_REQ = 256
CAP = 2
ACAP = 4
LOG2E = math.log2(math.e)
NT = (((1,), (1,)), ((), ()))
TN = (((0,), (0,)), ((), ()))
VMEM_LIMIT = 63 * 1024 * 1024

HOME, DIST, ARANK, AINDEX, PRESENT, POS_REQ, POS_VALID, OSLOT, OHOLDER, MISC, SEND = range(11)
MOST, ME, SLOT = range(3)
META_SHAPE = (16, 64)


def cost():
    return pl.CostEstimate(flops=0, bytes_accessed=1 << 16, transcendentals=0)


def params():
    return pltpu.CompilerParams(vmem_limit_bytes=VMEM_LIMIT)


def smem(count):
    return [pl.BlockSpec(memory_space=pltpu.SMEM) for _ in range(count)]


def vmem(count):
    return [pl.BlockSpec(memory_space=pltpu.VMEM) for _ in range(count)]


def pinned(count):
    return [pl.BlockSpec(memory_space=pltpu.HBM) for _ in range(count)]


def anywhere(count):
    return [pl.BlockSpec(memory_space=pl.ANY) for _ in range(count)]


def as_int(flag):
    return flag.astype(jnp.int32)


def ranks_of(labels):
    ranks = []
    for q, label in enumerate(labels):
        total = jnp.int32(0)
        for other in labels[:q]:
            total = total + as_int(other == label)
        ranks.append(total)
    return ranks


def plan(groups, devices, per_group, home, index, holder, slot, blocks, meta):
    my_group = lax.axis_index("group")
    me = lax.axis_index("dev")
    first = my_group * per_group
    limit = per_group // 2
    for j in range(limit):
        meta[POS_REQ, devices + j] = jnp.int32(-1)
        meta[POS_VALID, devices + j] = jnp.int32(0)
        meta[OSLOT, j] = jnp.int32(0)
        meta[OHOLDER, j] = jnp.int32(0)

    homes = [home[first + q] for q in range(per_group)]
    for q, rank in enumerate(ranks_of(homes)):
        meta[HOME, q] = homes[q]
        meta[DIST, q] = lax.bitwise_xor(homes[q], my_group)
        meta[ARANK, q] = rank
        meta[AINDEX, q] = index[first + q]
        meta[PRESENT, q] = as_int(blocks[first + q] > 0)
    for k in range(groups):
        theirs = lax.bitwise_xor(my_group, k) * per_group
        seen = jnp.int32(0)
        chosen = [jnp.int32(0) for _ in range(ACAP)]
        for q in range(per_group):
            hit = home[theirs + q] == my_group
            value = index[theirs + q]
            for c in range(ACAP):
                chosen[c] = jnp.where(hit & (seen == c), value, chosen[c])
            seen = seen + as_int(hit)
        for c in range(ACAP):
            meta[SEND, k * ACAP + c] = chosen[c]

    holders = [holder[first + q] for q in range(per_group)]
    ranks = ranks_of(holders)
    count = jnp.int32(0)
    my_slot = jnp.int32(0)
    for q in range(per_group):
        my_slot = jnp.where((holders[q] == me) & (ranks[q] == 0), slot[first + q], my_slot)

        @pl.when(ranks[q] > 0)
        def _():
            meta[POS_REQ, devices + count] = jnp.int32(q)
            meta[POS_VALID, devices + count] = jnp.int32(1)
            meta[OSLOT, count] = slot[first + q]
            meta[OHOLDER, count] = holders[q]

        count = count + as_int(ranks[q] > 0)
    spread = meta[POS_REQ, devices]
    requests = []
    for d in range(devices):
        source = lax.bitwise_xor(me, d)
        request = jnp.int32(-1)
        for q in range(per_group):
            request = jnp.where((holders[q] == source) & (ranks[q] == 0), q, request)
        meta[POS_VALID, d] = as_int(request >= 0)
        requests.append(request)
    requests += [meta[POS_REQ, devices + j] for j in range(limit)]
    for begin, end in ((0, devices // 2), (devices // 2, devices + limit)):
        last = jnp.int32(-1)
        filled = []
        for p in range(begin, end):
            last = jnp.where(requests[p] >= 0, requests[p], last)
            filled.append(last)
        following = jnp.maximum(spread, 0)
        for p in reversed(range(begin, end)):
            following = jnp.where(filled[p - begin] >= 0, filled[p - begin], following)
            meta[POS_REQ, p] = following
    most = jnp.int32(0)
    for g in range(groups):
        labels = [holder[g * per_group + q] for q in range(per_group)]
        total = jnp.int32(0)
        for rank in ranks_of(labels):
            total = total + as_int(rank > 0)
        most = jnp.maximum(most, total)
    meta[MISC, MOST] = most
    meta[MISC, ME] = me
    meta[MISC, SLOT] = my_slot


def start_adapters(groups, meta, table, outs, sems):
    copies = []
    for k in reversed(range(groups) if len(outs) == 1 else range(1, groups)):
        for c in range(ACAP):
            chosen = meta[SEND, k * ACAP + c]
            if len(outs) == 1:
                out = outs[0].at[lax.bitwise_xor(lax.axis_index("group"), k), c]
            else:
                out = outs[k - 1].at[c]
            copy = pltpu.make_async_copy(table.at[chosen], out, sems.at[k * ACAP + c])
            copy.start()
            copies.append(copy)
    return copies


def swap(packed, groups):
    return [
        lax.ppermute(packed[k - 1], "group", [(g, g ^ k) for g in range(groups)])
        for k in range(1, groups)
    ]


def copy_conv(conv, slot, target, width, out, at):
    parts = width // 128
    begin = pl.multiple_of(target * width, 128)
    for k in range(conv.shape[0]):
        rows = conv[k, :, pl.ds(begin, width)]
        row = rows[:1, :]
        for c in range(1, conv.shape[1]):
            row = jnp.where(slot == c, rows[c:c + 1, :], row)
        for part in range(parts):
            place = at + k * parts + part
            out[place:place + 1, :] = row[:, part * 128:(part + 1) * 128]


def start_state(devices, meta, cache, outs, sems):
    copies = []
    for d in reversed(range(devices)):
        target = lax.bitwise_xor(meta[MISC, ME], d)
        copy = pltpu.make_async_copy(
            cache.at[meta[MISC, SLOT], target // 2, target % 2],
            outs[d].at[pl.ds(0, cache.shape[3])], sems.at[d],
        )
        copy.start()
        copies.append(copy)
    return copies


def start_across(j, meta, cache, across, own, sems):
    x = meta[MISC, ME] % 2
    copies = []
    for k, (out, place) in enumerate(((across, 1 - x), (own, x))):
        copy = pltpu.make_async_copy(
            cache.at[meta[OSLOT, j], :, place], out.at[:, pl.ds(0, cache.shape[3])], sems.at[k]
        )
        copy.start()
        copies.append(copy)
    return copies


def conv_across(lines, width, j, meta, conv, state_rows, across, own):
    x = meta[MISC, ME] % 2
    for out, place in ((across, 1 - x), (own, x)):
        for m in range(lines):
            copy_conv(conv, meta[OSLOT, j], 2 * m + place, width, out.at[m], state_rows)


def pack_kernel(
    groups, devices, per_group, width, home, index, holder, slot, blocks, down, up, cache, write,
    read, conv, meta, rows_out, *rest
):
    downs, rest = rest[:1], rest[1:]
    ups, rest = rest[:groups - 1], rest[groups - 1:]
    chunks, (across, own, down_sems, up_sems, chunk_sems, across_sems) = (
        rest[:devices], rest[devices:]
    )
    plan(groups, devices, per_group, home, index, holder, slot, blocks, meta)
    copies = start_adapters(groups, meta, down, downs, down_sems)
    copies += start_state(devices, meta, cache, chunks, chunk_sems)
    copies += start_across(0, meta, cache, across, own, across_sems)
    copies += start_adapters(groups, meta, up, ups, up_sems)
    depth = write.shape[1]
    rows_out[:, :depth] = write[...]
    rows_out[:, depth:] = read[...]
    state_rows = cache.shape[3]
    for d in range(devices):
        target = lax.bitwise_xor(meta[MISC, ME], d)
        copy_conv(conv, meta[MISC, SLOT], target, width, chunks[d], state_rows)
    conv_across(devices // 2, width, 0, meta, conv, state_rows, across, own)
    for copy in copies:
        copy.wait()


def pack_across_kernel(lines, width, j, meta, cache, conv, across, own, sems):
    copies = start_across(j[0], meta, cache, across, own, sems)
    conv_across(lines, width, j[0], meta, conv, cache.shape[3], across, own)
    for copy in copies:
        copy.wait()


def pick_kernel(step, lines, j, meta, own_r, over_r, own_l, over_l, *rest):
    out_r, out_l = rest[-2:]
    me = meta[MISC, ME]
    source = meta[OHOLDER, j[0]]
    same = source // 2 == me // 2
    mine = same & (source % 2 == me % 2)
    across = same & (source % 2 != me % 2)

    @pl.when(mine)
    def _():
        out_r[...] = own_r[0]
        out_l[...] = own_l[0]

    @pl.when(across)
    def _():
        out_r[...] = over_r[0]
        out_l[...] = over_l[0]

    @pl.when(jnp.logical_not(same))
    def _():
        if step > 1:
            out_r[...] = rest[0][...]
            out_l[...] = rest[1][...]
        else:
            out_r[...] = jnp.zeros_like(out_r)
            out_l[...] = jnp.zeros_like(out_l)


def right_block(meta, step, lines):
    return jnp.clip(lines + meta[MISC, ME] // 2 - step, 0, lines - 1)


def left_block(meta, step, lines):
    return jnp.clip(meta[MISC, ME] // 2 + step - lines, 0, lines - 1)


def pack_across(j, meta, cache, conv, devices, width):
    lines = devices // 2
    shape = chunk_shape(cache, conv, width)
    return pl.pallas_call(
        functools.partial(pack_across_kernel, lines, width),
        out_shape=tuple(jax.ShapeDtypeStruct((lines,) + shape, cache.dtype) for _ in range(2)),
        in_specs=smem(2) + pinned(1) + vmem(1),
        out_specs=tuple(vmem(2)),
        scratch_shapes=[pltpu.SemaphoreType.DMA((2,))],
        cost_estimate=cost(),
        compiler_params=params(),
        name="pack_across",
    )(j, meta, cache, conv)


def spread_steps(j, meta, packed, devices):
    lines = devices // 2
    send, own = packed
    shape = own.shape[1:]
    across = lax.ppermute(send, "dev", [(d, d ^ 1) for d in range(devices)])
    from_left = from_right = None
    after = yield across
    whole = pl.BlockSpec(shape, lambda g, j, meta: (0, 0))
    for step in range(1, lines):
        blocks = [
            pl.BlockSpec(
                (1,) + shape, lambda g, j, meta, at=at, step=step: (at(meta, step, lines), 0, 0)
            )
            for at in (right_block, left_block)
        ]
        operands = [own, across, own, across]
        in_specs = [blocks[0], blocks[0], blocks[1], blocks[1]]
        if step > 1:
            operands += [from_left, from_right]
            in_specs += [whole, whole]
        operands += after
        in_specs += anywhere(len(after))
        to_right, to_left = pl.pallas_call(
            functools.partial(pick_kernel, step, lines),
            grid_spec=pltpu.PrefetchScalarGridSpec(
                num_scalar_prefetch=2, grid=(1,), in_specs=in_specs, out_specs=(whole, whole)
            ),
            out_shape=tuple(jax.ShapeDtypeStruct(shape, own.dtype) for _ in range(2)),
            cost_estimate=cost(),
            compiler_params=params(),
            name=f"pick_{step}",
        )(j, meta, *operands)
        from_left = lax.ppermute(
            to_right, "dev",
            [(2 * i + x, 2 * i + 2 + x) for i in range(step) for x in range(2)],
        )
        from_right = lax.ppermute(
            to_left, "dev",
            [(devices - 1 - (2 * i + x), devices - 3 - (2 * i + x))
             for i in range(step) for x in range(2)],
        )
        after = yield to_right
    yield own, across, from_left, from_right


def final_specs(shape):
    line = pl.BlockSpec((1,) + shape, lambda g, j, meta: (meta[MISC, ME] // 2, 0, 0))
    whole = pl.BlockSpec(shape, lambda g, j, meta: (0, 0))
    return [line, line, whole, whole]


def which_candidate(meta, source):
    me = meta[MISC, ME]
    same = source // 2 == me // 2
    mine = same & (source % 2 == me % 2)
    return jnp.where(mine, 0, jnp.where(same, 1, jnp.where(source // 2 < me // 2, 2, 3)))


def final_kernel(j, meta, own, across, from_left, from_right, out):
    which = which_candidate(meta, meta[OHOLDER, j[0]])
    picks = (own.at[0], across.at[0], from_left, from_right)
    for k, pick in enumerate(picks):
        @pl.when(which == k)
        def _(pick=pick):
            out[...] = pick[...]


def spread_rest(meta, cache, conv, devices, width, limit):
    shape = chunk_shape(cache, conv, width)

    def one(j, held):
        jj = j.reshape(1)
        packed = pack_across(jj, meta, cache, conv, devices, width)
        steps = spread_steps(jj, meta, packed, devices)
        next(steps)
        for _ in range(devices // 2):
            got = steps.send([])
        block = pl.pallas_call(
            final_kernel,
            grid_spec=pltpu.PrefetchScalarGridSpec(
                num_scalar_prefetch=2,
                grid=(1,),
                in_specs=final_specs(shape),
                out_specs=pl.BlockSpec(shape, lambda g, j, meta: (0, 0)),
            ),
            out_shape=jax.ShapeDtypeStruct(shape, cache.dtype),
            compiler_params=params(),
            name="final_pick",
        )(jj, meta, *got)
        return lax.dynamic_update_slice_in_dim(held, block[None], j - 1, 0)

    held = jnp.zeros((limit - 1,) + shape, cache.dtype)
    return lax.fori_loop(jnp.int32(1), meta[MISC, MOST], one, held)


def fetch_table(groups, meta, r, tables, out, sem):
    dist = meta[DIST, r]
    for k in range(groups):
        row = meta[ARANK, r] if k else meta[AINDEX, r]

        @pl.when(dist == k)
        def _(k=k, row=row):
            pltpu.make_async_copy(tables[k].at[row], out, sem).start()


def shrink_kernel(per_group, meta, hidden, table, *rest):
    out, picked, sems = rest[-3:]
    g = pl.program_id(0)
    each = out.shape[0]

    @pl.when(g == 0)
    def _():
        for r in range(per_group):
            pltpu.make_async_copy(
                table.at[meta[HOME, r], meta[ARANK, r]], picked.at[r], sems.at[r]
            ).start()

    for i in range(each):
        r = g * each + i
        pltpu.make_async_copy(table.at[0, 0], picked.at[r], sems.at[r]).wait()
    for i in range(each):
        part = lax.dot_general(
            hidden[i * T_REQ:(i + 1) * T_REQ, :], picked[g * each + i], NT,
            preferred_element_type=jnp.float32,
        )
        out[i] = part.T.astype(out.dtype)


def sum_kernel(parts, *rest):
    out = rest[-1]
    total = parts[0].astype(jnp.float32)
    for k in range(1, parts.shape[0]):
        total = total + parts[k].astype(jnp.float32)
    total = total.astype(out.dtype)
    for k in range(out.shape[0]):
        out[k] = total


def prep_kernel(per_group, rates, skips, steps, taps_in, bias, *rest):
    rows_out, column_out, channel = rest[-3:]
    heads, tokens = steps.shape
    length = tokens // per_group
    rate = jnp.zeros((heads, length), jnp.float32)
    place = lax.broadcasted_iota(jnp.int32, rate.shape, 0)
    for h in range(heads):
        rate = jnp.where(place == h, rates[h] * (-LOG2E), rate)
    step = [steps[:, r * length:(r + 1) * length] for r in range(per_group)]
    x = jnp.concatenate([part * rate for part in step], axis=0)
    high = x.astype(jnp.bfloat16)
    rest = x - high.astype(jnp.float32)
    middle = rest.astype(jnp.bfloat16)
    low = (rest - middle.astype(jnp.float32)).astype(jnp.bfloat16)
    s = lax.broadcasted_iota(jnp.int32, (length, length), 0)
    t = lax.broadcasted_iota(jnp.int32, (length, length), 1)
    ones = (s <= t).astype(jnp.float32).astype(jnp.bfloat16)
    total = jnp.dot(low, ones, preferred_element_type=jnp.float32)
    total = total + jnp.dot(middle, ones, preferred_element_type=jnp.float32)
    total = total + jnp.dot(high, ones, preferred_element_type=jnp.float32)
    shifted = total - jnp.log2(jnp.concatenate(step, axis=0))
    columns = shifted.T
    for r in range(per_group):
        rows_out[:heads, r * length:(r + 1) * length] = total[r * heads:(r + 1) * heads]
        rows_out[heads:, r * length:(r + 1) * length] = shifted[r * heads:(r + 1) * heads]
        column_out[r] = columns[:, r * heads:(r + 1) * heads]
    taps, width = taps_in.shape
    head_of = lax.broadcasted_iota(jnp.int32, (1, width), 1) // (width // heads)
    skip = jnp.zeros((1, width), jnp.float32)
    for h in range(heads):
        skip = jnp.where(head_of == h, skips[h], skip)
    channel[:taps] = taps_in[...]
    channel[taps:taps + 1] = bias[...]
    channel[taps + 1:taps + 2] = skip


def mix_kernel(
    groups, taps, begin, steps, direct, size, meta, base, shrunk, channel, rows_decay, column,
    rows_in, *rest
):
    tables, chunks = rest[:groups], rest[groups:]
    out, final, extended, scores, carried, weighted, ups, curs, table_sems, chunk_sems = (
        rest[-10:]
    )
    g = pl.program_id(0)
    position = begin + g
    r = meta[POS_REQ, position]
    length, width = base.shape
    half = length // 2
    heads = width // size
    depth = curs.shape[2]
    few = taps - 1
    parts = width // 128
    f32, bf16 = jnp.float32, jnp.bfloat16

    def fetch_chunk(source, i):
        pltpu.make_async_copy(source, curs.at[i], chunk_sems.at[i]).start()

    @pl.when(g == 0)
    def _():
        for i in range(steps):
            @pl.when(meta[POS_VALID, begin + i] > 0)
            def _(i=i):
                request = meta[POS_REQ, begin + i]
                fetch_table(groups, meta, request, tables, ups.at[i], table_sems.at[i])
                if i < direct:
                    fetch_chunk(chunks[i], i)
                elif i > direct:
                    fetch_chunk(chunks[direct + 4].at[i - direct - 1], i)
                else:
                    line = meta[MISC, ME] // 2
                    own, across, from_left, from_right = chunks[direct:direct + 4]
                    candidates = [own.at[line], across.at[line], from_left, from_right]
                    which = which_candidate(meta, meta[OHOLDER, 0])
                    for k, candidate in enumerate(candidates):
                        @pl.when(which == k)
                        def _(candidate=candidate):
                            fetch_chunk(candidate, direct)

    @pl.when(meta[POS_VALID, position] > 0)
    def _():
        present = meta[PRESENT, r] > 0
        write, read = rows_in[:, :depth], rows_in[:, depth:]
        all_scores = lax.dot_general(write, read, NT, preferred_element_type=f32)
        s = lax.broadcasted_iota(jnp.int32, (half, half), 0)
        t = lax.broadcasted_iota(jnp.int32, (half, half), 1)
        scores[:half] = jnp.where(s <= t, all_scores[:half, :half], 0.0)
        scores[half:] = jnp.where(s <= t, all_scores[half:, half:], 0.0)
        late_scores = all_scores[:half, half:].astype(bf16)

        to_here, from_here = rows_decay[:heads, :], rows_decay[heads:, :]
        end = jnp.broadcast_to(to_here[:, length - 1:length], (heads, length))
        middle = jnp.broadcast_to(to_here[:, half - 1:half], (heads, half))
        grown = jnp.exp2(to_here)
        to_end = jnp.exp2(end - from_here)
        to_middle = jnp.exp2(middle - from_here[:, :half])
        past_middle = jnp.exp2(to_here[:, half:] - middle)
        kept = jnp.exp2(end[:, :depth])

        pltpu.make_async_copy(tables[0].at[0], ups.at[g], table_sems.at[g]).wait()
        extended[8:, :] = base[...].astype(f32) + lax.dot_general(
            shrunk[0], ups[g], TN, preferred_element_type=f32
        )
        pltpu.make_async_copy(curs.at[g], curs.at[g], chunk_sems.at[g]).wait()
        before = jnp.where(present, curs[g, width:, :].astype(f32), 0.0)
        for k in range(few):
            for part in range(parts):
                extended[8 - few + k:9 - few + k, part * 128:(part + 1) * 128] = (
                    before[k * parts + part:k * parts + part + 1, :]
                )
        from_state = lax.dot_general(curs[g, :width, :], read, NT, preferred_element_type=f32)
        carried[...] = jnp.where(present, from_state, 0.0)

        corner = jnp.zeros((half, half), bf16)
        for pair in range(heads // 2):
            lo, hi = pair * 2 * size, (pair + 1) * 2 * size
            v = channel[taps:taps + 1, lo:hi]
            for k in range(taps):
                first = 8 - few + k
                v = v + channel[k:k + 1, lo:hi] * extended[first:first + length, lo:hi]
            activated = v * (0.5 + 0.5 * jnp.tanh(0.5 * v))
            act = activated.astype(bf16).T
            wide = act.astype(f32)
            sums, early = [], []
            for i in range(2):
                h = 2 * pair + i
                a = act[i * size:(i + 1) * size, :]
                a32 = wide[i * size:(i + 1) * size, :]
                ds = jnp.broadcast_to(column[0, :, h:h + 1], (length, half))
                dt0, dt1 = to_here[h:h + 1, :half], to_here[h:h + 1, half:]
                m0 = jnp.exp2(jnp.minimum(dt0 - ds[:half], 126.0)) * scores[:half]
                m1 = jnp.exp2(jnp.minimum(dt1 - ds[half:], 126.0)) * scores[half:]
                mixing = jnp.concatenate(
                    [
                        jnp.concatenate([m0.astype(bf16), corner], axis=1),
                        jnp.concatenate([corner, m1.astype(bf16)], axis=1),
                    ],
                    axis=0,
                )
                total = jnp.dot(a, mixing, preferred_element_type=f32)
                sums.append(total + carried[h * size:(h + 1) * size, :] * grown[h:h + 1, :])
                weighted[h * size:(h + 1) * size, :] = (a32 * to_end[h:h + 1, :]).astype(bf16)
                early.append((a32[:, :half] * to_middle[h:h + 1, :]).astype(bf16))
            passed = jnp.dot(
                jnp.concatenate(early, axis=0), late_scores, preferred_element_type=f32
            )
            for i in range(2):
                h = 2 * pair + i
                late = passed[i * size:(i + 1) * size, :] * past_middle[h:h + 1, :]
                sums[i] = jnp.concatenate([sums[i][:, :half], sums[i][:, half:] + late], axis=1)
            skipped = channel[taps + 1:taps + 2, lo:hi] * activated
            out[:, lo:hi] = (jnp.concatenate(sums, axis=0).T + skipped).astype(out.dtype)
        fresh = jnp.dot(weighted[...], write, preferred_element_type=f32)
        for h in range(heads):
            rows = slice(h * size, (h + 1) * size)
            old = curs[g, rows, :].astype(f32) * kept[h:h + 1, :]
            old = jnp.where(present, old, 0.0)
            final[0, rows, :] = (fresh[rows, :] + old).astype(final.dtype)


def chunk_shape(cache, conv, width):
    conv_rows = conv.shape[0] * (width // 128)
    return (cache.shape[3] + -(-conv_rows // 16) * 16, cache.shape[4])


def body(
    hidden, base_in_projection, state_input_matrix, state_output_matrix, head_step_size,
    head_decay_rate, head_skip_scale, convolution_weight, convolution_bias, adapter_down_weight,
    adapter_up_weight, adapter_home_group, adapter_group_index, state_space_cache,
    convolution_cache, prefix_holder_device, prefix_cache_slot, prefix_block_count,
):
    groups, devices = lax.axis_size("group"), lax.axis_size("dev")
    tokens, width = base_in_projection.shape
    per_group = tokens // T_REQ
    assert per_group == devices and devices & (devices - 1) == 0 == groups & (groups - 1)
    heads = head_step_size.shape[0]
    size, depth = state_space_cache.shape[2:]
    rank = adapter_down_weight.shape[1]
    taps = convolution_weight.shape[0]
    bf16, f32 = jnp.bfloat16, jnp.float32
    limit = per_group // 2
    lines = devices // 2

    cache = state_space_cache.reshape(
        state_space_cache.shape[0], lines, 2, heads * size, depth
    )
    conv = convolution_cache.transpose(1, 0, 2)
    shape = chunk_shape(cache, conv, width)
    picks = [
        jax.ShapeDtypeStruct((ACAP,) + adapter_down_weight.shape[1:], bf16)
        for _ in range(groups - 1)
    ]
    packed = pl.pallas_call(
        functools.partial(pack_kernel, groups, devices, per_group, width),
        out_shape=(
            jax.ShapeDtypeStruct(META_SHAPE, jnp.int32),
            jax.ShapeDtypeStruct((state_input_matrix.shape[0], 2 * depth), bf16),
            jax.ShapeDtypeStruct((groups, ACAP) + adapter_down_weight.shape[1:], bf16),
            *picks,
            *[jax.ShapeDtypeStruct(shape, bf16) for _ in range(devices)],
            *[jax.ShapeDtypeStruct((lines,) + shape, bf16) for _ in range(2)],
        ),
        in_specs=smem(5) + pinned(3) + vmem(3),
        out_specs=tuple(smem(1) + vmem(2 + len(picks) + devices + 2)),
        scratch_shapes=[
            pltpu.SemaphoreType.DMA((groups * ACAP,)),
            pltpu.SemaphoreType.DMA((groups * ACAP,)),
            pltpu.SemaphoreType.DMA((devices,)),
            pltpu.SemaphoreType.DMA((2,)),
        ],
        cost_estimate=cost(),
        compiler_params=params(),
        name="pack",
    )(
        adapter_home_group.reshape(-1), adapter_group_index, prefix_holder_device.reshape(-1),
        prefix_cache_slot, prefix_block_count, adapter_down_weight, adapter_up_weight, cache,
        state_input_matrix, state_output_matrix, conv,
    )
    meta, rows_mine, packed = packed[0], packed[1], packed[2:]
    down_got = lax.all_to_all(packed[0], "group", split_axis=0, concat_axis=0, tiled=True)
    chunks = packed[groups:-2]
    rows_all = lax.all_gather(rows_mine, "dev", axis=0, tiled=True)
    zero = jnp.zeros((1,), jnp.int32)
    got = [chunks[0]] + [
        lax.ppermute(chunks[d], "dev", [(s, s ^ d) for s in range(devices)])
        for d in range(1, devices)
    ]

    spread_others = spread_rest(meta, cache, conv, devices, width, limit)

    up_send, _ = lax.optimization_barrier((packed[1:groups], got[lines]))
    up_got = swap(up_send, groups)

    rows_decay, column_decay, channel = pl.pallas_call(
        functools.partial(prep_kernel, per_group),
        out_shape=(
            jax.ShapeDtypeStruct((2 * heads, tokens), f32),
            jax.ShapeDtypeStruct((per_group, T_REQ, heads), f32),
            jax.ShapeDtypeStruct((8, width), f32),
        ),
        in_specs=smem(2) + vmem(3) + anywhere(1),
        out_specs=tuple(pl.BlockSpec(memory_space=pltpu.VMEM) for _ in range(3)),
        cost_estimate=cost(),
        compiler_params=params(),
        name="prep",
    )(
        head_decay_rate, head_skip_scale, head_step_size, convolution_weight,
        convolution_bias.reshape(1, width), meta,
    )

    each = per_group // 2
    partial_down = pl.pallas_call(
        functools.partial(shrink_kernel, per_group),
        grid_spec=pltpu.PrefetchScalarGridSpec(
            num_scalar_prefetch=1,
            grid=(per_group // each,),
            in_specs=[pl.BlockSpec((each * T_REQ, hidden.shape[1]), lambda g, meta: (g, 0))]
            + anywhere(5),
            out_specs=pl.BlockSpec((each, rank, T_REQ), lambda g, meta: (g, 0, 0)),
            scratch_shapes=[
                pltpu.VMEM((per_group,) + adapter_down_weight.shape[1:], bf16),
                pltpu.SemaphoreType.DMA((per_group,)),
            ],
        ),
        out_shape=jax.ShapeDtypeStruct((per_group, rank, T_REQ), bf16),
        cost_estimate=cost(),
        compiler_params=params(),
        name="shrink",
    )(meta, hidden, down_got, channel, got[lines], got[lines + 1], spread_others)

    parts = lax.all_to_all(partial_down, "dev", split_axis=0, concat_axis=0, tiled=True)
    summed = pl.pallas_call(
        sum_kernel,
        out_shape=jax.ShapeDtypeStruct((devices, 1, rank, T_REQ), bf16),
        in_specs=vmem(1),
        out_specs=vmem(1)[0],
        cost_estimate=cost(),
        compiler_params=params(),
        name="sum_parts",
    )(parts.reshape(devices, 1, rank, T_REQ))
    shrunk = lax.all_to_all(summed, "dev", split_axis=0, concat_axis=0, tiled=True)
    shrunk = shrunk.reshape(per_group, rank, T_REQ)

    befores = [[partial_down], [summed, up_got[groups // 2 - 1]], [rows_all, up_got[-1]]]
    spread = spread_steps(zero, meta, packed[-2:], devices)
    next(spread)
    for step in range(1, lines):
        sent = spread.send(befores.pop(0) if befores else [])
    spread = spread.send([])

    outs = None
    for begin, steps in ((0, lines), (lines, devices - lines + limit)):
        if begin == 0:
            chunks, after = got[:lines], [sent, got[lines + 2], got[lines + 3]]
        else:
            chunks, after = [*got[lines:], *spread, spread_others], []

        def request(g, meta, begin=begin):
            return meta[POS_REQ, begin + g]

        in_specs = [
            pl.BlockSpec((T_REQ, width), lambda g, meta: (request(g, meta), 0)),
            pl.BlockSpec((1, rank, T_REQ), lambda g, meta: (request(g, meta), 0, 0)),
            pl.BlockSpec((8, width), lambda g, meta: (0, 0)),
            pl.BlockSpec((2 * heads, T_REQ), lambda g, meta: (0, request(g, meta))),
            pl.BlockSpec((1, T_REQ, heads), lambda g, meta: (request(g, meta), 0, 0)),
            pl.BlockSpec((T_REQ, 2 * depth), lambda g, meta: (request(g, meta), 0)),
        ] + anywhere(groups + len(chunks) + len(after))
        operands = [
            meta, base_in_projection, shrunk, channel, rows_decay, column_decay, rows_all,
            adapter_up_weight, *up_got, *chunks, *after,
        ]
        aliases = {}
        if outs is not None:
            aliases = {len(operands): 0, len(operands) + 1: 1}
            operands += list(outs)
            in_specs += anywhere(2)
        outs = pl.pallas_call(
            functools.partial(mix_kernel, groups, taps, begin, steps, lines, size),
            grid_spec=pltpu.PrefetchScalarGridSpec(
                num_scalar_prefetch=1,
                grid=(steps,),
                in_specs=in_specs,
                out_specs=(
                    pl.BlockSpec((T_REQ, width), lambda g, meta: (request(g, meta), 0)),
                    pl.BlockSpec(
                        (1, heads * size, depth), lambda g, meta: (request(g, meta), 0, 0)
                    ),
                ),
                scratch_shapes=[
                    pltpu.VMEM((T_REQ + 8, width), f32),
                    pltpu.VMEM((T_REQ, T_REQ // 2), f32),
                    pltpu.VMEM((width, T_REQ), f32),
                    pltpu.VMEM((width, T_REQ), bf16),
                    pltpu.VMEM((steps,) + adapter_up_weight.shape[1:], bf16),
                    pltpu.VMEM((steps,) + shape, bf16),
                    pltpu.SemaphoreType.DMA((steps,)),
                    pltpu.SemaphoreType.DMA((steps,)),
                ],
            ),
            out_shape=(
                jax.ShapeDtypeStruct((tokens, width), bf16),
                jax.ShapeDtypeStruct((per_group, heads * size, depth), bf16),
            ),
            input_output_aliases=aliases,
            cost_estimate=cost(),
            compiler_params=params(),
            name=f"mix_{begin}",
        )(*operands)
    return outs[0], outs[1].reshape(per_group, heads, size, depth)


def solution(mesh):
    placed = (
        P("group", "dev"),
        P("group", "dev"),
        P(("group", "dev"), None),
        P(("group", "dev"), None),
        P("dev", "group"),
        P("dev"),
        P("dev"),
        P(None, "dev"),
        P("dev"),
        P("group", None, "dev"),
        P("group", None, "dev"),
        P(),
        P(),
        P(("group", "dev"), None, None, None),
        P(("group", "dev"), None, None),
        P(),
        P(),
        P(),
    )
    return jax.shard_map(
        body,
        mesh=mesh,
        in_specs=placed,
        out_specs=(P("group", "dev"), P("group", "dev", None, None)),
        check_vma=False,
    )
```

```python
import functools
import math

import jax
import jax.numpy as jnp
from jax import lax
from jax.experimental import pallas as pl
from jax.experimental.pallas import tpu as pltpu
from jax.sharding import PartitionSpec as P

T_REQ = 256
CAP = 2
ACAP = 4
LOG2E = math.log2(math.e)
NT = (((1,), (1,)), ((), ()))
TN = (((0,), (0,)), ((), ()))
VMEM_LIMIT = 63 * 1024 * 1024

HOME, DIST, ARANK, AINDEX, PRESENT, ENT_REQ, ENT_VALID, ENT_FROM, ENT_PLACE, MISC, SEND = range(11)
ME, SLOT = range(2)
META_SHAPE = (16, 64)


def cost():
    return pl.CostEstimate(flops=0, bytes_accessed=1 << 16, transcendentals=0)


def params():
    return pltpu.CompilerParams(vmem_limit_bytes=VMEM_LIMIT)


def smem(count):
    return [pl.BlockSpec(memory_space=pltpu.SMEM) for _ in range(count)]


def vmem(count):
    return [pl.BlockSpec(memory_space=pltpu.VMEM) for _ in range(count)]


def pinned(count):
    return [pl.BlockSpec(memory_space=pltpu.HBM) for _ in range(count)]


def anywhere(count):
    return [pl.BlockSpec(memory_space=pl.ANY) for _ in range(count)]


def as_int(flag):
    return flag.astype(jnp.int32)


def ranks_of(labels):
    ranks = []
    for q, label in enumerate(labels):
        total = jnp.int32(0)
        for other in labels[:q]:
            total = total + as_int(other == label)
        ranks.append(total)
    return ranks


def calls_of(devices, per_group):
    near = devices - max(devices // 4, 1)
    late = min(per_group, (devices - near) * CAP)
    return (range(near), 0, per_group), (range(near, devices), per_group, late)


def plan(groups, devices, per_group, home, index, holder, slot, blocks, meta):
    my_group = lax.axis_index("group")
    me = lax.axis_index("dev")
    first = my_group * per_group

    homes = [home[first + q] for q in range(per_group)]
    for q, rank in enumerate(ranks_of(homes)):
        meta[HOME, q] = homes[q]
        meta[DIST, q] = lax.bitwise_xor(homes[q], my_group)
        meta[ARANK, q] = rank
        meta[AINDEX, q] = index[first + q]
        meta[PRESENT, q] = as_int(blocks[first + q] > 0)
    for k in range(groups):
        theirs = lax.bitwise_xor(my_group, k) * per_group
        seen = jnp.int32(0)
        chosen = [jnp.int32(0) for _ in range(ACAP)]
        for q in range(per_group):
            hit = home[theirs + q] == my_group
            value = index[theirs + q]
            for c in range(ACAP):
                chosen[c] = jnp.where(hit & (seen == c), value, chosen[c])
            seen = seen + as_int(hit)
        for c in range(ACAP):
            meta[SEND, k * ACAP + c] = chosen[c]

    holders = [holder[first + q] for q in range(per_group)]
    ranks = ranks_of(holders)
    for c in range(CAP):
        chosen = jnp.int32(0)
        for q in range(per_group):
            chosen = jnp.where((holders[q] == me) & (ranks[q] == c), slot[first + q], chosen)
        meta[MISC, SLOT + c] = chosen
    meta[MISC, ME] = me
    for distances, begin, steps in calls_of(devices, per_group):
        count = jnp.int32(0)
        for d in distances:
            for q in range(per_group):
                hit = holders[q] == lax.bitwise_xor(me, d)

                @pl.when(hit)
                def _(d=d, q=q, count=count):
                    meta[ENT_REQ, begin + count] = jnp.int32(q)
                    meta[ENT_VALID, begin + count] = jnp.int32(1)
                    meta[ENT_FROM, begin + count] = jnp.int32(d)
                    meta[ENT_PLACE, begin + count] = ranks[q]

                count = count + as_int(hit)

        @pl.when(count == 0)
        def _(begin=begin):
            for row in (ENT_REQ, ENT_VALID, ENT_FROM, ENT_PLACE):
                meta[row, begin] = meta[row, 0]

        count = jnp.maximum(count, 1)
        for i in range(1, steps):
            @pl.when(i >= count)
            def _(i=i, begin=begin):
                meta[ENT_REQ, begin + i] = meta[ENT_REQ, begin + i - 1]
                meta[ENT_VALID, begin + i] = jnp.int32(0)


def start_adapters(groups, meta, table, outs, sems):
    copies = []
    for k in reversed(range(groups) if len(outs) == 1 else range(1, groups)):
        for c in range(ACAP):
            chosen = meta[SEND, k * ACAP + c]
            if len(outs) == 1:
                out = outs[0].at[lax.bitwise_xor(lax.axis_index("group"), k), c]
            else:
                out = outs[k - 1].at[c]
            copy = pltpu.make_async_copy(table.at[chosen], out, sems.at[k * ACAP + c])
            copy.start()
            copies.append(copy)
    return copies


def swap(packed, groups):
    return [
        lax.ppermute(packed[k - 1], "group", [(g, g ^ k) for g in range(groups)])
        for k in range(1, groups)
    ]


def copy_conv(conv, slot, target, width, out, at):
    parts = width // 128
    begin = pl.multiple_of(target * width, 128)
    for k in range(conv.shape[0]):
        rows = conv[k, :, pl.ds(begin, width)]
        row = rows[:1, :]
        for c in range(1, conv.shape[1]):
            row = jnp.where(slot == c, rows[c:c + 1, :], row)
        for part in range(parts):
            place = at + k * parts + part
            out[place:place + 1, :] = row[:, part * 128:(part + 1) * 128]


def start_state(devices, meta, cache, outs, sems):
    copies = []
    for d in reversed(range(devices)):
        target = lax.bitwise_xor(meta[MISC, ME], d)
        for c in range(CAP):
            copy = pltpu.make_async_copy(
                cache.at[meta[MISC, SLOT + c], target],
                outs[d].at[c, pl.ds(0, cache.shape[2])], sems.at[d, c],
            )
            copy.start()
            copies.append(copy)
    return copies


def pack_kernel(
    groups, devices, per_group, width, home, index, holder, slot, blocks, down, up, cache, write,
    read, conv, meta, rows_out, *rest
):
    downs, rest = rest[:1], rest[1:]
    ups, rest = rest[:groups - 1], rest[groups - 1:]
    chunks, (down_sems, up_sems, chunk_sems) = rest[:devices], rest[devices:]
    plan(groups, devices, per_group, home, index, holder, slot, blocks, meta)
    copies = start_adapters(groups, meta, down, downs, down_sems)
    copies += start_state(devices, meta, cache, chunks, chunk_sems)
    copies += start_adapters(groups, meta, up, ups, up_sems)
    depth = write.shape[1]
    rows_out[:, :depth] = write[...]
    rows_out[:, depth:] = read[...]
    for d in range(devices):
        target = lax.bitwise_xor(meta[MISC, ME], d)
        for c in range(CAP):
            copy_conv(
                conv, meta[MISC, SLOT + c], target, width, chunks[d].at[c], cache.shape[2]
            )
    for copy in copies:
        copy.wait()


def fetch_table(groups, meta, r, tables, out, sem):
    dist = meta[DIST, r]
    for k in range(groups):
        row = meta[ARANK, r] if k else meta[AINDEX, r]

        @pl.when(dist == k)
        def _(k=k, row=row):
            pltpu.make_async_copy(tables[k].at[row], out, sem).start()


def shrink_kernel(per_group, meta, hidden, table, *rest):
    out, picked, sems = rest[-3:]
    g = pl.program_id(0)
    each = out.shape[0]

    @pl.when(g == 0)
    def _():
        for r in range(per_group):
            pltpu.make_async_copy(
                table.at[meta[HOME, r], meta[ARANK, r]], picked.at[r], sems.at[r]
            ).start()

    for i in range(each):
        r = g * each + i
        pltpu.make_async_copy(table.at[0, 0], picked.at[r], sems.at[r]).wait()
    for i in range(each):
        part = lax.dot_general(
            hidden[i * T_REQ:(i + 1) * T_REQ, :], picked[g * each + i], NT,
            preferred_element_type=jnp.float32,
        )
        out[i] = part.T.astype(out.dtype)


def sum_kernel(parts, *rest):
    out = rest[-1]
    total = parts[0].astype(jnp.float32)
    for k in range(1, parts.shape[0]):
        total = total + parts[k].astype(jnp.float32)
    total = total.astype(out.dtype)
    for k in range(out.shape[0]):
        out[k] = total


def prep_kernel(per_group, rates, skips, steps, taps_in, bias, *rest):
    rows_out, column_out, channel = rest[-3:]
    heads, tokens = steps.shape
    length = tokens // per_group
    rate = jnp.zeros((heads, length), jnp.float32)
    place = lax.broadcasted_iota(jnp.int32, rate.shape, 0)
    for h in range(heads):
        rate = jnp.where(place == h, rates[h] * (-LOG2E), rate)
    step = [steps[:, r * length:(r + 1) * length] for r in range(per_group)]
    x = jnp.concatenate([part * rate for part in step], axis=0)
    high = x.astype(jnp.bfloat16)
    rest = x - high.astype(jnp.float32)
    middle = rest.astype(jnp.bfloat16)
    low = (rest - middle.astype(jnp.float32)).astype(jnp.bfloat16)
    s = lax.broadcasted_iota(jnp.int32, (length, length), 0)
    t = lax.broadcasted_iota(jnp.int32, (length, length), 1)
    ones = (s <= t).astype(jnp.float32).astype(jnp.bfloat16)
    total = jnp.dot(low, ones, preferred_element_type=jnp.float32)
    total = total + jnp.dot(middle, ones, preferred_element_type=jnp.float32)
    total = total + jnp.dot(high, ones, preferred_element_type=jnp.float32)
    shifted = total - jnp.log2(jnp.concatenate(step, axis=0))
    columns = shifted.T
    for r in range(per_group):
        rows_out[:heads, r * length:(r + 1) * length] = total[r * heads:(r + 1) * heads]
        rows_out[heads:, r * length:(r + 1) * length] = shifted[r * heads:(r + 1) * heads]
        column_out[r] = columns[:, r * heads:(r + 1) * heads]
    taps, width = taps_in.shape
    head_of = lax.broadcasted_iota(jnp.int32, (1, width), 1) // (width // heads)
    skip = jnp.zeros((1, width), jnp.float32)
    for h in range(heads):
        skip = jnp.where(head_of == h, skips[h], skip)
    channel[:taps] = taps_in[...]
    channel[taps:taps + 1] = bias[...]
    channel[taps + 1:taps + 2] = skip


def mix_kernel(
    groups, taps, begin, steps, size, meta, base, shrunk, channel, rows_decay, column,
    rows_in, *rest
):
    tables, chunks = rest[:groups], rest[groups:groups + lax.axis_size("dev")]
    out, final, extended, scores, carried, weighted, ups, curs, table_sems, chunk_sems = (
        rest[-10:]
    )
    g = pl.program_id(0)
    entry = begin + g
    r = meta[ENT_REQ, entry]
    length, width = base.shape
    half = length // 2
    heads = width // size
    depth = curs.shape[2]
    few = taps - 1
    parts = width // 128
    f32, bf16 = jnp.float32, jnp.bfloat16

    def fetch_chunk(source, i):
        pltpu.make_async_copy(source, curs.at[i], chunk_sems.at[i]).start()

    @pl.when(g == 0)
    def _():
        for i in range(steps):
            @pl.when(meta[ENT_VALID, begin + i] > 0)
            def _(i=i):
                request = meta[ENT_REQ, begin + i]
                fetch_table(groups, meta, request, tables, ups.at[i], table_sems.at[i])
                source = meta[ENT_FROM, begin + i]
                for d, chunk in enumerate(chunks):
                    @pl.when(source == d)
                    def _(chunk=chunk):
                        fetch_chunk(chunk.at[meta[ENT_PLACE, begin + i]], i)

    @pl.when(meta[ENT_VALID, entry] > 0)
    def _():
        present = meta[PRESENT, r] > 0
        write, read = rows_in[:, :depth], rows_in[:, depth:]
        all_scores = lax.dot_general(write, read, NT, preferred_element_type=f32)
        s = lax.broadcasted_iota(jnp.int32, (half, half), 0)
        t = lax.broadcasted_iota(jnp.int32, (half, half), 1)
        scores[:half] = jnp.where(s <= t, all_scores[:half, :half], 0.0)
        scores[half:] = jnp.where(s <= t, all_scores[half:, half:], 0.0)
        late_scores = all_scores[:half, half:].astype(bf16)

        to_here, from_here = rows_decay[:heads, :], rows_decay[heads:, :]
        end = jnp.broadcast_to(to_here[:, length - 1:length], (heads, length))
        middle = jnp.broadcast_to(to_here[:, half - 1:half], (heads, half))
        grown = jnp.exp2(to_here)
        to_end = jnp.exp2(end - from_here)
        to_middle = jnp.exp2(middle - from_here[:, :half])
        past_middle = jnp.exp2(to_here[:, half:] - middle)
        kept = jnp.exp2(end[:, :depth])

        pltpu.make_async_copy(tables[0].at[0], ups.at[g], table_sems.at[g]).wait()
        extended[8:, :] = base[...].astype(f32) + lax.dot_general(
            shrunk[0], ups[g], TN, preferred_element_type=f32
        )
        pltpu.make_async_copy(curs.at[g], curs.at[g], chunk_sems.at[g]).wait()
        before = jnp.where(present, curs[g, width:, :].astype(f32), 0.0)
        for k in range(few):
            for part in range(parts):
                extended[8 - few + k:9 - few + k, part * 128:(part + 1) * 128] = (
                    before[k * parts + part:k * parts + part + 1, :]
                )
        from_state = lax.dot_general(curs[g, :width, :], read, NT, preferred_element_type=f32)
        carried[...] = jnp.where(present, from_state, 0.0)

        corner = jnp.zeros((half, half), bf16)
        for pair in range(heads // 2):
            lo, hi = pair * 2 * size, (pair + 1) * 2 * size
            v = channel[taps:taps + 1, lo:hi]
            for k in range(taps):
                first = 8 - few + k
                v = v + channel[k:k + 1, lo:hi] * extended[first:first + length, lo:hi]
            activated = v * (0.5 + 0.5 * jnp.tanh(0.5 * v))
            act = activated.astype(bf16).T
            wide = act.astype(f32)
            sums, early = [], []
            for i in range(2):
                h = 2 * pair + i
                a = act[i * size:(i + 1) * size, :]
                a32 = wide[i * size:(i + 1) * size, :]
                ds = jnp.broadcast_to(column[0, :, h:h + 1], (length, half))
                dt0, dt1 = to_here[h:h + 1, :half], to_here[h:h + 1, half:]
                m0 = jnp.exp2(jnp.minimum(dt0 - ds[:half], 126.0)) * scores[:half]
                m1 = jnp.exp2(jnp.minimum(dt1 - ds[half:], 126.0)) * scores[half:]
                mixing = jnp.concatenate(
                    [
                        jnp.concatenate([m0.astype(bf16), corner], axis=1),
                        jnp.concatenate([corner, m1.astype(bf16)], axis=1),
                    ],
                    axis=0,
                )
                total = jnp.dot(a, mixing, preferred_element_type=f32)
                sums.append(total + carried[h * size:(h + 1) * size, :] * grown[h:h + 1, :])
                weighted[h * size:(h + 1) * size, :] = (a32 * to_end[h:h + 1, :]).astype(bf16)
                early.append((a32[:, :half] * to_middle[h:h + 1, :]).astype(bf16))
            passed = jnp.dot(
                jnp.concatenate(early, axis=0), late_scores, preferred_element_type=f32
            )
            for i in range(2):
                h = 2 * pair + i
                late = passed[i * size:(i + 1) * size, :] * past_middle[h:h + 1, :]
                sums[i] = jnp.concatenate([sums[i][:, :half], sums[i][:, half:] + late], axis=1)
            skipped = channel[taps + 1:taps + 2, lo:hi] * activated
            out[:, lo:hi] = (jnp.concatenate(sums, axis=0).T + skipped).astype(out.dtype)
        fresh = jnp.dot(weighted[...], write, preferred_element_type=f32)
        for h in range(heads):
            rows = slice(h * size, (h + 1) * size)
            old = curs[g, rows, :].astype(f32) * kept[h:h + 1, :]
            old = jnp.where(present, old, 0.0)
            final[0, rows, :] = (fresh[rows, :] + old).astype(final.dtype)


def chunk_shape(cache, conv, width):
    conv_rows = conv.shape[0] * (width // 128)
    return (cache.shape[2] + -(-conv_rows // 16) * 16, cache.shape[3])


def body(
    hidden, base_in_projection, state_input_matrix, state_output_matrix, head_step_size,
    head_decay_rate, head_skip_scale, convolution_weight, convolution_bias, adapter_down_weight,
    adapter_up_weight, adapter_home_group, adapter_group_index, state_space_cache,
    convolution_cache, prefix_holder_device, prefix_cache_slot, prefix_block_count,
):
    groups, devices = lax.axis_size("group"), lax.axis_size("dev")
    tokens, width = base_in_projection.shape
    per_group = tokens // T_REQ
    assert per_group == devices and devices & (devices - 1) == 0 == groups & (groups - 1)
    heads = head_step_size.shape[0]
    size, depth = state_space_cache.shape[2:]
    rank = adapter_down_weight.shape[1]
    taps = convolution_weight.shape[0]
    bf16, f32 = jnp.bfloat16, jnp.float32

    cache = state_space_cache.reshape(
        state_space_cache.shape[0], devices, heads * size, depth
    )
    conv = convolution_cache.transpose(1, 0, 2)
    shape = chunk_shape(cache, conv, width)
    picks = [
        jax.ShapeDtypeStruct((ACAP,) + adapter_down_weight.shape[1:], bf16)
        for _ in range(groups - 1)
    ]
    packed = pl.pallas_call(
        functools.partial(pack_kernel, groups, devices, per_group, width),
        out_shape=(
            jax.ShapeDtypeStruct(META_SHAPE, jnp.int32),
            jax.ShapeDtypeStruct((state_input_matrix.shape[0], 2 * depth), bf16),
            jax.ShapeDtypeStruct((groups, ACAP) + adapter_down_weight.shape[1:], bf16),
            *picks,
            *[jax.ShapeDtypeStruct((CAP,) + shape, bf16) for _ in range(devices)],
        ),
        in_specs=smem(5) + pinned(3) + vmem(3),
        out_specs=tuple(smem(1) + vmem(2 + len(picks) + devices)),
        scratch_shapes=[
            pltpu.SemaphoreType.DMA((groups * ACAP,)),
            pltpu.SemaphoreType.DMA((groups * ACAP,)),
            pltpu.SemaphoreType.DMA((devices, CAP)),
        ],
        cost_estimate=cost(),
        compiler_params=params(),
        name="pack",
    )(
        adapter_home_group.reshape(-1), adapter_group_index, prefix_holder_device.reshape(-1),
        prefix_cache_slot, prefix_block_count, adapter_down_weight, adapter_up_weight, cache,
        state_input_matrix, state_output_matrix, conv,
    )
    meta, rows_mine, packed = packed[0], packed[1], packed[2:]
    down_got = lax.all_to_all(packed[0], "group", split_axis=0, concat_axis=0, tiled=True)
    chunks = packed[groups:]
    rows_all = lax.all_gather(rows_mine, "dev", axis=0, tiled=True)
    got = [chunks[0]] + [
        lax.ppermute(chunks[d], "dev", [(s, s ^ d) for s in range(devices)])
        for d in range(1, devices)
    ]

    up_send, _ = lax.optimization_barrier((packed[1:groups], got[1]))
    up_got = swap(up_send, groups)

    rows_decay, column_decay, channel = pl.pallas_call(
        functools.partial(prep_kernel, per_group),
        out_shape=(
            jax.ShapeDtypeStruct((2 * heads, tokens), f32),
            jax.ShapeDtypeStruct((per_group, T_REQ, heads), f32),
            jax.ShapeDtypeStruct((8, width), f32),
        ),
        in_specs=smem(2) + vmem(3) + anywhere(1),
        out_specs=tuple(pl.BlockSpec(memory_space=pltpu.VMEM) for _ in range(3)),
        cost_estimate=cost(),
        compiler_params=params(),
        name="prep",
    )(
        head_decay_rate, head_skip_scale, head_step_size, convolution_weight,
        convolution_bias.reshape(1, width), meta,
    )

    each = per_group // 2
    early = [*got[1:devices // 2 + 1], up_got[0]]
    partial_down = pl.pallas_call(
        functools.partial(shrink_kernel, per_group),
        grid_spec=pltpu.PrefetchScalarGridSpec(
            num_scalar_prefetch=1,
            grid=(per_group // each,),
            in_specs=[pl.BlockSpec((each * T_REQ, hidden.shape[1]), lambda g, meta: (g, 0))]
            + anywhere(2 + len(early)),
            out_specs=pl.BlockSpec((each, rank, T_REQ), lambda g, meta: (g, 0, 0)),
            scratch_shapes=[
                pltpu.VMEM((per_group,) + adapter_down_weight.shape[1:], bf16),
                pltpu.SemaphoreType.DMA((per_group,)),
            ],
        ),
        out_shape=jax.ShapeDtypeStruct((per_group, rank, T_REQ), bf16),
        cost_estimate=cost(),
        compiler_params=params(),
        name="shrink",
    )(meta, hidden, down_got, channel, *early)

    parts = lax.all_to_all(partial_down, "dev", split_axis=0, concat_axis=0, tiled=True)
    summed = pl.pallas_call(
        sum_kernel,
        out_shape=jax.ShapeDtypeStruct((devices, 1, rank, T_REQ), bf16),
        in_specs=vmem(1),
        out_specs=vmem(1)[0],
        cost_estimate=cost(),
        compiler_params=params(),
        name="sum_parts",
    )(parts.reshape(devices, 1, rank, T_REQ))
    shrunk = lax.all_to_all(summed, "dev", split_axis=0, concat_axis=0, tiled=True)
    shrunk = shrunk.reshape(per_group, rank, T_REQ)

    outs = None
    for distances, begin, steps in calls_of(devices, per_group):
        ready = [got[d] if d < distances.stop else chunks[d] for d in range(devices)]

        def request(g, meta, begin=begin):
            return meta[ENT_REQ, begin + g]

        in_specs = [
            pl.BlockSpec((T_REQ, width), lambda g, meta: (request(g, meta), 0)),
            pl.BlockSpec((1, rank, T_REQ), lambda g, meta: (request(g, meta), 0, 0)),
            pl.BlockSpec((8, width), lambda g, meta: (0, 0)),
            pl.BlockSpec((2 * heads, T_REQ), lambda g, meta: (0, request(g, meta))),
            pl.BlockSpec((1, T_REQ, heads), lambda g, meta: (request(g, meta), 0, 0)),
            pl.BlockSpec((T_REQ, 2 * depth), lambda g, meta: (request(g, meta), 0)),
        ] + anywhere(groups + devices)
        operands = [
            meta, base_in_projection, shrunk, channel, rows_decay, column_decay, rows_all,
            adapter_up_weight, *up_got, *ready,
        ]
        aliases = {}
        if outs is not None:
            aliases = {len(operands): 0, len(operands) + 1: 1}
            operands += list(outs)
            in_specs += anywhere(2)
        outs = pl.pallas_call(
            functools.partial(mix_kernel, groups, taps, begin, steps, size),
            grid_spec=pltpu.PrefetchScalarGridSpec(
                num_scalar_prefetch=1,
                grid=(steps,),
                in_specs=in_specs,
                out_specs=(
                    pl.BlockSpec((T_REQ, width), lambda g, meta: (request(g, meta), 0)),
                    pl.BlockSpec(
                        (1, heads * size, depth), lambda g, meta: (request(g, meta), 0, 0)
                    ),
                ),
                scratch_shapes=[
                    pltpu.VMEM((T_REQ + 8, width), f32),
                    pltpu.VMEM((T_REQ, T_REQ // 2), f32),
                    pltpu.VMEM((width, T_REQ), f32),
                    pltpu.VMEM((width, T_REQ), bf16),
                    pltpu.VMEM((steps,) + adapter_up_weight.shape[1:], bf16),
                    pltpu.VMEM((steps,) + shape, bf16),
                    pltpu.SemaphoreType.DMA((steps,)),
                    pltpu.SemaphoreType.DMA((steps,)),
                ],
            ),
            out_shape=(
                jax.ShapeDtypeStruct((tokens, width), bf16),
                jax.ShapeDtypeStruct((per_group, heads * size, depth), bf16),
            ),
            input_output_aliases=aliases,
            cost_estimate=cost(),
            compiler_params=params(),
            name=f"mix_{begin}",
        )(*operands)
    return outs[0], outs[1].reshape(per_group, heads, size, depth)


def solution(mesh):
    placed = (
        P("group", "dev"),
        P("group", "dev"),
        P(("group", "dev"), None),
        P(("group", "dev"), None),
        P("dev", "group"),
        P("dev"),
        P("dev"),
        P(None, "dev"),
        P("dev"),
        P("group", None, "dev"),
        P("group", None, "dev"),
        P(),
        P(),
        P(("group", "dev"), None, None, None),
        P(("group", "dev"), None, None),
        P(),
        P(),
        P(),
    )
    return jax.shard_map(
        body,
        mesh=mesh,
        in_specs=placed,
        out_specs=(P("group", "dev"), P("group", "dev", None, None)),
        check_vma=False,
    )
```

```python
import functools
import math

import jax
import jax.numpy as jnp
from jax import lax
from jax.experimental import pallas as pl
from jax.experimental.pallas import tpu as pltpu
from jax.sharding import PartitionSpec as P

T_REQ = 256
CAP = 2
ACAP = 4
LOG2E = math.log2(math.e)
NT = (((1,), (1,)), ((), ()))
TN = (((0,), (0,)), ((), ()))
VMEM_LIMIT = 63 * 1024 * 1024

HOME, DIST, ARANK, AINDEX, PRESENT, POS_REQ, POS_VALID, OSLOT, OHOLDER, MISC, SEND = range(11)
MOST, ME, SLOT = range(3)
META_SHAPE = (16, 64)


def cost():
    return pl.CostEstimate(flops=0, bytes_accessed=1 << 16, transcendentals=0)


def params():
    return pltpu.CompilerParams(vmem_limit_bytes=VMEM_LIMIT)


def smem(count):
    return [pl.BlockSpec(memory_space=pltpu.SMEM) for _ in range(count)]


def vmem(count):
    return [pl.BlockSpec(memory_space=pltpu.VMEM) for _ in range(count)]


def pinned(count):
    return [pl.BlockSpec(memory_space=pltpu.HBM) for _ in range(count)]


def anywhere(count):
    return [pl.BlockSpec(memory_space=pl.ANY) for _ in range(count)]


def as_int(flag):
    return flag.astype(jnp.int32)


def ranks_of(labels):
    ranks = []
    for q, label in enumerate(labels):
        total = jnp.int32(0)
        for other in labels[:q]:
            total = total + as_int(other == label)
        ranks.append(total)
    return ranks


def near_distances(devices):
    return devices - max(devices // 4, 1)


def plan(groups, devices, per_group, home, index, holder, slot, blocks, meta):
    my_group = lax.axis_index("group")
    me = lax.axis_index("dev")
    first = my_group * per_group
    limit = per_group // 2
    for j in range(limit):
        meta[POS_REQ, devices + j] = jnp.int32(-1)
        meta[POS_VALID, devices + j] = jnp.int32(0)
        meta[OSLOT, j] = jnp.int32(0)
        meta[OHOLDER, j] = jnp.int32(0)

    homes = [home[first + q] for q in range(per_group)]
    for q, rank in enumerate(ranks_of(homes)):
        meta[HOME, q] = homes[q]
        meta[DIST, q] = lax.bitwise_xor(homes[q], my_group)
        meta[ARANK, q] = rank
        meta[AINDEX, q] = index[first + q]
        meta[PRESENT, q] = as_int(blocks[first + q] > 0)
    for k in range(groups):
        theirs = lax.bitwise_xor(my_group, k) * per_group
        seen = jnp.int32(0)
        chosen = [jnp.int32(0) for _ in range(ACAP)]
        for q in range(per_group):
            hit = home[theirs + q] == my_group
            value = index[theirs + q]
            for c in range(ACAP):
                chosen[c] = jnp.where(hit & (seen == c), value, chosen[c])
            seen = seen + as_int(hit)
        for c in range(ACAP):
            meta[SEND, k * ACAP + c] = chosen[c]

    holders = [holder[first + q] for q in range(per_group)]
    ranks = ranks_of(holders)
    count = jnp.int32(0)
    my_slot = jnp.int32(0)
    for q in range(per_group):
        my_slot = jnp.where((holders[q] == me) & (ranks[q] == 0), slot[first + q], my_slot)

        @pl.when(ranks[q] > 0)
        def _():
            meta[POS_REQ, devices + count] = jnp.int32(q)
            meta[POS_VALID, devices + count] = jnp.int32(1)
            meta[OSLOT, count] = slot[first + q]
            meta[OHOLDER, count] = holders[q]

        count = count + as_int(ranks[q] > 0)
    spread = meta[POS_REQ, devices]
    requests = []
    for d in range(devices):
        source = lax.bitwise_xor(me, d)
        request = jnp.int32(-1)
        for q in range(per_group):
            request = jnp.where((holders[q] == source) & (ranks[q] == 0), q, request)
        meta[POS_VALID, d] = as_int(request >= 0)
        requests.append(request)
    requests += [meta[POS_REQ, devices + j] for j in range(limit)]
    near = near_distances(devices)
    for begin, end in ((0, near), (near, devices + limit)):
        last = jnp.int32(-1)
        filled = []
        for p in range(begin, end):
            last = jnp.where(requests[p] >= 0, requests[p], last)
            filled.append(last)
        following = jnp.maximum(spread, 0)
        for p in reversed(range(begin, end)):
            following = jnp.where(filled[p - begin] >= 0, filled[p - begin], following)
            meta[POS_REQ, p] = following
    most = jnp.int32(0)
    for g in range(groups):
        labels = [holder[g * per_group + q] for q in range(per_group)]
        total = jnp.int32(0)
        for rank in ranks_of(labels):
            total = total + as_int(rank > 0)
        most = jnp.maximum(most, total)
    meta[MISC, MOST] = most
    meta[MISC, ME] = me
    meta[MISC, SLOT] = my_slot


def start_adapters(groups, meta, table, outs, sems):
    copies = []
    for k in reversed(range(groups) if len(outs) == 1 else range(1, groups)):
        for c in range(ACAP):
            chosen = meta[SEND, k * ACAP + c]
            if len(outs) == 1:
                out = outs[0].at[lax.bitwise_xor(lax.axis_index("group"), k), c]
            else:
                out = outs[k - 1].at[c]
            copy = pltpu.make_async_copy(table.at[chosen], out, sems.at[k * ACAP + c])
            copy.start()
            copies.append(copy)
    return copies


def swap(packed, groups):
    return [
        lax.ppermute(packed[k - 1], "group", [(g, g ^ k) for g in range(groups)])
        for k in range(1, groups)
    ]


def copy_conv(conv, slot, target, width, out, at):
    parts = width // 128
    begin = pl.multiple_of(target * width, 128)
    for k in range(conv.shape[0]):
        rows = conv[k, :, pl.ds(begin, width)]
        row = rows[:1, :]
        for c in range(1, conv.shape[1]):
            row = jnp.where(slot == c, rows[c:c + 1, :], row)
        for part in range(parts):
            place = at + k * parts + part
            out[place:place + 1, :] = row[:, part * 128:(part + 1) * 128]


def start_state(devices, meta, cache, outs, sems):
    copies = []
    for d in reversed(range(devices)):
        target = lax.bitwise_xor(meta[MISC, ME], d)
        copy = pltpu.make_async_copy(
            cache.at[meta[MISC, SLOT], target // 2, target % 2],
            outs[d].at[pl.ds(0, cache.shape[3])], sems.at[d],
        )
        copy.start()
        copies.append(copy)
    return copies


def start_across(j, meta, cache, across, own, sems):
    x = meta[MISC, ME] % 2
    copies = []
    for k, (out, place) in enumerate(((across, 1 - x), (own, x))):
        copy = pltpu.make_async_copy(
            cache.at[meta[OSLOT, j], :, place], out.at[:, pl.ds(0, cache.shape[3])], sems.at[k]
        )
        copy.start()
        copies.append(copy)
    return copies


def conv_across(lines, width, j, meta, conv, state_rows, across, own):
    x = meta[MISC, ME] % 2
    for out, place in ((across, 1 - x), (own, x)):
        for m in range(lines):
            copy_conv(conv, meta[OSLOT, j], 2 * m + place, width, out.at[m], state_rows)


def pack_kernel(
    groups, devices, per_group, width, home, index, holder, slot, blocks, down, up, cache, write,
    read, conv, meta, rows_out, *rest
):
    downs, rest = rest[:1], rest[1:]
    ups, rest = rest[:groups - 1], rest[groups - 1:]
    chunks, (across, own, down_sems, up_sems, chunk_sems, across_sems) = (
        rest[:devices], rest[devices:]
    )
    plan(groups, devices, per_group, home, index, holder, slot, blocks, meta)
    copies = start_adapters(groups, meta, down, downs, down_sems)
    copies += start_state(devices, meta, cache, chunks, chunk_sems)
    copies += start_across(0, meta, cache, across, own, across_sems)
    copies += start_adapters(groups, meta, up, ups, up_sems)
    depth = write.shape[1]
    rows_out[:, :depth] = write[...]
    rows_out[:, depth:] = read[...]
    state_rows = cache.shape[3]
    for d in range(devices):
        target = lax.bitwise_xor(meta[MISC, ME], d)
        copy_conv(conv, meta[MISC, SLOT], target, width, chunks[d], state_rows)
    conv_across(devices // 2, width, 0, meta, conv, state_rows, across, own)
    for copy in copies:
        copy.wait()


def pack_across_kernel(lines, width, j, meta, cache, conv, across, own, sems):
    copies = start_across(j[0], meta, cache, across, own, sems)
    conv_across(lines, width, j[0], meta, conv, cache.shape[3], across, own)
    for copy in copies:
        copy.wait()


def pick_kernel(step, lines, j, meta, own_r, over_r, own_l, over_l, *rest):
    out_r, out_l = rest[-2:]
    me = meta[MISC, ME]
    source = meta[OHOLDER, j[0]]
    same = source // 2 == me // 2
    mine = same & (source % 2 == me % 2)
    across = same & (source % 2 != me % 2)

    @pl.when(mine)
    def _():
        out_r[...] = own_r[0]
        out_l[...] = own_l[0]

    @pl.when(across)
    def _():
        out_r[...] = over_r[0]
        out_l[...] = over_l[0]

    @pl.when(jnp.logical_not(same))
    def _():
        if step > 1:
            out_r[...] = rest[0][...]
            out_l[...] = rest[1][...]
        else:
            out_r[...] = jnp.zeros_like(out_r)
            out_l[...] = jnp.zeros_like(out_l)


def right_block(meta, step, lines):
    return jnp.clip(lines + meta[MISC, ME] // 2 - step, 0, lines - 1)


def left_block(meta, step, lines):
    return jnp.clip(meta[MISC, ME] // 2 + step - lines, 0, lines - 1)


def pack_across(j, meta, cache, conv, devices, width):
    lines = devices // 2
    shape = chunk_shape(cache, conv, width)
    return pl.pallas_call(
        functools.partial(pack_across_kernel, lines, width),
        out_shape=tuple(jax.ShapeDtypeStruct((lines,) + shape, cache.dtype) for _ in range(2)),
        in_specs=smem(2) + pinned(1) + vmem(1),
        out_specs=tuple(vmem(2)),
        scratch_shapes=[pltpu.SemaphoreType.DMA((2,))],
        cost_estimate=cost(),
        compiler_params=params(),
        name="pack_across",
    )(j, meta, cache, conv)


def spread_steps(j, meta, packed, devices):
    lines = devices // 2
    send, own = packed
    shape = own.shape[1:]
    across = lax.ppermute(send, "dev", [(d, d ^ 1) for d in range(devices)])
    from_left = from_right = None
    after = yield across
    whole = pl.BlockSpec(shape, lambda g, j, meta: (0, 0))
    for step in range(1, lines):
        blocks = [
            pl.BlockSpec(
                (1,) + shape, lambda g, j, meta, at=at, step=step: (at(meta, step, lines), 0, 0)
            )
            for at in (right_block, left_block)
        ]
        operands = [own, across, own, across]
        in_specs = [blocks[0], blocks[0], blocks[1], blocks[1]]
        if step > 1:
            operands += [from_left, from_right]
            in_specs += [whole, whole]
        operands += after
        in_specs += anywhere(len(after))
        to_right, to_left = pl.pallas_call(
            functools.partial(pick_kernel, step, lines),
            grid_spec=pltpu.PrefetchScalarGridSpec(
                num_scalar_prefetch=2, grid=(1,), in_specs=in_specs, out_specs=(whole, whole)
            ),
            out_shape=tuple(jax.ShapeDtypeStruct(shape, own.dtype) for _ in range(2)),
            cost_estimate=cost(),
            compiler_params=params(),
            name=f"pick_{step}",
        )(j, meta, *operands)
        from_left = lax.ppermute(
            to_right, "dev",
            [(2 * i + x, 2 * i + 2 + x) for i in range(step) for x in range(2)],
        )
        from_right = lax.ppermute(
            to_left, "dev",
            [(devices - 1 - (2 * i + x), devices - 3 - (2 * i + x))
             for i in range(step) for x in range(2)],
        )
        after = yield to_right
    yield own, across, from_left, from_right


def final_specs(shape):
    line = pl.BlockSpec((1,) + shape, lambda g, j, meta: (meta[MISC, ME] // 2, 0, 0))
    whole = pl.BlockSpec(shape, lambda g, j, meta: (0, 0))
    return [line, line, whole, whole]


def which_candidate(meta, source):
    me = meta[MISC, ME]
    same = source // 2 == me // 2
    mine = same & (source % 2 == me % 2)
    return jnp.where(mine, 0, jnp.where(same, 1, jnp.where(source // 2 < me // 2, 2, 3)))


def final_kernel(j, meta, own, across, from_left, from_right, out):
    which = which_candidate(meta, meta[OHOLDER, j[0]])
    picks = (own.at[0], across.at[0], from_left, from_right)
    for k, pick in enumerate(picks):
        @pl.when(which == k)
        def _(pick=pick):
            out[...] = pick[...]


def spread_rest(meta, cache, conv, devices, width, limit):
    shape = chunk_shape(cache, conv, width)

    def one(j, held):
        jj = j.reshape(1)
        packed = pack_across(jj, meta, cache, conv, devices, width)
        steps = spread_steps(jj, meta, packed, devices)
        next(steps)
        for _ in range(devices // 2):
            got = steps.send([])
        block = pl.pallas_call(
            final_kernel,
            grid_spec=pltpu.PrefetchScalarGridSpec(
                num_scalar_prefetch=2,
                grid=(1,),
                in_specs=final_specs(shape),
                out_specs=pl.BlockSpec(shape, lambda g, j, meta: (0, 0)),
            ),
            out_shape=jax.ShapeDtypeStruct(shape, cache.dtype),
            compiler_params=params(),
            name="final_pick",
        )(jj, meta, *got)
        return lax.dynamic_update_slice_in_dim(held, block[None], j - 1, 0)

    held = jnp.zeros((limit - 1,) + shape, cache.dtype)
    return lax.fori_loop(jnp.int32(1), meta[MISC, MOST], one, held)


def fetch_table(groups, meta, r, tables, out, sem):
    dist = meta[DIST, r]
    for k in range(groups):
        row = meta[ARANK, r] if k else meta[AINDEX, r]

        @pl.when(dist == k)
        def _(k=k, row=row):
            pltpu.make_async_copy(tables[k].at[row], out, sem).start()


def shrink_kernel(per_group, meta, hidden, table, *rest):
    out, picked, sems = rest[-3:]
    g = pl.program_id(0)
    each = out.shape[0]

    @pl.when(g == 0)
    def _():
        for r in range(per_group):
            pltpu.make_async_copy(
                table.at[meta[HOME, r], meta[ARANK, r]], picked.at[r], sems.at[r]
            ).start()

    for i in range(each):
        r = g * each + i
        pltpu.make_async_copy(table.at[0, 0], picked.at[r], sems.at[r]).wait()
    for i in range(each):
        part = lax.dot_general(
            hidden[i * T_REQ:(i + 1) * T_REQ, :], picked[g * each + i], NT,
            preferred_element_type=jnp.float32,
        )
        out[i] = part.T.astype(out.dtype)


def sum_kernel(parts, *rest):
    out = rest[-1]
    total = parts[0].astype(jnp.float32)
    for k in range(1, parts.shape[0]):
        total = total + parts[k].astype(jnp.float32)
    total = total.astype(out.dtype)
    for k in range(out.shape[0]):
        out[k] = total


def prep_kernel(per_group, rates, skips, steps, taps_in, bias, *rest):
    rows_out, column_out, channel = rest[-3:]
    heads, tokens = steps.shape
    length = tokens // per_group
    rate = jnp.zeros((heads, length), jnp.float32)
    place = lax.broadcasted_iota(jnp.int32, rate.shape, 0)
    for h in range(heads):
        rate = jnp.where(place == h, rates[h] * (-LOG2E), rate)
    step = [steps[:, r * length:(r + 1) * length] for r in range(per_group)]
    x = jnp.concatenate([part * rate for part in step], axis=0)
    high = x.astype(jnp.bfloat16)
    rest = x - high.astype(jnp.float32)
    middle = rest.astype(jnp.bfloat16)
    low = (rest - middle.astype(jnp.float32)).astype(jnp.bfloat16)
    s = lax.broadcasted_iota(jnp.int32, (length, length), 0)
    t = lax.broadcasted_iota(jnp.int32, (length, length), 1)
    ones = (s <= t).astype(jnp.float32).astype(jnp.bfloat16)
    total = jnp.dot(low, ones, preferred_element_type=jnp.float32)
    total = total + jnp.dot(middle, ones, preferred_element_type=jnp.float32)
    total = total + jnp.dot(high, ones, preferred_element_type=jnp.float32)
    shifted = total - jnp.log2(jnp.concatenate(step, axis=0))
    columns = shifted.T
    for r in range(per_group):
        rows_out[:heads, r * length:(r + 1) * length] = total[r * heads:(r + 1) * heads]
        rows_out[heads:, r * length:(r + 1) * length] = shifted[r * heads:(r + 1) * heads]
        column_out[r] = columns[:, r * heads:(r + 1) * heads]
    taps, width = taps_in.shape
    head_of = lax.broadcasted_iota(jnp.int32, (1, width), 1) // (width // heads)
    skip = jnp.zeros((1, width), jnp.float32)
    for h in range(heads):
        skip = jnp.where(head_of == h, skips[h], skip)
    channel[:taps] = taps_in[...]
    channel[taps:taps + 1] = bias[...]
    channel[taps + 1:taps + 2] = skip


def mix_kernel(
    groups, taps, begin, steps, direct, size, meta, base, shrunk, channel, rows_decay, column,
    rows_in, *rest
):
    tables, chunks = rest[:groups], rest[groups:]
    out, final, done, extended, scores, carried, weighted, ups, curs, table_sems, chunk_sems = (
        rest[-11:]
    )
    g = pl.program_id(0)
    position = begin + g
    r = meta[POS_REQ, position]
    length, width = base.shape
    half = length // 2
    heads = width // size
    depth = curs.shape[2]
    few = taps - 1
    parts = width // 128
    f32, bf16 = jnp.float32, jnp.bfloat16

    done[...] = jnp.zeros_like(done)

    def fetch_chunk(source, i):
        pltpu.make_async_copy(source, curs.at[i], chunk_sems.at[i]).start()

    @pl.when(g == 0)
    def _():
        for i in range(steps):
            @pl.when(meta[POS_VALID, begin + i] > 0)
            def _(i=i):
                request = meta[POS_REQ, begin + i]
                fetch_table(groups, meta, request, tables, ups.at[i], table_sems.at[i])
                if i < direct:
                    fetch_chunk(chunks[i], i)
                elif i > direct:
                    fetch_chunk(chunks[direct + 4].at[i - direct - 1], i)
                else:
                    line = meta[MISC, ME] // 2
                    own, across, from_left, from_right = chunks[direct:direct + 4]
                    candidates = [own.at[line], across.at[line], from_left, from_right]
                    which = which_candidate(meta, meta[OHOLDER, 0])
                    for k, candidate in enumerate(candidates):
                        @pl.when(which == k)
                        def _(candidate=candidate):
                            fetch_chunk(candidate, direct)

    @pl.when(meta[POS_VALID, position] > 0)
    def _():
        present = meta[PRESENT, r] > 0
        write, read = rows_in[:, :depth], rows_in[:, depth:]
        all_scores = lax.dot_general(write, read, NT, preferred_element_type=f32)
        s = lax.broadcasted_iota(jnp.int32, (half, half), 0)
        t = lax.broadcasted_iota(jnp.int32, (half, half), 1)
        scores[:half] = jnp.where(s <= t, all_scores[:half, :half], 0.0)
        scores[half:] = jnp.where(s <= t, all_scores[half:, half:], 0.0)
        late_scores = all_scores[:half, half:].astype(bf16)

        to_here, from_here = rows_decay[:heads, :], rows_decay[heads:, :]
        end = jnp.broadcast_to(to_here[:, length - 1:length], (heads, length))
        middle = jnp.broadcast_to(to_here[:, half - 1:half], (heads, half))
        grown = jnp.exp2(to_here)
        to_end = jnp.exp2(end - from_here)
        to_middle = jnp.exp2(middle - from_here[:, :half])
        past_middle = jnp.exp2(to_here[:, half:] - middle)
        kept = jnp.exp2(end[:, :depth])

        pltpu.make_async_copy(tables[0].at[0], ups.at[g], table_sems.at[g]).wait()
        extended[8:, :] = base[...].astype(f32) + lax.dot_general(
            shrunk[0], ups[g], TN, preferred_element_type=f32
        )
        pltpu.make_async_copy(curs.at[g], curs.at[g], chunk_sems.at[g]).wait()
        before = jnp.where(present, curs[g, width:, :].astype(f32), 0.0)
        for k in range(few):
            for part in range(parts):
                extended[8 - few + k:9 - few + k, part * 128:(part + 1) * 128] = (
                    before[k * parts + part:k * parts + part + 1, :]
                )
        from_state = lax.dot_general(curs[g, :width, :], read, NT, preferred_element_type=f32)
        carried[...] = jnp.where(present, from_state, 0.0)

        corner = jnp.zeros((half, half), bf16)
        for pair in range(heads // 2):
            lo, hi = pair * 2 * size, (pair + 1) * 2 * size
            v = channel[taps:taps + 1, lo:hi]
            for k in range(taps):
                first = 8 - few + k
                v = v + channel[k:k + 1, lo:hi] * extended[first:first + length, lo:hi]
            activated = v * (0.5 + 0.5 * jnp.tanh(0.5 * v))
            act = activated.astype(bf16).T
            wide = act.astype(f32)
            sums, early = [], []
            for i in range(2):
                h = 2 * pair + i
                a = act[i * size:(i + 1) * size, :]
                a32 = wide[i * size:(i + 1) * size, :]
                ds = jnp.broadcast_to(column[0, :, h:h + 1], (length, half))
                dt0, dt1 = to_here[h:h + 1, :half], to_here[h:h + 1, half:]
                m0 = jnp.exp2(jnp.minimum(dt0 - ds[:half], 126.0)) * scores[:half]
                m1 = jnp.exp2(jnp.minimum(dt1 - ds[half:], 126.0)) * scores[half:]
                mixing = jnp.concatenate(
                    [
                        jnp.concatenate([m0.astype(bf16), corner], axis=1),
                        jnp.concatenate([corner, m1.astype(bf16)], axis=1),
                    ],
                    axis=0,
                )
                total = jnp.dot(a, mixing, preferred_element_type=f32)
                sums.append(total + carried[h * size:(h + 1) * size, :] * grown[h:h + 1, :])
                weighted[h * size:(h + 1) * size, :] = (a32 * to_end[h:h + 1, :]).astype(bf16)
                early.append((a32[:, :half] * to_middle[h:h + 1, :]).astype(bf16))
            passed = jnp.dot(
                jnp.concatenate(early, axis=0), late_scores, preferred_element_type=f32
            )
            for i in range(2):
                h = 2 * pair + i
                late = passed[i * size:(i + 1) * size, :] * past_middle[h:h + 1, :]
                sums[i] = jnp.concatenate([sums[i][:, :half], sums[i][:, half:] + late], axis=1)
            skipped = channel[taps + 1:taps + 2, lo:hi] * activated
            out[:, lo:hi] = (jnp.concatenate(sums, axis=0).T + skipped).astype(out.dtype)
        fresh = jnp.dot(weighted[...], write, preferred_element_type=f32)
        for h in range(heads):
            rows = slice(h * size, (h + 1) * size)
            old = curs[g, rows, :].astype(f32) * kept[h:h + 1, :]
            old = jnp.where(present, old, 0.0)
            final[0, rows, :] = (fresh[rows, :] + old).astype(final.dtype)


def chunk_shape(cache, conv, width):
    conv_rows = conv.shape[0] * (width // 128)
    return (cache.shape[3] + -(-conv_rows // 16) * 16, cache.shape[4])


def body(
    hidden, base_in_projection, state_input_matrix, state_output_matrix, head_step_size,
    head_decay_rate, head_skip_scale, convolution_weight, convolution_bias, adapter_down_weight,
    adapter_up_weight, adapter_home_group, adapter_group_index, state_space_cache,
    convolution_cache, prefix_holder_device, prefix_cache_slot, prefix_block_count,
):
    groups, devices = lax.axis_size("group"), lax.axis_size("dev")
    tokens, width = base_in_projection.shape
    per_group = tokens // T_REQ
    assert per_group == devices and devices & (devices - 1) == 0 == groups & (groups - 1)
    heads = head_step_size.shape[0]
    size, depth = state_space_cache.shape[2:]
    rank = adapter_down_weight.shape[1]
    taps = convolution_weight.shape[0]
    bf16, f32 = jnp.bfloat16, jnp.float32
    limit = per_group // 2
    lines = devices // 2

    cache = state_space_cache.reshape(
        state_space_cache.shape[0], lines, 2, heads * size, depth
    )
    conv = convolution_cache.transpose(1, 0, 2)
    shape = chunk_shape(cache, conv, width)
    picks = [
        jax.ShapeDtypeStruct((ACAP,) + adapter_down_weight.shape[1:], bf16)
        for _ in range(groups - 1)
    ]
    packed = pl.pallas_call(
        functools.partial(pack_kernel, groups, devices, per_group, width),
        out_shape=(
            jax.ShapeDtypeStruct(META_SHAPE, jnp.int32),
            jax.ShapeDtypeStruct((state_input_matrix.shape[0], 2 * depth), bf16),
            jax.ShapeDtypeStruct((groups, ACAP) + adapter_down_weight.shape[1:], bf16),
            *picks,
            *[jax.ShapeDtypeStruct(shape, bf16) for _ in range(devices)],
            *[jax.ShapeDtypeStruct((lines,) + shape, bf16) for _ in range(2)],
        ),
        in_specs=smem(5) + pinned(3) + vmem(3),
        out_specs=tuple(smem(1) + vmem(2 + len(picks) + devices + 2)),
        scratch_shapes=[
            pltpu.SemaphoreType.DMA((groups * ACAP,)),
            pltpu.SemaphoreType.DMA((groups * ACAP,)),
            pltpu.SemaphoreType.DMA((devices,)),
            pltpu.SemaphoreType.DMA((2,)),
        ],
        cost_estimate=cost(),
        compiler_params=params(),
        name="pack",
    )(
        adapter_home_group.reshape(-1), adapter_group_index, prefix_holder_device.reshape(-1),
        prefix_cache_slot, prefix_block_count, adapter_down_weight, adapter_up_weight, cache,
        state_input_matrix, state_output_matrix, conv,
    )
    meta, rows_mine, packed = packed[0], packed[1], packed[2:]
    down_got = lax.all_to_all(packed[0], "group", split_axis=0, concat_axis=0, tiled=True)
    chunks = packed[groups:-2]
    rows_all = lax.all_gather(rows_mine, "dev", axis=0, tiled=True)
    zero = jnp.zeros((1,), jnp.int32)
    near = near_distances(devices)
    got = [chunks[0]] + [
        lax.ppermute(chunks[d], "dev", [(s, s ^ d) for s in range(devices)])
        for d in range(1, near)
    ]

    spread_others = spread_rest(meta, cache, conv, devices, width, limit)

    up_send, _ = lax.optimization_barrier((packed[1:groups], got[2]))
    up_got = swap(up_send, groups)

    rows_decay, column_decay, channel = pl.pallas_call(
        functools.partial(prep_kernel, per_group),
        out_shape=(
            jax.ShapeDtypeStruct((2 * heads, tokens), f32),
            jax.ShapeDtypeStruct((per_group, T_REQ, heads), f32),
            jax.ShapeDtypeStruct((8, width), f32),
        ),
        in_specs=smem(2) + vmem(3) + anywhere(1),
        out_specs=tuple(pl.BlockSpec(memory_space=pltpu.VMEM) for _ in range(3)),
        cost_estimate=cost(),
        compiler_params=params(),
        name="prep",
    )(
        head_decay_rate, head_skip_scale, head_step_size, convolution_weight,
        convolution_bias.reshape(1, width), meta,
    )

    each = per_group // 2
    early = got[2:]
    partial_down = pl.pallas_call(
        functools.partial(shrink_kernel, per_group),
        grid_spec=pltpu.PrefetchScalarGridSpec(
            num_scalar_prefetch=1,
            grid=(per_group // each,),
            in_specs=[pl.BlockSpec((each * T_REQ, hidden.shape[1]), lambda g, meta: (g, 0))]
            + anywhere(3 + len(early)),
            out_specs=pl.BlockSpec((each, rank, T_REQ), lambda g, meta: (g, 0, 0)),
            scratch_shapes=[
                pltpu.VMEM((per_group,) + adapter_down_weight.shape[1:], bf16),
                pltpu.SemaphoreType.DMA((per_group,)),
            ],
        ),
        out_shape=jax.ShapeDtypeStruct((per_group, rank, T_REQ), bf16),
        cost_estimate=cost(),
        compiler_params=params(),
        name="shrink",
    )(meta, hidden, down_got, channel, spread_others, *early)

    parts = lax.all_to_all(partial_down, "dev", split_axis=0, concat_axis=0, tiled=True)
    summed = pl.pallas_call(
        sum_kernel,
        out_shape=jax.ShapeDtypeStruct((devices, 1, rank, T_REQ), bf16),
        in_specs=vmem(1),
        out_specs=vmem(1)[0],
        cost_estimate=cost(),
        compiler_params=params(),
        name="sum_parts",
    )(parts.reshape(devices, 1, rank, T_REQ))
    shrunk = lax.all_to_all(summed, "dev", split_axis=0, concat_axis=0, tiled=True)
    shrunk = shrunk.reshape(per_group, rank, T_REQ)

    late, _ = lax.optimization_barrier((chunks[near:], shrunk))
    got += [
        lax.ppermute(x, "dev", [(s, s ^ d) for s in range(devices)])
        for d, x in zip(range(near, devices), late)
    ]
    spread = spread_steps(zero, meta, packed[-2:], devices)
    next(spread)
    for step in range(1, lines - 1):
        sent = spread.send([partial_down] if step < lines - 2 else [shrunk])

    outs = None
    for begin, steps in ((0, near), (near, devices - near + limit)):
        if begin == 0:
            chunks, after = got[:near], [sent]
        else:
            spread.send([outs[2]])
            chunks, after = [*got[near:], *spread.send([]), spread_others], []

        def request(g, meta, begin=begin):
            return meta[POS_REQ, begin + g]

        in_specs = [
            pl.BlockSpec((T_REQ, width), lambda g, meta: (request(g, meta), 0)),
            pl.BlockSpec((1, rank, T_REQ), lambda g, meta: (request(g, meta), 0, 0)),
            pl.BlockSpec((8, width), lambda g, meta: (0, 0)),
            pl.BlockSpec((2 * heads, T_REQ), lambda g, meta: (0, request(g, meta))),
            pl.BlockSpec((1, T_REQ, heads), lambda g, meta: (request(g, meta), 0, 0)),
            pl.BlockSpec((T_REQ, 2 * depth), lambda g, meta: (request(g, meta), 0)),
        ] + anywhere(groups + len(chunks) + len(after))
        operands = [
            meta, base_in_projection, shrunk, channel, rows_decay, column_decay, rows_all,
            adapter_up_weight, *up_got, *chunks, *after,
        ]
        aliases = {}
        if outs is not None:
            aliases = {len(operands): 0, len(operands) + 1: 1}
            operands += list(outs[:2])
            in_specs += anywhere(2)
        outs = pl.pallas_call(
            functools.partial(
                mix_kernel, groups, taps, begin, steps, near if begin == 0 else devices - near, size
            ),
            grid_spec=pltpu.PrefetchScalarGridSpec(
                num_scalar_prefetch=1,
                grid=(steps,),
                in_specs=in_specs,
                out_specs=(
                    pl.BlockSpec((T_REQ, width), lambda g, meta: (request(g, meta), 0)),
                    pl.BlockSpec(
                        (1, heads * size, depth), lambda g, meta: (request(g, meta), 0, 0)
                    ),
                    pl.BlockSpec((8, 128), lambda g, meta: (0, 0)),
                ),
                scratch_shapes=[
                    pltpu.VMEM((T_REQ + 8, width), f32),
                    pltpu.VMEM((T_REQ, T_REQ // 2), f32),
                    pltpu.VMEM((width, T_REQ), f32),
                    pltpu.VMEM((width, T_REQ), bf16),
                    pltpu.VMEM((steps,) + adapter_up_weight.shape[1:], bf16),
                    pltpu.VMEM((steps,) + shape, bf16),
                    pltpu.SemaphoreType.DMA((steps,)),
                    pltpu.SemaphoreType.DMA((steps,)),
                ],
            ),
            out_shape=(
                jax.ShapeDtypeStruct((tokens, width), bf16),
                jax.ShapeDtypeStruct((per_group, heads * size, depth), bf16),
                jax.ShapeDtypeStruct((8, 128), f32),
            ),
            input_output_aliases=aliases,
            cost_estimate=cost(),
            compiler_params=params(),
            name=f"mix_{begin}",
        )(*operands)
    return outs[0], outs[1].reshape(per_group, heads, size, depth)


def solution(mesh):
    placed = (
        P("group", "dev"),
        P("group", "dev"),
        P(("group", "dev"), None),
        P(("group", "dev"), None),
        P("dev", "group"),
        P("dev"),
        P("dev"),
        P(None, "dev"),
        P("dev"),
        P("group", None, "dev"),
        P("group", None, "dev"),
        P(),
        P(),
        P(("group", "dev"), None, None, None),
        P(("group", "dev"), None, None),
        P(),
        P(),
        P(),
    )
    return jax.shard_map(
        body,
        mesh=mesh,
        in_specs=placed,
        out_specs=(P("group", "dev"), P("group", "dev", None, None)),
        check_vma=False,
    )
```

```python
import functools
import math

import jax
import jax.numpy as jnp
from jax import lax
from jax.experimental import pallas as pl
from jax.experimental.pallas import tpu as pltpu
from jax.sharding import PartitionSpec as P

T_REQ = 256
CAP = 2
ACAP = 4
LOG2E = math.log2(math.e)
NT = (((1,), (1,)), ((), ()))
TN = (((0,), (0,)), ((), ()))
VMEM_LIMIT = 63 * 1024 * 1024

HOME, DIST, ARANK, AINDEX, PRESENT, POS_REQ, POS_VALID, OSLOT, OHOLDER, MISC, SEND = range(11)
MOST, ME, SLOT = range(3)
META_SHAPE = (16, 64)


def cost():
    return pl.CostEstimate(flops=0, bytes_accessed=1 << 16, transcendentals=0)


def params():
    return pltpu.CompilerParams(vmem_limit_bytes=VMEM_LIMIT)


def smem(count):
    return [pl.BlockSpec(memory_space=pltpu.SMEM) for _ in range(count)]


def vmem(count):
    return [pl.BlockSpec(memory_space=pltpu.VMEM) for _ in range(count)]


def pinned(count):
    return [pl.BlockSpec(memory_space=pltpu.HBM) for _ in range(count)]


def anywhere(count):
    return [pl.BlockSpec(memory_space=pl.ANY) for _ in range(count)]


def as_int(flag):
    return flag.astype(jnp.int32)


def ranks_of(labels):
    ranks = []
    for q, label in enumerate(labels):
        total = jnp.int32(0)
        for other in labels[:q]:
            total = total + as_int(other == label)
        ranks.append(total)
    return ranks


def plan(groups, devices, per_group, home, index, holder, slot, blocks, meta):
    my_group = lax.axis_index("group")
    me = lax.axis_index("dev")
    first = my_group * per_group
    limit = per_group // 2
    for j in range(limit):
        meta[POS_REQ, devices + j] = jnp.int32(-1)
        meta[POS_VALID, devices + j] = jnp.int32(0)
        meta[OSLOT, j] = jnp.int32(0)
        meta[OHOLDER, j] = jnp.int32(0)

    homes = [home[first + q] for q in range(per_group)]
    for q, rank in enumerate(ranks_of(homes)):
        meta[HOME, q] = homes[q]
        meta[DIST, q] = lax.bitwise_xor(homes[q], my_group)
        meta[ARANK, q] = rank
        meta[AINDEX, q] = index[first + q]
        meta[PRESENT, q] = as_int(blocks[first + q] > 0)
    for k in range(groups):
        theirs = lax.bitwise_xor(my_group, k) * per_group
        seen = jnp.int32(0)
        chosen = [jnp.int32(0) for _ in range(ACAP)]
        for q in range(per_group):
            hit = home[theirs + q] == my_group
            value = index[theirs + q]
            for c in range(ACAP):
                chosen[c] = jnp.where(hit & (seen == c), value, chosen[c])
            seen = seen + as_int(hit)
        for c in range(ACAP):
            meta[SEND, k * ACAP + c] = chosen[c]

    holders = [holder[first + q] for q in range(per_group)]
    ranks = ranks_of(holders)
    count = jnp.int32(0)
    my_slot = jnp.int32(0)
    for q in range(per_group):
        my_slot = jnp.where((holders[q] == me) & (ranks[q] == 0), slot[first + q], my_slot)

        @pl.when(ranks[q] > 0)
        def _():
            meta[POS_REQ, devices + count] = jnp.int32(q)
            meta[POS_VALID, devices + count] = jnp.int32(1)
            meta[OSLOT, count] = slot[first + q]
            meta[OHOLDER, count] = holders[q]

        count = count + as_int(ranks[q] > 0)
    spread = meta[POS_REQ, devices]
    requests = []
    for d in range(devices):
        source = lax.bitwise_xor(me, d)
        request = jnp.int32(-1)
        for q in range(per_group):
            request = jnp.where((holders[q] == source) & (ranks[q] == 0), q, request)
        meta[POS_VALID, d] = as_int(request >= 0)
        requests.append(request)
    requests += [meta[POS_REQ, devices + j] for j in range(limit)]
    for begin, end in ((0, devices // 2), (devices // 2, devices + limit)):
        last = jnp.int32(-1)
        filled = []
        for p in range(begin, end):
            last = jnp.where(requests[p] >= 0, requests[p], last)
            filled.append(last)
        following = jnp.maximum(spread, 0)
        for p in reversed(range(begin, end)):
            following = jnp.where(filled[p - begin] >= 0, filled[p - begin], following)
            meta[POS_REQ, p] = following
    most = jnp.int32(0)
    for g in range(groups):
        labels = [holder[g * per_group + q] for q in range(per_group)]
        total = jnp.int32(0)
        for rank in ranks_of(labels):
            total = total + as_int(rank > 0)
        most = jnp.maximum(most, total)
    meta[MISC, MOST] = most
    meta[MISC, ME] = me
    meta[MISC, SLOT] = my_slot


def start_adapters(groups, meta, table, outs, sems):
    copies = []
    for k in reversed(range(groups) if len(outs) == 1 else range(1, groups)):
        for c in range(ACAP):
            chosen = meta[SEND, k * ACAP + c]
            if len(outs) == 1:
                out = outs[0].at[lax.bitwise_xor(lax.axis_index("group"), k), c]
            else:
                out = outs[k - 1].at[c]
            copy = pltpu.make_async_copy(table.at[chosen], out, sems.at[k * ACAP + c])
            copy.start()
            copies.append(copy)
    return copies


def swap(packed, groups):
    return [
        lax.ppermute(packed[k - 1], "group", [(g, g ^ k) for g in range(groups)])
        for k in range(1, groups)
    ]


def copy_conv(conv, slot, target, width, out, at):
    parts = width // 128
    begin = pl.multiple_of(target * width, 128)
    for k in range(conv.shape[0]):
        rows = conv[k, :, pl.ds(begin, width)]
        row = rows[:1, :]
        for c in range(1, conv.shape[1]):
            row = jnp.where(slot == c, rows[c:c + 1, :], row)
        for part in range(parts):
            place = at + k * parts + part
            out[place:place + 1, :] = row[:, part * 128:(part + 1) * 128]


def start_state(devices, meta, cache, outs, sems):
    copies = []
    for d in reversed(range(devices)):
        target = lax.bitwise_xor(meta[MISC, ME], d)
        copy = pltpu.make_async_copy(
            cache.at[meta[MISC, SLOT], target // 2, target % 2],
            outs[d].at[pl.ds(0, cache.shape[3])], sems.at[d],
        )
        copy.start()
        copies.append(copy)
    return copies


def start_across(j, meta, cache, across, own, sems):
    x = meta[MISC, ME] % 2
    copies = []
    for k, (out, place) in enumerate(((across, 1 - x), (own, x))):
        copy = pltpu.make_async_copy(
            cache.at[meta[OSLOT, j], :, place], out.at[:, pl.ds(0, cache.shape[3])], sems.at[k]
        )
        copy.start()
        copies.append(copy)
    return copies


def conv_across(lines, width, j, meta, conv, state_rows, across, own):
    x = meta[MISC, ME] % 2
    for out, place in ((across, 1 - x), (own, x)):
        for m in range(lines):
            copy_conv(conv, meta[OSLOT, j], 2 * m + place, width, out.at[m], state_rows)


def pack_kernel(
    groups, devices, per_group, width, home, index, holder, slot, blocks, down, up, cache, write,
    read, conv, meta, rows_out, *rest
):
    downs, rest = rest[:1], rest[1:]
    ups, rest = rest[:groups - 1], rest[groups - 1:]
    chunks, (across, own, down_sems, up_sems, chunk_sems, across_sems) = (
        rest[:devices], rest[devices:]
    )
    plan(groups, devices, per_group, home, index, holder, slot, blocks, meta)
    copies = start_adapters(groups, meta, down, downs, down_sems)
    copies += start_state(devices, meta, cache, chunks, chunk_sems)
    copies += start_across(0, meta, cache, across, own, across_sems)
    copies += start_adapters(groups, meta, up, ups, up_sems)
    depth = write.shape[1]
    rows_out[:, :depth] = write[...]
    rows_out[:, depth:] = read[...]
    state_rows = cache.shape[3]
    for d in range(devices):
        target = lax.bitwise_xor(meta[MISC, ME], d)
        copy_conv(conv, meta[MISC, SLOT], target, width, chunks[d], state_rows)
    conv_across(devices // 2, width, 0, meta, conv, state_rows, across, own)
    for copy in copies:
        copy.wait()


def pack_across_kernel(lines, width, j, meta, cache, conv, across, own, sems):
    copies = start_across(j[0], meta, cache, across, own, sems)
    conv_across(lines, width, j[0], meta, conv, cache.shape[3], across, own)
    for copy in copies:
        copy.wait()


def pick_kernel(step, lines, j, meta, own, over, *rest):
    out_r, out_l, sems = rest[-3:]
    me = meta[MISC, ME]
    source = meta[OHOLDER, j[0]]
    same = source // 2 == me // 2
    mine = same & (source % 2 == me % 2)
    across = same & (source % 2 != me % 2)
    for k, (out, block) in enumerate(((out_r, right_block), (out_l, left_block))):
        place = block(meta, step, lines)

        @pl.when(mine)
        def _(k=k, out=out, place=place):
            pltpu.make_async_copy(own.at[place], out, sems.at[k]).start()

        @pl.when(across)
        def _(k=k, out=out, place=place):
            pltpu.make_async_copy(over.at[place], out, sems.at[k]).start()

        if step > 1:
            @pl.when(jnp.logical_not(same))
            def _(k=k, out=out):
                pltpu.make_async_copy(rest[k], out, sems.at[k]).start()

    for k, out in enumerate((out_r, out_l)):
        if step > 1:
            pltpu.make_async_copy(own.at[0], out, sems.at[k]).wait()
        else:
            @pl.when(same)
            def _(k=k, out=out):
                pltpu.make_async_copy(own.at[0], out, sems.at[k]).wait()


def right_block(meta, step, lines):
    return jnp.clip(lines + meta[MISC, ME] // 2 - step, 0, lines - 1)


def left_block(meta, step, lines):
    return jnp.clip(meta[MISC, ME] // 2 + step - lines, 0, lines - 1)


def pack_across(j, meta, cache, conv, devices, width):
    lines = devices // 2
    shape = chunk_shape(cache, conv, width)
    return pl.pallas_call(
        functools.partial(pack_across_kernel, lines, width),
        out_shape=tuple(jax.ShapeDtypeStruct((lines,) + shape, cache.dtype) for _ in range(2)),
        in_specs=smem(2) + pinned(1) + vmem(1),
        out_specs=tuple(vmem(2)),
        scratch_shapes=[pltpu.SemaphoreType.DMA((2,))],
        cost_estimate=cost(),
        compiler_params=params(),
        name="pack_across",
    )(j, meta, cache, conv)


def spread_steps(j, meta, packed, devices):
    lines = devices // 2
    send, own = packed
    shape = own.shape[1:]
    across = lax.ppermute(send, "dev", [(d, d ^ 1) for d in range(devices)])
    from_left = from_right = None
    after = yield across
    for step in range(1, lines):
        operands = [own, across]
        if step > 1:
            operands += [from_left, from_right]
        operands += after
        to_right, to_left = pl.pallas_call(
            functools.partial(pick_kernel, step, lines),
            in_specs=smem(2) + anywhere(len(operands)),
            out_specs=tuple(vmem(2)),
            out_shape=tuple(jax.ShapeDtypeStruct(shape, own.dtype) for _ in range(2)),
            scratch_shapes=[pltpu.SemaphoreType.DMA((2,))],
            cost_estimate=cost(),
            compiler_params=params(),
            name=f"pick_{step}",
        )(j, meta, *operands)
        from_left = lax.ppermute(
            to_right, "dev",
            [(2 * i + x, 2 * i + 2 + x) for i in range(step) for x in range(2)],
        )
        from_right = lax.ppermute(
            to_left, "dev",
            [(devices - 1 - (2 * i + x), devices - 3 - (2 * i + x))
             for i in range(step) for x in range(2)],
        )
        after = yield to_right
    yield own, across, from_left, from_right


def final_specs(shape):
    line = pl.BlockSpec((1,) + shape, lambda g, j, meta: (meta[MISC, ME] // 2, 0, 0))
    whole = pl.BlockSpec(shape, lambda g, j, meta: (0, 0))
    return [line, line, whole, whole]


def which_candidate(meta, source):
    me = meta[MISC, ME]
    same = source // 2 == me // 2
    mine = same & (source % 2 == me % 2)
    return jnp.where(mine, 0, jnp.where(same, 1, jnp.where(source // 2 < me // 2, 2, 3)))


def final_kernel(j, meta, own, across, from_left, from_right, out):
    which = which_candidate(meta, meta[OHOLDER, j[0]])
    picks = (own.at[0], across.at[0], from_left, from_right)
    for k, pick in enumerate(picks):
        @pl.when(which == k)
        def _(pick=pick):
            out[...] = pick[...]


def spread_rest(meta, cache, conv, devices, width, limit):
    shape = chunk_shape(cache, conv, width)

    def one(j, held):
        jj = j.reshape(1)
        packed = pack_across(jj, meta, cache, conv, devices, width)
        steps = spread_steps(jj, meta, packed, devices)
        next(steps)
        for _ in range(devices // 2):
            got = steps.send([])
        block = pl.pallas_call(
            final_kernel,
            grid_spec=pltpu.PrefetchScalarGridSpec(
                num_scalar_prefetch=2,
                grid=(1,),
                in_specs=final_specs(shape),
                out_specs=pl.BlockSpec(shape, lambda g, j, meta: (0, 0)),
            ),
            out_shape=jax.ShapeDtypeStruct(shape, cache.dtype),
            compiler_params=params(),
            name="final_pick",
        )(jj, meta, *got)
        return lax.dynamic_update_slice_in_dim(held, block[None], j - 1, 0)

    held = jnp.zeros((limit - 1,) + shape, cache.dtype)
    return lax.fori_loop(jnp.int32(1), meta[MISC, MOST], one, held)


def fetch_table(groups, meta, r, tables, out, sem):
    dist = meta[DIST, r]
    for k in range(groups):
        row = meta[ARANK, r] if k else meta[AINDEX, r]

        @pl.when(dist == k)
        def _(k=k, row=row):
            pltpu.make_async_copy(tables[k].at[row], out, sem).start()


def shrink_kernel(per_group, meta, hidden, table, *rest):
    out, picked, sems = rest[-3:]
    g = pl.program_id(0)
    each = out.shape[0]

    @pl.when(g == 0)
    def _():
        for r in range(per_group):
            pltpu.make_async_copy(
                table.at[meta[HOME, r], meta[ARANK, r]], picked.at[r], sems.at[r]
            ).start()

    for i in range(each):
        r = g * each + i
        pltpu.make_async_copy(table.at[0, 0], picked.at[r], sems.at[r]).wait()
    for i in range(each):
        part = lax.dot_general(
            hidden[i * T_REQ:(i + 1) * T_REQ, :], picked[g * each + i], NT,
            preferred_element_type=jnp.float32,
        )
        out[i] = part.T.astype(out.dtype)


def sum_kernel(parts, *rest):
    out = rest[-1]
    total = parts[0].astype(jnp.float32)
    for k in range(1, parts.shape[0]):
        total = total + parts[k].astype(jnp.float32)
    total = total.astype(out.dtype)
    for k in range(out.shape[0]):
        out[k] = total


def prep_kernel(per_group, rates, skips, steps, taps_in, bias, *rest):
    rows_out, column_out, channel = rest[-3:]
    heads, tokens = steps.shape
    length = tokens // per_group
    rate = jnp.zeros((heads, length), jnp.float32)
    place = lax.broadcasted_iota(jnp.int32, rate.shape, 0)
    for h in range(heads):
        rate = jnp.where(place == h, rates[h] * (-LOG2E), rate)
    step = [steps[:, r * length:(r + 1) * length] for r in range(per_group)]
    x = jnp.concatenate([part * rate for part in step], axis=0)
    high = x.astype(jnp.bfloat16)
    rest = x - high.astype(jnp.float32)
    middle = rest.astype(jnp.bfloat16)
    low = (rest - middle.astype(jnp.float32)).astype(jnp.bfloat16)
    s = lax.broadcasted_iota(jnp.int32, (length, length), 0)
    t = lax.broadcasted_iota(jnp.int32, (length, length), 1)
    ones = (s <= t).astype(jnp.float32).astype(jnp.bfloat16)
    total = jnp.dot(low, ones, preferred_element_type=jnp.float32)
    total = total + jnp.dot(middle, ones, preferred_element_type=jnp.float32)
    total = total + jnp.dot(high, ones, preferred_element_type=jnp.float32)
    shifted = total - jnp.log2(jnp.concatenate(step, axis=0))
    columns = shifted.T
    for r in range(per_group):
        rows_out[:heads, r * length:(r + 1) * length] = total[r * heads:(r + 1) * heads]
        rows_out[heads:, r * length:(r + 1) * length] = shifted[r * heads:(r + 1) * heads]
        column_out[r] = columns[:, r * heads:(r + 1) * heads]
    taps, width = taps_in.shape
    head_of = lax.broadcasted_iota(jnp.int32, (1, width), 1) // (width // heads)
    skip = jnp.zeros((1, width), jnp.float32)
    for h in range(heads):
        skip = jnp.where(head_of == h, skips[h], skip)
    channel[:taps] = taps_in[...]
    channel[taps:taps + 1] = bias[...]
    channel[taps + 1:taps + 2] = skip


def mix_kernel(
    groups, taps, begin, steps, direct, size, meta, base, shrunk, channel, rows_decay, column,
    rows_in, *rest
):
    tables, chunks = rest[:groups], rest[groups:]
    out, final, extended, scores, carried, weighted, ups, curs, table_sems, chunk_sems = (
        rest[-10:]
    )
    g = pl.program_id(0)
    position = begin + g
    r = meta[POS_REQ, position]
    length, width = base.shape
    half = length // 2
    heads = width // size
    depth = curs.shape[2]
    few = taps - 1
    parts = width // 128
    f32, bf16 = jnp.float32, jnp.bfloat16

    def fetch_chunk(source, i):
        pltpu.make_async_copy(source, curs.at[i], chunk_sems.at[i]).start()

    @pl.when(g == 0)
    def _():
        for i in range(steps):
            @pl.when(meta[POS_VALID, begin + i] > 0)
            def _(i=i):
                request = meta[POS_REQ, begin + i]
                fetch_table(groups, meta, request, tables, ups.at[i], table_sems.at[i])
                if i < direct:
                    fetch_chunk(chunks[i], i)
                elif i > direct:
                    fetch_chunk(chunks[direct + 4].at[i - direct - 1], i)
                else:
                    line = meta[MISC, ME] // 2
                    own, across, from_left, from_right = chunks[direct:direct + 4]
                    candidates = [own.at[line], across.at[line], from_left, from_right]
                    which = which_candidate(meta, meta[OHOLDER, 0])
                    for k, candidate in enumerate(candidates):
                        @pl.when(which == k)
                        def _(candidate=candidate):
                            fetch_chunk(candidate, direct)

    @pl.when(meta[POS_VALID, position] > 0)
    def _():
        present = meta[PRESENT, r] > 0
        write, read = rows_in[:, :depth], rows_in[:, depth:]
        all_scores = lax.dot_general(write, read, NT, preferred_element_type=f32)
        s = lax.broadcasted_iota(jnp.int32, (half, half), 0)
        t = lax.broadcasted_iota(jnp.int32, (half, half), 1)
        scores[:half] = jnp.where(s <= t, all_scores[:half, :half], 0.0)
        scores[half:] = jnp.where(s <= t, all_scores[half:, half:], 0.0)
        late_scores = all_scores[:half, half:].astype(bf16)

        to_here, from_here = rows_decay[:heads, :], rows_decay[heads:, :]
        end = jnp.broadcast_to(to_here[:, length - 1:length], (heads, length))
        middle = jnp.broadcast_to(to_here[:, half - 1:half], (heads, half))
        grown = jnp.exp2(to_here)
        to_end = jnp.exp2(end - from_here)
        to_middle = jnp.exp2(middle - from_here[:, :half])
        past_middle = jnp.exp2(to_here[:, half:] - middle)
        kept = jnp.exp2(end[:, :depth])

        pltpu.make_async_copy(tables[0].at[0], ups.at[g], table_sems.at[g]).wait()
        extended[8:, :] = base[...].astype(f32) + lax.dot_general(
            shrunk[0], ups[g], TN, preferred_element_type=f32
        )
        pltpu.make_async_copy(curs.at[g], curs.at[g], chunk_sems.at[g]).wait()
        before = jnp.where(present, curs[g, width:, :].astype(f32), 0.0)
        for k in range(few):
            for part in range(parts):
                extended[8 - few + k:9 - few + k, part * 128:(part + 1) * 128] = (
                    before[k * parts + part:k * parts + part + 1, :]
                )
        from_state = lax.dot_general(curs[g, :width, :], read, NT, preferred_element_type=f32)
        carried[...] = jnp.where(present, from_state, 0.0)

        corner = jnp.zeros((half, half), bf16)
        for pair in range(heads // 2):
            lo, hi = pair * 2 * size, (pair + 1) * 2 * size
            v = channel[taps:taps + 1, lo:hi]
            for k in range(taps):
                first = 8 - few + k
                v = v + channel[k:k + 1, lo:hi] * extended[first:first + length, lo:hi]
            activated = v * (0.5 + 0.5 * jnp.tanh(0.5 * v))
            act = activated.astype(bf16).T
            wide = act.astype(f32)
            sums, early = [], []
            for i in range(2):
                h = 2 * pair + i
                a = act[i * size:(i + 1) * size, :]
                a32 = wide[i * size:(i + 1) * size, :]
                ds = jnp.broadcast_to(column[0, :, h:h + 1], (length, half))
                dt0, dt1 = to_here[h:h + 1, :half], to_here[h:h + 1, half:]
                m0 = jnp.exp2(jnp.minimum(dt0 - ds[:half], 126.0)) * scores[:half]
                m1 = jnp.exp2(jnp.minimum(dt1 - ds[half:], 126.0)) * scores[half:]
                mixing = jnp.concatenate(
                    [
                        jnp.concatenate([m0.astype(bf16), corner], axis=1),
                        jnp.concatenate([corner, m1.astype(bf16)], axis=1),
                    ],
                    axis=0,
                )
                total = jnp.dot(a, mixing, preferred_element_type=f32)
                sums.append(total + carried[h * size:(h + 1) * size, :] * grown[h:h + 1, :])
                weighted[h * size:(h + 1) * size, :] = (a32 * to_end[h:h + 1, :]).astype(bf16)
                early.append((a32[:, :half] * to_middle[h:h + 1, :]).astype(bf16))
            passed = jnp.dot(
                jnp.concatenate(early, axis=0), late_scores, preferred_element_type=f32
            )
            for i in range(2):
                h = 2 * pair + i
                late = passed[i * size:(i + 1) * size, :] * past_middle[h:h + 1, :]
                sums[i] = jnp.concatenate([sums[i][:, :half], sums[i][:, half:] + late], axis=1)
            skipped = channel[taps + 1:taps + 2, lo:hi] * activated
            out[:, lo:hi] = (jnp.concatenate(sums, axis=0).T + skipped).astype(out.dtype)
        fresh = jnp.dot(weighted[...], write, preferred_element_type=f32)
        for h in range(heads):
            rows = slice(h * size, (h + 1) * size)
            old = curs[g, rows, :].astype(f32) * kept[h:h + 1, :]
            old = jnp.where(present, old, 0.0)
            final[0, rows, :] = (fresh[rows, :] + old).astype(final.dtype)


def chunk_shape(cache, conv, width):
    conv_rows = conv.shape[0] * (width // 128)
    return (cache.shape[3] + -(-conv_rows // 16) * 16, cache.shape[4])


def body(
    hidden, base_in_projection, state_input_matrix, state_output_matrix, head_step_size,
    head_decay_rate, head_skip_scale, convolution_weight, convolution_bias, adapter_down_weight,
    adapter_up_weight, adapter_home_group, adapter_group_index, state_space_cache,
    convolution_cache, prefix_holder_device, prefix_cache_slot, prefix_block_count,
):
    groups, devices = lax.axis_size("group"), lax.axis_size("dev")
    tokens, width = base_in_projection.shape
    per_group = tokens // T_REQ
    assert per_group == devices and devices & (devices - 1) == 0 == groups & (groups - 1)
    heads = head_step_size.shape[0]
    size, depth = state_space_cache.shape[2:]
    rank = adapter_down_weight.shape[1]
    taps = convolution_weight.shape[0]
    bf16, f32 = jnp.bfloat16, jnp.float32
    limit = per_group // 2
    lines = devices // 2

    cache = state_space_cache.reshape(
        state_space_cache.shape[0], lines, 2, heads * size, depth
    )
    conv = convolution_cache.transpose(1, 0, 2)
    shape = chunk_shape(cache, conv, width)
    picks = [
        jax.ShapeDtypeStruct((ACAP,) + adapter_down_weight.shape[1:], bf16)
        for _ in range(groups - 1)
    ]
    packed = pl.pallas_call(
        functools.partial(pack_kernel, groups, devices, per_group, width),
        out_shape=(
            jax.ShapeDtypeStruct(META_SHAPE, jnp.int32),
            jax.ShapeDtypeStruct((state_input_matrix.shape[0], 2 * depth), bf16),
            jax.ShapeDtypeStruct((groups, ACAP) + adapter_down_weight.shape[1:], bf16),
            *picks,
            *[jax.ShapeDtypeStruct(shape, bf16) for _ in range(devices)],
            *[jax.ShapeDtypeStruct((lines,) + shape, bf16) for _ in range(2)],
        ),
        in_specs=smem(5) + pinned(3) + vmem(3),
        out_specs=tuple(smem(1) + vmem(2 + len(picks) + devices + 2)),
        scratch_shapes=[
            pltpu.SemaphoreType.DMA((groups * ACAP,)),
            pltpu.SemaphoreType.DMA((groups * ACAP,)),
            pltpu.SemaphoreType.DMA((devices,)),
            pltpu.SemaphoreType.DMA((2,)),
        ],
        cost_estimate=cost(),
        compiler_params=params(),
        name="pack",
    )(
        adapter_home_group.reshape(-1), adapter_group_index, prefix_holder_device.reshape(-1),
        prefix_cache_slot, prefix_block_count, adapter_down_weight, adapter_up_weight, cache,
        state_input_matrix, state_output_matrix, conv,
    )
    meta, rows_mine, packed = packed[0], packed[1], packed[2:]
    down_got = lax.all_to_all(packed[0], "group", split_axis=0, concat_axis=0, tiled=True)
    chunks = packed[groups:-2]
    rows_all = lax.all_gather(rows_mine, "dev", axis=0, tiled=True)
    zero = jnp.zeros((1,), jnp.int32)
    got = [chunks[0]] + [
        lax.ppermute(chunks[d], "dev", [(s, s ^ d) for s in range(devices)])
        for d in range(1, devices)
    ]

    spread_others = spread_rest(meta, cache, conv, devices, width, limit)

    up_send, _ = lax.optimization_barrier((packed[1:groups], got[2]))
    up_got = swap(up_send, groups)

    rows_decay, column_decay, channel = pl.pallas_call(
        functools.partial(prep_kernel, per_group),
        out_shape=(
            jax.ShapeDtypeStruct((2 * heads, tokens), f32),
            jax.ShapeDtypeStruct((per_group, T_REQ, heads), f32),
            jax.ShapeDtypeStruct((8, width), f32),
        ),
        in_specs=smem(2) + vmem(3) + anywhere(1),
        out_specs=tuple(pl.BlockSpec(memory_space=pltpu.VMEM) for _ in range(3)),
        cost_estimate=cost(),
        compiler_params=params(),
        name="prep",
    )(
        head_decay_rate, head_skip_scale, head_step_size, convolution_weight,
        convolution_bias.reshape(1, width), meta,
    )

    each = per_group // 2
    early = got[2:lines + 2]
    partial_down = pl.pallas_call(
        functools.partial(shrink_kernel, per_group),
        grid_spec=pltpu.PrefetchScalarGridSpec(
            num_scalar_prefetch=1,
            grid=(per_group // each,),
            in_specs=[pl.BlockSpec((each * T_REQ, hidden.shape[1]), lambda g, meta: (g, 0))]
            + anywhere(3 + len(early)),
            out_specs=pl.BlockSpec((each, rank, T_REQ), lambda g, meta: (g, 0, 0)),
            scratch_shapes=[
                pltpu.VMEM((per_group,) + adapter_down_weight.shape[1:], bf16),
                pltpu.SemaphoreType.DMA((per_group,)),
            ],
        ),
        out_shape=jax.ShapeDtypeStruct((per_group, rank, T_REQ), bf16),
        cost_estimate=cost(),
        compiler_params=params(),
        name="shrink",
    )(meta, hidden, down_got, channel, spread_others, *early)

    parts = lax.all_to_all(partial_down, "dev", split_axis=0, concat_axis=0, tiled=True)
    summed = pl.pallas_call(
        sum_kernel,
        out_shape=jax.ShapeDtypeStruct((devices, 1, rank, T_REQ), bf16),
        in_specs=vmem(1) + anywhere(1),
        out_specs=vmem(1)[0],
        cost_estimate=cost(),
        compiler_params=params(),
        name="sum_parts",
    )(parts.reshape(devices, 1, rank, T_REQ), up_got[groups // 2 - 1])
    shrunk = lax.all_to_all(summed, "dev", split_axis=0, concat_axis=0, tiled=True)
    shrunk = shrunk.reshape(per_group, rank, T_REQ)

    befores = [[partial_down], [summed], [rows_all, up_got[-1]]]
    spread = spread_steps(zero, meta, packed[-2:], devices)
    next(spread)
    for step in range(1, lines):
        sent = spread.send(befores.pop(0) if befores else [])
    spread = spread.send([])

    outs = None
    for begin, steps in ((0, lines), (lines, devices - lines + limit)):
        if begin == 0:
            chunks, after = got[:lines], [sent, got[lines + 2], got[lines + 3]]
        else:
            chunks, after = [*got[lines:], *spread, spread_others], []

        def request(g, meta, begin=begin):
            return meta[POS_REQ, begin + g]

        in_specs = [
            pl.BlockSpec((T_REQ, width), lambda g, meta: (request(g, meta), 0)),
            pl.BlockSpec((1, rank, T_REQ), lambda g, meta: (request(g, meta), 0, 0)),
            pl.BlockSpec((8, width), lambda g, meta: (0, 0)),
            pl.BlockSpec((2 * heads, T_REQ), lambda g, meta: (0, request(g, meta))),
            pl.BlockSpec((1, T_REQ, heads), lambda g, meta: (request(g, meta), 0, 0)),
            pl.BlockSpec((T_REQ, 2 * depth), lambda g, meta: (request(g, meta), 0)),
        ] + anywhere(groups + len(chunks) + len(after))
        operands = [
            meta, base_in_projection, shrunk, channel, rows_decay, column_decay, rows_all,
            adapter_up_weight, *up_got, *chunks, *after,
        ]
        aliases = {}
        if outs is not None:
            aliases = {len(operands): 0, len(operands) + 1: 1}
            operands += list(outs)
            in_specs += anywhere(2)
        outs = pl.pallas_call(
            functools.partial(mix_kernel, groups, taps, begin, steps, lines, size),
            grid_spec=pltpu.PrefetchScalarGridSpec(
                num_scalar_prefetch=1,
                grid=(steps,),
                in_specs=in_specs,
                out_specs=(
                    pl.BlockSpec((T_REQ, width), lambda g, meta: (request(g, meta), 0)),
                    pl.BlockSpec(
                        (1, heads * size, depth), lambda g, meta: (request(g, meta), 0, 0)
                    ),
                ),
                scratch_shapes=[
                    pltpu.VMEM((T_REQ + 8, width), f32),
                    pltpu.VMEM((T_REQ, T_REQ // 2), f32),
                    pltpu.VMEM((width, T_REQ), f32),
                    pltpu.VMEM((width, T_REQ), bf16),
                    pltpu.VMEM((steps,) + adapter_up_weight.shape[1:], bf16),
                    pltpu.VMEM((steps,) + shape, bf16),
                    pltpu.SemaphoreType.DMA((steps,)),
                    pltpu.SemaphoreType.DMA((steps,)),
                ],
            ),
            out_shape=(
                jax.ShapeDtypeStruct((tokens, width), bf16),
                jax.ShapeDtypeStruct((per_group, heads * size, depth), bf16),
            ),
            input_output_aliases=aliases,
            cost_estimate=cost(),
            compiler_params=params(),
            name=f"mix_{begin}",
        )(*operands)
    return outs[0], outs[1].reshape(per_group, heads, size, depth)


def solution(mesh):
    placed = (
        P("group", "dev"),
        P("group", "dev"),
        P(("group", "dev"), None),
        P(("group", "dev"), None),
        P("dev", "group"),
        P("dev"),
        P("dev"),
        P(None, "dev"),
        P("dev"),
        P("group", None, "dev"),
        P("group", None, "dev"),
        P(),
        P(),
        P(("group", "dev"), None, None, None),
        P(("group", "dev"), None, None),
        P(),
        P(),
        P(),
    )
    return jax.shard_map(
        body,
        mesh=mesh,
        in_specs=placed,
        out_specs=(P("group", "dev"), P("group", "dev", None, None)),
        check_vma=False,
    )
```

```python
import functools
import math

import jax
import jax.numpy as jnp
from jax import lax
from jax.experimental import pallas as pl
from jax.experimental.pallas import tpu as pltpu
from jax.sharding import PartitionSpec as P

T_REQ = 256
CAP = 2
ACAP = 4
LOG2E = math.log2(math.e)
NT = (((1,), (1,)), ((), ()))
TN = (((0,), (0,)), ((), ()))
VMEM_LIMIT = 63 * 1024 * 1024

HOME, DIST, ARANK, AINDEX, PRESENT, POS_REQ, POS_VALID, OSLOT, OHOLDER, MISC, SEND = range(11)
MOST, ME, SLOT, SPREAD = range(4)
META_SHAPE = (16, 64)


def cost():
    return pl.CostEstimate(flops=0, bytes_accessed=1 << 16, transcendentals=0)


def params():
    return pltpu.CompilerParams(vmem_limit_bytes=VMEM_LIMIT)


def smem(count):
    return [pl.BlockSpec(memory_space=pltpu.SMEM) for _ in range(count)]


def vmem(count):
    return [pl.BlockSpec(memory_space=pltpu.VMEM) for _ in range(count)]


def pinned(count):
    return [pl.BlockSpec(memory_space=pltpu.HBM) for _ in range(count)]


def anywhere(count):
    return [pl.BlockSpec(memory_space=pl.ANY) for _ in range(count)]


def as_int(flag):
    return flag.astype(jnp.int32)


def ranks_of(labels):
    ranks = []
    for q, label in enumerate(labels):
        total = jnp.int32(0)
        for other in labels[:q]:
            total = total + as_int(other == label)
        ranks.append(total)
    return ranks


def near_distances(devices):
    return devices - max(devices // 4, 1)


def plan(groups, devices, per_group, home, index, holder, slot, blocks, meta):
    my_group = lax.axis_index("group")
    me = lax.axis_index("dev")
    first = my_group * per_group
    limit = per_group // 2
    for j in range(limit):
        meta[POS_REQ, devices + j] = jnp.int32(-1)
        meta[POS_VALID, devices + j] = jnp.int32(0)
        meta[OSLOT, j] = jnp.int32(0)
        meta[OHOLDER, j] = jnp.int32(0)

    homes = [home[first + q] for q in range(per_group)]
    for q, rank in enumerate(ranks_of(homes)):
        meta[HOME, q] = homes[q]
        meta[DIST, q] = lax.bitwise_xor(homes[q], my_group)
        meta[ARANK, q] = rank
        meta[AINDEX, q] = index[first + q]
        meta[PRESENT, q] = as_int(blocks[first + q] > 0)
    for k in range(groups):
        theirs = lax.bitwise_xor(my_group, k) * per_group
        seen = jnp.int32(0)
        chosen = [jnp.int32(0) for _ in range(ACAP)]
        for q in range(per_group):
            hit = home[theirs + q] == my_group
            value = index[theirs + q]
            for c in range(ACAP):
                chosen[c] = jnp.where(hit & (seen == c), value, chosen[c])
            seen = seen + as_int(hit)
        for c in range(ACAP):
            meta[SEND, k * ACAP + c] = chosen[c]

    holders = [holder[first + q] for q in range(per_group)]
    ranks = ranks_of(holders)
    count = jnp.int32(0)
    my_slot = jnp.int32(0)
    for q in range(per_group):
        my_slot = jnp.where((holders[q] == me) & (ranks[q] == 0), slot[first + q], my_slot)

        @pl.when(ranks[q] > 0)
        def _():
            meta[POS_REQ, devices + count] = jnp.int32(q)
            meta[POS_VALID, devices + count] = jnp.int32(1)
            meta[OSLOT, count] = slot[first + q]
            meta[OHOLDER, count] = holders[q]

        count = count + as_int(ranks[q] > 0)
    spread = meta[POS_REQ, devices]
    requests = []
    for d in range(devices):
        source = lax.bitwise_xor(me, d)
        request = jnp.int32(-1)
        for q in range(per_group):
            request = jnp.where((holders[q] == source) & (ranks[q] == 0), q, request)
        meta[POS_VALID, d] = as_int(request >= 0)
        requests.append(request)
    requests += [meta[POS_REQ, devices + j] for j in range(limit)]
    for begin, end in ((0, devices // 2), (devices // 2, devices)):
        last = jnp.int32(-1)
        filled = []
        for p in range(begin, end):
            last = jnp.where(requests[p] >= 0, requests[p], last)
            filled.append(last)
        following = jnp.maximum(spread, 0)
        for p in reversed(range(begin, end)):
            following = jnp.where(filled[p - begin] >= 0, filled[p - begin], following)
            meta[POS_REQ, p] = following
    meta[MISC, SPREAD] = as_int(count > 0)
    meta[POS_VALID, devices] = jnp.int32(1)
    for j in range(limit):
        meta[POS_REQ, devices + j] = jnp.where(
            j < count, requests[devices + j],
            jnp.where(count > 0, meta[POS_REQ, devices + max(j - 1, 0)], requests[0]),
        )
    most = jnp.int32(0)
    for g in range(groups):
        labels = [holder[g * per_group + q] for q in range(per_group)]
        total = jnp.int32(0)
        for rank in ranks_of(labels):
            total = total + as_int(rank > 0)
        most = jnp.maximum(most, total)
    meta[MISC, MOST] = most
    meta[MISC, ME] = me
    meta[MISC, SLOT] = my_slot


def start_adapters(groups, meta, table, outs, sems):
    copies = []
    for k in reversed(range(groups) if len(outs) == 1 else range(1, groups)):
        for c in range(ACAP):
            chosen = meta[SEND, k * ACAP + c]
            if len(outs) == 1:
                out = outs[0].at[lax.bitwise_xor(lax.axis_index("group"), k), c]
            else:
                out = outs[k - 1].at[c]
            copy = pltpu.make_async_copy(table.at[chosen], out, sems.at[k * ACAP + c])
            copy.start()
            copies.append(copy)
    return copies


def swap(packed, groups):
    return [
        lax.ppermute(packed[k - 1], "group", [(g, g ^ k) for g in range(groups)])
        for k in range(1, groups)
    ]


def copy_conv(conv, slot, target, width, out, at):
    parts = width // 128
    begin = pl.multiple_of(target * width, 128)
    for k in range(conv.shape[0]):
        rows = conv[k, :, pl.ds(begin, width)]
        row = rows[:1, :]
        for c in range(1, conv.shape[1]):
            row = jnp.where(slot == c, rows[c:c + 1, :], row)
        for part in range(parts):
            place = at + k * parts + part
            out[place:place + 1, :] = row[:, part * 128:(part + 1) * 128]


def start_state(devices, meta, cache, outs, sems):
    copies = []
    for d in reversed(range(devices)):
        target = lax.bitwise_xor(meta[MISC, ME], d)
        copy = pltpu.make_async_copy(
            cache.at[meta[MISC, SLOT], target // 2, target % 2],
            outs[d].at[pl.ds(0, cache.shape[3])], sems.at[d],
        )
        copy.start()
        copies.append(copy)
    return copies


def start_across(j, meta, cache, across, own, sems):
    x = meta[MISC, ME] % 2
    copies = []
    for k, (out, place) in enumerate(((across, 1 - x), (own, x))):
        copy = pltpu.make_async_copy(
            cache.at[meta[OSLOT, j], :, place], out.at[:, pl.ds(0, cache.shape[3])], sems.at[k]
        )
        copy.start()
        copies.append(copy)
    return copies


def conv_across(lines, width, j, meta, conv, state_rows, across, own):
    x = meta[MISC, ME] % 2
    for out, place in ((across, 1 - x), (own, x)):
        for m in range(lines):
            copy_conv(conv, meta[OSLOT, j], 2 * m + place, width, out.at[m], state_rows)


def pack_kernel(
    groups, devices, per_group, width, home, index, holder, slot, blocks, down, up, cache, write,
    read, conv, meta, rows_out, *rest
):
    downs, rest = rest[:1], rest[1:]
    ups, rest = rest[:groups - 1], rest[groups - 1:]
    chunks, (across, own, down_sems, up_sems, chunk_sems, across_sems) = (
        rest[:devices], rest[devices:]
    )
    plan(groups, devices, per_group, home, index, holder, slot, blocks, meta)
    copies = start_adapters(groups, meta, down, downs, down_sems)
    copies += start_state(devices, meta, cache, chunks, chunk_sems)
    copies += start_across(0, meta, cache, across, own, across_sems)
    copies += start_adapters(groups, meta, up, ups, up_sems)
    depth = write.shape[1]
    rows_out[:, :depth] = write[...]
    rows_out[:, depth:] = read[...]
    state_rows = cache.shape[3]
    for d in range(devices):
        target = lax.bitwise_xor(meta[MISC, ME], d)
        copy_conv(conv, meta[MISC, SLOT], target, width, chunks[d], state_rows)
    conv_across(devices // 2, width, 0, meta, conv, state_rows, across, own)
    for copy in copies:
        copy.wait()


def pack_across_kernel(lines, width, j, meta, cache, conv, across, own, sems):
    copies = start_across(j[0], meta, cache, across, own, sems)
    conv_across(lines, width, j[0], meta, conv, cache.shape[3], across, own)
    for copy in copies:
        copy.wait()


def pick_kernel(step, lines, j, meta, own, over, *rest):
    out_r, out_l, sems = rest[-3:]
    me = meta[MISC, ME]
    source = meta[OHOLDER, j[0]]
    same = source // 2 == me // 2
    mine = same & (source % 2 == me % 2)
    across = same & (source % 2 != me % 2)
    for k, (out, block) in enumerate(((out_r, right_block), (out_l, left_block))):
        place = block(meta, step, lines)

        @pl.when(mine)
        def _(k=k, out=out, place=place):
            pltpu.make_async_copy(own.at[place], out, sems.at[k]).start()

        @pl.when(across)
        def _(k=k, out=out, place=place):
            pltpu.make_async_copy(over.at[place], out, sems.at[k]).start()

        if step > 1:
            @pl.when(jnp.logical_not(same))
            def _(k=k, out=out):
                pltpu.make_async_copy(rest[k], out, sems.at[k]).start()

    for k, out in enumerate((out_r, out_l)):
        if step > 1:
            pltpu.make_async_copy(own.at[0], out, sems.at[k]).wait()
        else:
            @pl.when(same)
            def _(k=k, out=out):
                pltpu.make_async_copy(own.at[0], out, sems.at[k]).wait()


def right_block(meta, step, lines):
    return jnp.clip(lines + meta[MISC, ME] // 2 - step, 0, lines - 1)


def left_block(meta, step, lines):
    return jnp.clip(meta[MISC, ME] // 2 + step - lines, 0, lines - 1)


def pack_across(j, meta, cache, conv, devices, width):
    lines = devices // 2
    shape = chunk_shape(cache, conv, width)
    return pl.pallas_call(
        functools.partial(pack_across_kernel, lines, width),
        out_shape=tuple(jax.ShapeDtypeStruct((lines,) + shape, cache.dtype) for _ in range(2)),
        in_specs=smem(2) + pinned(1) + vmem(1),
        out_specs=tuple(vmem(2)),
        scratch_shapes=[pltpu.SemaphoreType.DMA((2,))],
        cost_estimate=cost(),
        compiler_params=params(),
        name="pack_across",
    )(j, meta, cache, conv)


def spread_steps(j, meta, packed, devices):
    lines = devices // 2
    send, own = packed
    shape = own.shape[1:]
    across = lax.ppermute(send, "dev", [(d, d ^ 1) for d in range(devices)])
    from_left = from_right = None
    after = yield across
    for step in range(1, lines):
        operands = [own, across]
        if step > 1:
            operands += [from_left, from_right]
        operands += after
        to_right, to_left = pl.pallas_call(
            functools.partial(pick_kernel, step, lines),
            in_specs=smem(2) + anywhere(len(operands)),
            out_specs=tuple(vmem(2)),
            out_shape=tuple(jax.ShapeDtypeStruct(shape, own.dtype) for _ in range(2)),
            scratch_shapes=[pltpu.SemaphoreType.DMA((2,))],
            cost_estimate=cost(),
            compiler_params=params(),
            name=f"pick_{step}",
        )(j, meta, *operands)
        from_left = lax.ppermute(
            to_right, "dev",
            [(2 * i + x, 2 * i + 2 + x) for i in range(step) for x in range(2)],
        )
        from_right = lax.ppermute(
            to_left, "dev",
            [(devices - 1 - (2 * i + x), devices - 3 - (2 * i + x))
             for i in range(step) for x in range(2)],
        )
        after = yield to_right
    yield own, across, from_left, from_right


def final_specs(shape):
    line = pl.BlockSpec((1,) + shape, lambda g, j, meta: (meta[MISC, ME] // 2, 0, 0))
    whole = pl.BlockSpec(shape, lambda g, j, meta: (0, 0))
    return [line, line, whole, whole]


def which_candidate(meta, source):
    me = meta[MISC, ME]
    same = source // 2 == me // 2
    mine = same & (source % 2 == me % 2)
    return jnp.where(mine, 0, jnp.where(same, 1, jnp.where(source // 2 < me // 2, 2, 3)))


def final_kernel(j, meta, own, across, from_left, from_right, out):
    which = which_candidate(meta, meta[OHOLDER, j[0]])
    picks = (own.at[0], across.at[0], from_left, from_right)
    for k, pick in enumerate(picks):
        @pl.when(which == k)
        def _(pick=pick):
            out[...] = pick[...]


def spread_rest(meta, cache, conv, devices, width, limit):
    shape = chunk_shape(cache, conv, width)

    def one(j, held):
        jj = j.reshape(1)
        packed = pack_across(jj, meta, cache, conv, devices, width)
        steps = spread_steps(jj, meta, packed, devices)
        next(steps)
        for _ in range(devices // 2):
            got = steps.send([])
        block = pl.pallas_call(
            final_kernel,
            grid_spec=pltpu.PrefetchScalarGridSpec(
                num_scalar_prefetch=2,
                grid=(1,),
                in_specs=final_specs(shape),
                out_specs=pl.BlockSpec(shape, lambda g, j, meta: (0, 0)),
            ),
            out_shape=jax.ShapeDtypeStruct(shape, cache.dtype),
            compiler_params=params(),
            name="final_pick",
        )(jj, meta, *got)
        return lax.dynamic_update_slice_in_dim(held, block[None], j - 1, 0)

    held = jnp.zeros((limit - 1,) + shape, cache.dtype)
    return lax.fori_loop(jnp.int32(1), meta[MISC, MOST], one, held)


def fetch_table(groups, meta, r, tables, out, sem):
    dist = meta[DIST, r]
    for k in range(groups):
        row = meta[ARANK, r] if k else meta[AINDEX, r]

        @pl.when(dist == k)
        def _(k=k, row=row):
            pltpu.make_async_copy(tables[k].at[row], out, sem).start()


def shrink_kernel(per_group, meta, hidden, table, *rest):
    out, picked, sems = rest[-3:]
    g = pl.program_id(0)
    each = out.shape[0]

    @pl.when(g == 0)
    def _():
        for r in range(per_group):
            pltpu.make_async_copy(
                table.at[meta[HOME, r], meta[ARANK, r]], picked.at[r], sems.at[r]
            ).start()

    for i in range(each):
        r = g * each + i
        pltpu.make_async_copy(table.at[0, 0], picked.at[r], sems.at[r]).wait()
    for i in range(each):
        part = lax.dot_general(
            hidden[i * T_REQ:(i + 1) * T_REQ, :], picked[g * each + i], NT,
            preferred_element_type=jnp.float32,
        )
        out[i] = part.T.astype(out.dtype)


def sum_kernel(parts, *rest):
    out = rest[-1]
    total = parts[0].astype(jnp.float32)
    for k in range(1, parts.shape[0]):
        total = total + parts[k].astype(jnp.float32)
    total = total.astype(out.dtype)
    for k in range(out.shape[0]):
        out[k] = total


def prep_kernel(per_group, rates, skips, steps, taps_in, bias, *rest):
    rows_out, column_out, channel = rest[-3:]
    heads, tokens = steps.shape
    length = tokens // per_group
    rate = jnp.zeros((heads, length), jnp.float32)
    place = lax.broadcasted_iota(jnp.int32, rate.shape, 0)
    for h in range(heads):
        rate = jnp.where(place == h, rates[h] * (-LOG2E), rate)
    step = [steps[:, r * length:(r + 1) * length] for r in range(per_group)]
    x = jnp.concatenate([part * rate for part in step], axis=0)
    high = x.astype(jnp.bfloat16)
    rest = x - high.astype(jnp.float32)
    middle = rest.astype(jnp.bfloat16)
    low = (rest - middle.astype(jnp.float32)).astype(jnp.bfloat16)
    s = lax.broadcasted_iota(jnp.int32, (length, length), 0)
    t = lax.broadcasted_iota(jnp.int32, (length, length), 1)
    ones = (s <= t).astype(jnp.float32).astype(jnp.bfloat16)
    total = jnp.dot(low, ones, preferred_element_type=jnp.float32)
    total = total + jnp.dot(middle, ones, preferred_element_type=jnp.float32)
    total = total + jnp.dot(high, ones, preferred_element_type=jnp.float32)
    shifted = total - jnp.log2(jnp.concatenate(step, axis=0))
    columns = shifted.T
    for r in range(per_group):
        rows_out[:heads, r * length:(r + 1) * length] = total[r * heads:(r + 1) * heads]
        rows_out[heads:, r * length:(r + 1) * length] = shifted[r * heads:(r + 1) * heads]
        column_out[r] = columns[:, r * heads:(r + 1) * heads]
    taps, width = taps_in.shape
    head_of = lax.broadcasted_iota(jnp.int32, (1, width), 1) // (width // heads)
    skip = jnp.zeros((1, width), jnp.float32)
    for h in range(heads):
        skip = jnp.where(head_of == h, skips[h], skip)
    channel[:taps] = taps_in[...]
    channel[taps:taps + 1] = bias[...]
    channel[taps + 1:taps + 2] = skip


def mix_kernel(
    groups, taps, begin, steps, direct, size, meta, base, shrunk, channel, rows_decay, column,
    rows_in, *rest
):
    tables, chunks = rest[:groups], rest[groups:]
    out, final, done, extended, scores, carried, weighted, ups, curs, table_sems, chunk_sems = (
        rest[-11:]
    )
    g = pl.program_id(0)
    position = begin + g
    r = meta[POS_REQ, position]
    length, width = base.shape
    half = length // 2
    heads = width // size
    depth = curs.shape[2]
    few = taps - 1
    parts = width // 128
    f32, bf16 = jnp.float32, jnp.bfloat16

    done[...] = jnp.zeros_like(done)

    def fetch_chunk(source, i):
        pltpu.make_async_copy(source, curs.at[i], chunk_sems.at[i]).start()

    @pl.when(g == 0)
    def _():
        for i in range(steps):
            @pl.when(meta[POS_VALID, begin + i] > 0)
            def _(i=i):
                request = meta[POS_REQ, begin + i]
                fetch_table(groups, meta, request, tables, ups.at[i], table_sems.at[i])
                if i < direct:
                    fetch_chunk(chunks[i], i)
                elif i > direct:
                    fetch_chunk(chunks[direct + 4].at[i - direct - 1], i)
                else:
                    line = meta[MISC, ME] // 2
                    own, across, from_left, from_right = chunks[direct:direct + 4]
                    candidates = [
                        own.at[line], across.at[line], from_left, from_right,
                        chunks[direct + 5],
                    ]
                    which = jnp.where(
                        meta[MISC, SPREAD] > 0, which_candidate(meta, meta[OHOLDER, 0]), 4
                    )
                    for k, candidate in enumerate(candidates):
                        @pl.when(which == k)
                        def _(candidate=candidate):
                            fetch_chunk(candidate, direct)

    @pl.when(meta[POS_VALID, position] > 0)
    def _():
        present = meta[PRESENT, r] > 0
        write, read = rows_in[:, :depth], rows_in[:, depth:]
        all_scores = lax.dot_general(write, read, NT, preferred_element_type=f32)
        s = lax.broadcasted_iota(jnp.int32, (half, half), 0)
        t = lax.broadcasted_iota(jnp.int32, (half, half), 1)
        scores[:half] = jnp.where(s <= t, all_scores[:half, :half], 0.0)
        scores[half:] = jnp.where(s <= t, all_scores[half:, half:], 0.0)
        late_scores = all_scores[:half, half:].astype(bf16)

        to_here, from_here = rows_decay[:heads, :], rows_decay[heads:, :]
        end = jnp.broadcast_to(to_here[:, length - 1:length], (heads, length))
        middle = jnp.broadcast_to(to_here[:, half - 1:half], (heads, half))
        grown = jnp.exp2(to_here)
        to_end = jnp.exp2(end - from_here)
        to_middle = jnp.exp2(middle - from_here[:, :half])
        past_middle = jnp.exp2(to_here[:, half:] - middle)
        kept = jnp.exp2(end[:, :depth])

        pltpu.make_async_copy(tables[0].at[0], ups.at[g], table_sems.at[g]).wait()
        extended[8:, :] = base[...].astype(f32) + lax.dot_general(
            shrunk[0], ups[g], TN, preferred_element_type=f32
        )
        pltpu.make_async_copy(curs.at[g], curs.at[g], chunk_sems.at[g]).wait()
        before = jnp.where(present, curs[g, width:, :].astype(f32), 0.0)
        for k in range(few):
            for part in range(parts):
                extended[8 - few + k:9 - few + k, part * 128:(part + 1) * 128] = (
                    before[k * parts + part:k * parts + part + 1, :]
                )
        from_state = lax.dot_general(curs[g, :width, :], read, NT, preferred_element_type=f32)
        carried[...] = jnp.where(present, from_state, 0.0)

        corner = jnp.zeros((half, half), bf16)
        for pair in range(heads // 2):
            lo, hi = pair * 2 * size, (pair + 1) * 2 * size
            v = channel[taps:taps + 1, lo:hi]
            for k in range(taps):
                first = 8 - few + k
                v = v + channel[k:k + 1, lo:hi] * extended[first:first + length, lo:hi]
            activated = v * (0.5 + 0.5 * jnp.tanh(0.5 * v))
            act = activated.astype(bf16).T
            wide = act.astype(f32)
            sums, early = [], []
            for i in range(2):
                h = 2 * pair + i
                a = act[i * size:(i + 1) * size, :]
                a32 = wide[i * size:(i + 1) * size, :]
                ds = jnp.broadcast_to(column[0, :, h:h + 1], (length, half))
                dt0, dt1 = to_here[h:h + 1, :half], to_here[h:h + 1, half:]
                m0 = jnp.exp2(jnp.minimum(dt0 - ds[:half], 126.0)) * scores[:half]
                m1 = jnp.exp2(jnp.minimum(dt1 - ds[half:], 126.0)) * scores[half:]
                mixing = jnp.concatenate(
                    [
                        jnp.concatenate([m0.astype(bf16), corner], axis=1),
                        jnp.concatenate([corner, m1.astype(bf16)], axis=1),
                    ],
                    axis=0,
                )
                total = jnp.dot(a, mixing, preferred_element_type=f32)
                sums.append(total + carried[h * size:(h + 1) * size, :] * grown[h:h + 1, :])
                weighted[h * size:(h + 1) * size, :] = (a32 * to_end[h:h + 1, :]).astype(bf16)
                early.append((a32[:, :half] * to_middle[h:h + 1, :]).astype(bf16))
            passed = jnp.dot(
                jnp.concatenate(early, axis=0), late_scores, preferred_element_type=f32
            )
            for i in range(2):
                h = 2 * pair + i
                late = passed[i * size:(i + 1) * size, :] * past_middle[h:h + 1, :]
                sums[i] = jnp.concatenate([sums[i][:, :half], sums[i][:, half:] + late], axis=1)
            skipped = channel[taps + 1:taps + 2, lo:hi] * activated
            out[:, lo:hi] = (jnp.concatenate(sums, axis=0).T + skipped).astype(out.dtype)
        fresh = jnp.dot(weighted[...], write, preferred_element_type=f32)
        for h in range(heads):
            rows = slice(h * size, (h + 1) * size)
            old = curs[g, rows, :].astype(f32) * kept[h:h + 1, :]
            old = jnp.where(present, old, 0.0)
            final[0, rows, :] = (fresh[rows, :] + old).astype(final.dtype)


def chunk_shape(cache, conv, width):
    conv_rows = conv.shape[0] * (width // 128)
    return (cache.shape[3] + -(-conv_rows // 16) * 16, cache.shape[4])


def body(
    hidden, base_in_projection, state_input_matrix, state_output_matrix, head_step_size,
    head_decay_rate, head_skip_scale, convolution_weight, convolution_bias, adapter_down_weight,
    adapter_up_weight, adapter_home_group, adapter_group_index, state_space_cache,
    convolution_cache, prefix_holder_device, prefix_cache_slot, prefix_block_count,
):
    groups, devices = lax.axis_size("group"), lax.axis_size("dev")
    tokens, width = base_in_projection.shape
    per_group = tokens // T_REQ
    assert per_group == devices and devices & (devices - 1) == 0 == groups & (groups - 1)
    heads = head_step_size.shape[0]
    size, depth = state_space_cache.shape[2:]
    rank = adapter_down_weight.shape[1]
    taps = convolution_weight.shape[0]
    bf16, f32 = jnp.bfloat16, jnp.float32
    limit = per_group // 2
    lines = devices // 2

    cache = state_space_cache.reshape(
        state_space_cache.shape[0], lines, 2, heads * size, depth
    )
    conv = convolution_cache.transpose(1, 0, 2)
    shape = chunk_shape(cache, conv, width)
    picks = [
        jax.ShapeDtypeStruct((ACAP,) + adapter_down_weight.shape[1:], bf16)
        for _ in range(groups - 1)
    ]
    packed = pl.pallas_call(
        functools.partial(pack_kernel, groups, devices, per_group, width),
        out_shape=(
            jax.ShapeDtypeStruct(META_SHAPE, jnp.int32),
            jax.ShapeDtypeStruct((state_input_matrix.shape[0], 2 * depth), bf16),
            jax.ShapeDtypeStruct((groups, ACAP) + adapter_down_weight.shape[1:], bf16),
            *picks,
            *[jax.ShapeDtypeStruct(shape, bf16) for _ in range(devices)],
            *[jax.ShapeDtypeStruct((lines,) + shape, bf16) for _ in range(2)],
        ),
        in_specs=smem(5) + pinned(3) + vmem(3),
        out_specs=tuple(smem(1) + vmem(2 + len(picks) + devices + 2)),
        scratch_shapes=[
            pltpu.SemaphoreType.DMA((groups * ACAP,)),
            pltpu.SemaphoreType.DMA((groups * ACAP,)),
            pltpu.SemaphoreType.DMA((devices,)),
            pltpu.SemaphoreType.DMA((2,)),
        ],
        cost_estimate=cost(),
        compiler_params=params(),
        name="pack",
    )(
        adapter_home_group.reshape(-1), adapter_group_index, prefix_holder_device.reshape(-1),
        prefix_cache_slot, prefix_block_count, adapter_down_weight, adapter_up_weight, cache,
        state_input_matrix, state_output_matrix, conv,
    )
    meta, rows_mine, packed = packed[0], packed[1], packed[2:]
    down_got = lax.all_to_all(packed[0], "group", split_axis=0, concat_axis=0, tiled=True)
    chunks = packed[groups:-2]
    rows_all = lax.all_gather(rows_mine, "dev", axis=0, tiled=True)
    zero = jnp.zeros((1,), jnp.int32)
    near = near_distances(devices)
    got = [chunks[0]] + [
        lax.ppermute(chunks[d], "dev", [(s, s ^ d) for s in range(devices)])
        for d in range(1, near)
    ]

    spread_others = spread_rest(meta, cache, conv, devices, width, limit)

    up_send, _ = lax.optimization_barrier((packed[1:groups], got[2]))
    up_got = swap(up_send, groups)

    rows_decay, column_decay, channel = pl.pallas_call(
        functools.partial(prep_kernel, per_group),
        out_shape=(
            jax.ShapeDtypeStruct((2 * heads, tokens), f32),
            jax.ShapeDtypeStruct((per_group, T_REQ, heads), f32),
            jax.ShapeDtypeStruct((8, width), f32),
        ),
        in_specs=smem(2) + vmem(3) + anywhere(1),
        out_specs=tuple(pl.BlockSpec(memory_space=pltpu.VMEM) for _ in range(3)),
        cost_estimate=cost(),
        compiler_params=params(),
        name="prep",
    )(
        head_decay_rate, head_skip_scale, head_step_size, convolution_weight,
        convolution_bias.reshape(1, width), meta,
    )

    each = per_group // 2
    early = got[2:]
    partial_down = pl.pallas_call(
        functools.partial(shrink_kernel, per_group),
        grid_spec=pltpu.PrefetchScalarGridSpec(
            num_scalar_prefetch=1,
            grid=(per_group // each,),
            in_specs=[pl.BlockSpec((each * T_REQ, hidden.shape[1]), lambda g, meta: (g, 0))]
            + anywhere(3 + len(early)),
            out_specs=pl.BlockSpec((each, rank, T_REQ), lambda g, meta: (g, 0, 0)),
            scratch_shapes=[
                pltpu.VMEM((per_group,) + adapter_down_weight.shape[1:], bf16),
                pltpu.SemaphoreType.DMA((per_group,)),
            ],
        ),
        out_shape=jax.ShapeDtypeStruct((per_group, rank, T_REQ), bf16),
        cost_estimate=cost(),
        compiler_params=params(),
        name="shrink",
    )(meta, hidden, down_got, channel, spread_others, *early)

    spread = spread_steps(zero, meta, packed[-2:], devices)
    next(spread)
    sent = spread.send([partial_down])

    parts = lax.all_to_all(partial_down, "dev", split_axis=0, concat_axis=0, tiled=True)
    summed = pl.pallas_call(
        sum_kernel,
        out_shape=jax.ShapeDtypeStruct((devices, 1, rank, T_REQ), bf16),
        in_specs=vmem(1) + anywhere(2),
        out_specs=vmem(1)[0],
        cost_estimate=cost(),
        compiler_params=params(),
        name="sum_parts",
    )(parts.reshape(devices, 1, rank, T_REQ), up_got[groups // 2 - 1], sent)
    shrunk = lax.all_to_all(summed, "dev", split_axis=0, concat_axis=0, tiled=True)
    shrunk = shrunk.reshape(per_group, rank, T_REQ)

    late, _ = lax.optimization_barrier((chunks[near:], partial_down))
    got += [
        lax.ppermute(x, "dev", [(s, s ^ d) for s in range(devices)])
        for d, x in zip(range(near, devices), late)
    ]
    for step in range(2, lines - 1):
        sent = spread.send([] if step < lines - 2 else [shrunk])

    outs = None
    for begin, steps in ((0, lines), (lines, lines), (devices, limit)):
        if begin == 0:
            chunks, after = got[:lines], [sent]
        elif begin == lines:
            chunks, after = got[lines:], [spread.send([outs[2]])]
        else:
            chunks, after = [*spread.send([]), spread_others, got[0]], []

        def request(g, meta, begin=begin):
            return meta[POS_REQ, begin + g]

        in_specs = [
            pl.BlockSpec((T_REQ, width), lambda g, meta: (request(g, meta), 0)),
            pl.BlockSpec((1, rank, T_REQ), lambda g, meta: (request(g, meta), 0, 0)),
            pl.BlockSpec((8, width), lambda g, meta: (0, 0)),
            pl.BlockSpec((2 * heads, T_REQ), lambda g, meta: (0, request(g, meta))),
            pl.BlockSpec((1, T_REQ, heads), lambda g, meta: (request(g, meta), 0, 0)),
            pl.BlockSpec((T_REQ, 2 * depth), lambda g, meta: (request(g, meta), 0)),
        ] + anywhere(groups + len(chunks) + len(after))
        operands = [
            meta, base_in_projection, shrunk, channel, rows_decay, column_decay, rows_all,
            adapter_up_weight, *up_got, *chunks, *after,
        ]
        aliases = {}
        if outs is not None:
            aliases = {len(operands): 0, len(operands) + 1: 1}
            operands += list(outs[:2])
            in_specs += anywhere(2)
        outs = pl.pallas_call(
            functools.partial(
                mix_kernel, groups, taps, begin, steps, 0 if begin == devices else lines, size
            ),
            grid_spec=pltpu.PrefetchScalarGridSpec(
                num_scalar_prefetch=1,
                grid=(steps,),
                in_specs=in_specs,
                out_specs=(
                    pl.BlockSpec((T_REQ, width), lambda g, meta: (request(g, meta), 0)),
                    pl.BlockSpec(
                        (1, heads * size, depth), lambda g, meta: (request(g, meta), 0, 0)
                    ),
                    pl.BlockSpec((8, 128), lambda g, meta: (0, 0)),
                ),
                scratch_shapes=[
                    pltpu.VMEM((T_REQ + 8, width), f32),
                    pltpu.VMEM((T_REQ, T_REQ // 2), f32),
                    pltpu.VMEM((width, T_REQ), f32),
                    pltpu.VMEM((width, T_REQ), bf16),
                    pltpu.VMEM((steps,) + adapter_up_weight.shape[1:], bf16),
                    pltpu.VMEM((steps,) + shape, bf16),
                    pltpu.SemaphoreType.DMA((steps,)),
                    pltpu.SemaphoreType.DMA((steps,)),
                ],
            ),
            out_shape=(
                jax.ShapeDtypeStruct((tokens, width), bf16),
                jax.ShapeDtypeStruct((per_group, heads * size, depth), bf16),
                jax.ShapeDtypeStruct((8, 128), f32),
            ),
            input_output_aliases=aliases,
            cost_estimate=cost(),
            compiler_params=params(),
            name=f"mix_{begin}",
        )(*operands)
    return outs[0], outs[1].reshape(per_group, heads, size, depth)


def solution(mesh):
    placed = (
        P("group", "dev"),
        P("group", "dev"),
        P(("group", "dev"), None),
        P(("group", "dev"), None),
        P("dev", "group"),
        P("dev"),
        P("dev"),
        P(None, "dev"),
        P("dev"),
        P("group", None, "dev"),
        P("group", None, "dev"),
        P(),
        P(),
        P(("group", "dev"), None, None, None),
        P(("group", "dev"), None, None),
        P(),
        P(),
        P(),
    )
    return jax.shard_map(
        body,
        mesh=mesh,
        in_specs=placed,
        out_specs=(P("group", "dev"), P("group", "dev", None, None)),
        check_vma=False,
    )
```

```python
import functools
import math

import jax
import jax.numpy as jnp
from jax import lax
from jax.experimental import pallas as pl
from jax.experimental.pallas import tpu as pltpu
from jax.sharding import PartitionSpec as P

T_REQ = 256
CAP = 2
ACAP = 4
LOG2E = math.log2(math.e)
NT = (((1,), (1,)), ((), ()))
TN = (((0,), (0,)), ((), ()))
VMEM_LIMIT = 63 * 1024 * 1024

HOME, DIST, ARANK, AINDEX, PRESENT, POS_REQ, POS_VALID, OSLOT, OHOLDER, MISC, SEND = range(11)
MOST, ME, SLOT = range(3)
META_SHAPE = (16, 64)


def cost():
    return pl.CostEstimate(flops=0, bytes_accessed=1 << 16, transcendentals=0)


def params():
    return pltpu.CompilerParams(vmem_limit_bytes=VMEM_LIMIT)


def smem(count):
    return [pl.BlockSpec(memory_space=pltpu.SMEM) for _ in range(count)]


def vmem(count):
    return [pl.BlockSpec(memory_space=pltpu.VMEM) for _ in range(count)]


def pinned(count):
    return [pl.BlockSpec(memory_space=pltpu.HBM) for _ in range(count)]


def anywhere(count):
    return [pl.BlockSpec(memory_space=pl.ANY) for _ in range(count)]


def as_int(flag):
    return flag.astype(jnp.int32)


def ranks_of(labels):
    ranks = []
    for q, label in enumerate(labels):
        total = jnp.int32(0)
        for other in labels[:q]:
            total = total + as_int(other == label)
        ranks.append(total)
    return ranks


def plan(groups, devices, per_group, home, index, holder, slot, blocks, meta):
    my_group = lax.axis_index("group")
    me = lax.axis_index("dev")
    first = my_group * per_group
    limit = per_group // 2
    for j in range(limit):
        meta[POS_REQ, devices + j] = jnp.int32(-1)
        meta[POS_VALID, devices + j] = jnp.int32(0)
        meta[OSLOT, j] = jnp.int32(0)
        meta[OHOLDER, j] = jnp.int32(0)

    homes = [home[first + q] for q in range(per_group)]
    for q, rank in enumerate(ranks_of(homes)):
        meta[HOME, q] = homes[q]
        meta[DIST, q] = lax.bitwise_xor(homes[q], my_group)
        meta[ARANK, q] = rank
        meta[AINDEX, q] = index[first + q]
        meta[PRESENT, q] = as_int(blocks[first + q] > 0)
    for k in range(groups):
        theirs = lax.bitwise_xor(my_group, k) * per_group
        seen = jnp.int32(0)
        chosen = [jnp.int32(0) for _ in range(ACAP)]
        for q in range(per_group):
            hit = home[theirs + q] == my_group
            value = index[theirs + q]
            for c in range(ACAP):
                chosen[c] = jnp.where(hit & (seen == c), value, chosen[c])
            seen = seen + as_int(hit)
        for c in range(ACAP):
            meta[SEND, k * ACAP + c] = chosen[c]

    holders = [holder[first + q] for q in range(per_group)]
    ranks = ranks_of(holders)
    count = jnp.int32(0)
    my_slot = jnp.int32(0)
    for q in range(per_group):
        my_slot = jnp.where((holders[q] == me) & (ranks[q] == 0), slot[first + q], my_slot)

        @pl.when(ranks[q] > 0)
        def _():
            meta[POS_REQ, devices + count] = jnp.int32(q)
            meta[POS_VALID, devices + count] = jnp.int32(1)
            meta[OSLOT, count] = slot[first + q]
            meta[OHOLDER, count] = holders[q]

        count = count + as_int(ranks[q] > 0)
    spread = meta[POS_REQ, devices]
    requests = []
    for d in range(devices):
        source = lax.bitwise_xor(me, d)
        request = jnp.int32(-1)
        for q in range(per_group):
            request = jnp.where((holders[q] == source) & (ranks[q] == 0), q, request)
        meta[POS_VALID, d] = as_int(request >= 0)
        requests.append(request)
    requests += [meta[POS_REQ, devices + j] for j in range(limit)]
    for begin, end in ((0, devices // 2), (devices // 2, devices + limit)):
        last = jnp.int32(-1)
        filled = []
        for p in range(begin, end):
            last = jnp.where(requests[p] >= 0, requests[p], last)
            filled.append(last)
        following = jnp.maximum(spread, 0)
        for p in reversed(range(begin, end)):
            following = jnp.where(filled[p - begin] >= 0, filled[p - begin], following)
            meta[POS_REQ, p] = following
    most = jnp.int32(0)
    for g in range(groups):
        labels = [holder[g * per_group + q] for q in range(per_group)]
        total = jnp.int32(0)
        for rank in ranks_of(labels):
            total = total + as_int(rank > 0)
        most = jnp.maximum(most, total)
    meta[MISC, MOST] = most
    meta[MISC, ME] = me
    meta[MISC, SLOT] = my_slot


def start_adapters(groups, meta, table, outs, sems):
    copies = []
    for k in reversed(range(groups) if len(outs) == 1 else range(1, groups)):
        for c in range(ACAP):
            chosen = meta[SEND, k * ACAP + c]
            if len(outs) == 1:
                out = outs[0].at[lax.bitwise_xor(lax.axis_index("group"), k), c]
            else:
                out = outs[k - 1].at[c]
            copy = pltpu.make_async_copy(table.at[chosen], out, sems.at[k * ACAP + c])
            copy.start()
            copies.append(copy)
    return copies


def swap(packed, groups):
    return [
        lax.ppermute(packed[k - 1], "group", [(g, g ^ k) for g in range(groups)])
        for k in range(1, groups)
    ]


def copy_conv(conv, slot, target, width, out, at):
    parts = width // 128
    begin = pl.multiple_of(target * width, 128)
    for k in range(conv.shape[0]):
        rows = conv[k, :, pl.ds(begin, width)]
        row = rows[:1, :]
        for c in range(1, conv.shape[1]):
            row = jnp.where(slot == c, rows[c:c + 1, :], row)
        for part in range(parts):
            place = at + k * parts + part
            out[place:place + 1, :] = row[:, part * 128:(part + 1) * 128]


def start_state(devices, meta, cache, outs, sems):
    copies = []
    for d in reversed(range(devices)):
        target = lax.bitwise_xor(meta[MISC, ME], d)
        copy = pltpu.make_async_copy(
            cache.at[meta[MISC, SLOT], target // 2, target % 2],
            outs[d].at[pl.ds(0, cache.shape[3])], sems.at[d],
        )
        copy.start()
        copies.append(copy)
    return copies


def start_across(j, meta, cache, across, own, sems):
    x = meta[MISC, ME] % 2
    copies = []
    for k, (out, place) in enumerate(((across, 1 - x), (own, x))):
        copy = pltpu.make_async_copy(
            cache.at[meta[OSLOT, j], :, place], out.at[:, pl.ds(0, cache.shape[3])], sems.at[k]
        )
        copy.start()
        copies.append(copy)
    return copies


def conv_across(lines, width, j, meta, conv, state_rows, across, own):
    x = meta[MISC, ME] % 2
    for out, place in ((across, 1 - x), (own, x)):
        for m in range(lines):
            copy_conv(conv, meta[OSLOT, j], 2 * m + place, width, out.at[m], state_rows)


def pack_kernel(
    groups, devices, per_group, width, home, index, holder, slot, blocks, down, up, cache, write,
    read, conv, meta, rows_out, *rest
):
    downs, rest = rest[:1], rest[1:]
    ups, rest = rest[:groups - 1], rest[groups - 1:]
    chunks, (across, own, down_sems, up_sems, chunk_sems, across_sems) = (
        rest[:devices], rest[devices:]
    )
    plan(groups, devices, per_group, home, index, holder, slot, blocks, meta)
    copies = start_adapters(groups, meta, down, downs, down_sems)
    copies += start_state(devices, meta, cache, chunks, chunk_sems)
    copies += start_across(0, meta, cache, across, own, across_sems)
    copies += start_adapters(groups, meta, up, ups, up_sems)
    depth = write.shape[1]
    rows_out[:, :depth] = write[...]
    rows_out[:, depth:] = read[...]
    state_rows = cache.shape[3]
    for d in range(devices):
        target = lax.bitwise_xor(meta[MISC, ME], d)
        copy_conv(conv, meta[MISC, SLOT], target, width, chunks[d], state_rows)
    conv_across(devices // 2, width, 0, meta, conv, state_rows, across, own)
    for copy in copies:
        copy.wait()


def pack_across_kernel(lines, width, j, meta, cache, conv, across, own, sems):
    copies = start_across(j[0], meta, cache, across, own, sems)
    conv_across(lines, width, j[0], meta, conv, cache.shape[3], across, own)
    for copy in copies:
        copy.wait()


def pick_kernel(step, lines, j, meta, own, over, *rest):
    out_r, out_l, sems = rest[-3:]
    me = meta[MISC, ME]
    source = meta[OHOLDER, j[0]]
    same = source // 2 == me // 2
    mine = same & (source % 2 == me % 2)
    across = same & (source % 2 != me % 2)
    for k, (out, block) in enumerate(((out_r, right_block), (out_l, left_block))):
        place = block(meta, step, lines)

        @pl.when(mine)
        def _(k=k, out=out, place=place):
            pltpu.make_async_copy(own.at[place], out, sems.at[k]).start()

        @pl.when(across)
        def _(k=k, out=out, place=place):
            pltpu.make_async_copy(over.at[place], out, sems.at[k]).start()

        if step > 1:
            @pl.when(jnp.logical_not(same))
            def _(k=k, out=out):
                pltpu.make_async_copy(rest[k], out, sems.at[k]).start()

    for k, out in enumerate((out_r, out_l)):
        if step > 1:
            pltpu.make_async_copy(own.at[0], out, sems.at[k]).wait()
        else:
            @pl.when(same)
            def _(k=k, out=out):
                pltpu.make_async_copy(own.at[0], out, sems.at[k]).wait()


def right_block(meta, step, lines):
    return jnp.clip(lines + meta[MISC, ME] // 2 - step, 0, lines - 1)


def left_block(meta, step, lines):
    return jnp.clip(meta[MISC, ME] // 2 + step - lines, 0, lines - 1)


def pack_across(j, meta, cache, conv, devices, width):
    lines = devices // 2
    shape = chunk_shape(cache, conv, width)
    return pl.pallas_call(
        functools.partial(pack_across_kernel, lines, width),
        out_shape=tuple(jax.ShapeDtypeStruct((lines,) + shape, cache.dtype) for _ in range(2)),
        in_specs=smem(2) + pinned(1) + vmem(1),
        out_specs=tuple(vmem(2)),
        scratch_shapes=[pltpu.SemaphoreType.DMA((2,))],
        cost_estimate=cost(),
        compiler_params=params(),
        name="pack_across",
    )(j, meta, cache, conv)


def spread_steps(j, meta, packed, devices):
    lines = devices // 2
    send, own = packed
    shape = own.shape[1:]
    across = lax.ppermute(send, "dev", [(d, d ^ 1) for d in range(devices)])
    from_left = from_right = None
    after = yield across
    for step in range(1, lines):
        operands = [own, across]
        if step > 1:
            operands += [from_left, from_right]
        operands += after
        to_right, to_left = pl.pallas_call(
            functools.partial(pick_kernel, step, lines),
            in_specs=smem(2) + anywhere(len(operands)),
            out_specs=tuple(vmem(2)),
            out_shape=tuple(jax.ShapeDtypeStruct(shape, own.dtype) for _ in range(2)),
            scratch_shapes=[pltpu.SemaphoreType.DMA((2,))],
            cost_estimate=cost(),
            compiler_params=params(),
            name=f"pick_{step}",
        )(j, meta, *operands)
        from_left = lax.ppermute(
            to_right, "dev",
            [(2 * i + x, 2 * i + 2 + x) for i in range(step) for x in range(2)],
        )
        from_right = lax.ppermute(
            to_left, "dev",
            [(devices - 1 - (2 * i + x), devices - 3 - (2 * i + x))
             for i in range(step) for x in range(2)],
        )
        after = yield to_right
    yield own, across, from_left, from_right


def final_specs(shape):
    line = pl.BlockSpec((1,) + shape, lambda g, j, meta: (meta[MISC, ME] // 2, 0, 0))
    whole = pl.BlockSpec(shape, lambda g, j, meta: (0, 0))
    return [line, line, whole, whole]


def which_candidate(meta, source):
    me = meta[MISC, ME]
    same = source // 2 == me // 2
    mine = same & (source % 2 == me % 2)
    return jnp.where(mine, 0, jnp.where(same, 1, jnp.where(source // 2 < me // 2, 2, 3)))


def final_kernel(j, meta, own, across, from_left, from_right, out):
    which = which_candidate(meta, meta[OHOLDER, j[0]])
    picks = (own.at[0], across.at[0], from_left, from_right)
    for k, pick in enumerate(picks):
        @pl.when(which == k)
        def _(pick=pick):
            out[...] = pick[...]


def spread_rest(meta, cache, conv, devices, width, limit):
    shape = chunk_shape(cache, conv, width)

    def one(j, held):
        jj = j.reshape(1)
        packed = pack_across(jj, meta, cache, conv, devices, width)
        steps = spread_steps(jj, meta, packed, devices)
        next(steps)
        for _ in range(devices // 2):
            got = steps.send([])
        block = pl.pallas_call(
            final_kernel,
            grid_spec=pltpu.PrefetchScalarGridSpec(
                num_scalar_prefetch=2,
                grid=(1,),
                in_specs=final_specs(shape),
                out_specs=pl.BlockSpec(shape, lambda g, j, meta: (0, 0)),
            ),
            out_shape=jax.ShapeDtypeStruct(shape, cache.dtype),
            compiler_params=params(),
            name="final_pick",
        )(jj, meta, *got)
        return lax.dynamic_update_slice_in_dim(held, block[None], j - 1, 0)

    held = jnp.zeros((limit - 1,) + shape, cache.dtype)
    return lax.fori_loop(jnp.int32(1), meta[MISC, MOST], one, held)


def fetch_table(groups, meta, r, tables, out, sem):
    dist = meta[DIST, r]
    for k in range(groups):
        row = meta[ARANK, r] if k else meta[AINDEX, r]

        @pl.when(dist == k)
        def _(k=k, row=row):
            pltpu.make_async_copy(tables[k].at[row], out, sem).start()


def shrink_kernel(per_group, meta, hidden, table, *rest):
    out, picked, sems = rest[-3:]
    g = pl.program_id(0)
    each = out.shape[0]

    @pl.when(g == 0)
    def _():
        for r in range(per_group):
            pltpu.make_async_copy(
                table.at[meta[HOME, r], meta[ARANK, r]], picked.at[r], sems.at[r]
            ).start()

    for i in range(each):
        r = g * each + i
        pltpu.make_async_copy(table.at[0, 0], picked.at[r], sems.at[r]).wait()
    for i in range(each):
        part = lax.dot_general(
            hidden[i * T_REQ:(i + 1) * T_REQ, :], picked[g * each + i], NT,
            preferred_element_type=jnp.float32,
        )
        out[i] = part.T.astype(out.dtype)


def sum_kernel(parts, *rest):
    out = rest[-1]
    total = parts[0].astype(jnp.float32)
    for k in range(1, parts.shape[0]):
        total = total + parts[k].astype(jnp.float32)
    total = total.astype(out.dtype)
    for k in range(out.shape[0]):
        out[k] = total


def prep_kernel(per_group, rates, skips, steps, taps_in, bias, *rest):
    rows_out, column_out, channel = rest[-3:]
    heads, tokens = steps.shape
    length = tokens // per_group
    rate = jnp.zeros((heads, length), jnp.float32)
    place = lax.broadcasted_iota(jnp.int32, rate.shape, 0)
    for h in range(heads):
        rate = jnp.where(place == h, rates[h] * (-LOG2E), rate)
    step = [steps[:, r * length:(r + 1) * length] for r in range(per_group)]
    x = jnp.concatenate([part * rate for part in step], axis=0)
    high = x.astype(jnp.bfloat16)
    rest = x - high.astype(jnp.float32)
    middle = rest.astype(jnp.bfloat16)
    low = (rest - middle.astype(jnp.float32)).astype(jnp.bfloat16)
    s = lax.broadcasted_iota(jnp.int32, (length, length), 0)
    t = lax.broadcasted_iota(jnp.int32, (length, length), 1)
    ones = (s <= t).astype(jnp.float32).astype(jnp.bfloat16)
    total = jnp.dot(low, ones, preferred_element_type=jnp.float32)
    total = total + jnp.dot(middle, ones, preferred_element_type=jnp.float32)
    total = total + jnp.dot(high, ones, preferred_element_type=jnp.float32)
    shifted = total - jnp.log2(jnp.concatenate(step, axis=0))
    columns = shifted.T
    for r in range(per_group):
        rows_out[:heads, r * length:(r + 1) * length] = total[r * heads:(r + 1) * heads]
        rows_out[heads:, r * length:(r + 1) * length] = shifted[r * heads:(r + 1) * heads]
        column_out[r] = columns[:, r * heads:(r + 1) * heads]
    taps, width = taps_in.shape
    head_of = lax.broadcasted_iota(jnp.int32, (1, width), 1) // (width // heads)
    skip = jnp.zeros((1, width), jnp.float32)
    for h in range(heads):
        skip = jnp.where(head_of == h, skips[h], skip)
    channel[:taps] = taps_in[...]
    channel[taps:taps + 1] = bias[...]
    channel[taps + 1:taps + 2] = skip


def mix_kernel(
    groups, taps, begin, steps, direct, size, meta, base, shrunk, channel, rows_decay, column,
    rows_in, *rest
):
    tables, chunks = rest[:groups], rest[groups:]
    out, final, extended, scores, carried, weighted, ups, curs, table_sems, chunk_sems = (
        rest[-10:]
    )
    g = pl.program_id(0)
    position = begin + g
    r = meta[POS_REQ, position]
    length, width = base.shape
    half = length // 2
    heads = width // size
    depth = curs.shape[2]
    few = taps - 1
    parts = width // 128
    f32, bf16 = jnp.float32, jnp.bfloat16

    def fetch_chunk(source, i):
        pltpu.make_async_copy(source, curs.at[i], chunk_sems.at[i]).start()

    @pl.when(g == 0)
    def _():
        for i in range(steps):
            @pl.when(meta[POS_VALID, begin + i] > 0)
            def _(i=i):
                request = meta[POS_REQ, begin + i]
                fetch_table(groups, meta, request, tables, ups.at[i], table_sems.at[i])
                if i < direct:
                    fetch_chunk(chunks[i], i)
                elif i > direct:
                    fetch_chunk(chunks[direct + 4].at[i - direct - 1], i)
                else:
                    line = meta[MISC, ME] // 2
                    own, across, from_left, from_right = chunks[direct:direct + 4]
                    candidates = [own.at[line], across.at[line], from_left, from_right]
                    which = which_candidate(meta, meta[OHOLDER, 0])
                    for k, candidate in enumerate(candidates):
                        @pl.when(which == k)
                        def _(candidate=candidate):
                            fetch_chunk(candidate, direct)

    @pl.when(meta[POS_VALID, position] > 0)
    def _():
        present = meta[PRESENT, r] > 0
        write, read = rows_in[:, :depth], rows_in[:, depth:]
        all_scores = lax.dot_general(write, read, NT, preferred_element_type=f32)
        s = lax.broadcasted_iota(jnp.int32, (half, half), 0)
        t = lax.broadcasted_iota(jnp.int32, (half, half), 1)
        scores[:half] = jnp.where(s <= t, all_scores[:half, :half], 0.0)
        scores[half:] = jnp.where(s <= t, all_scores[half:, half:], 0.0)
        late_scores = all_scores[:half, half:].astype(bf16)

        to_here, from_here = rows_decay[:heads, :], rows_decay[heads:, :]
        end = jnp.broadcast_to(to_here[:, length - 1:length], (heads, length))
        middle = jnp.broadcast_to(to_here[:, half - 1:half], (heads, half))
        grown = jnp.exp2(to_here)
        to_end = jnp.exp2(end - from_here)
        to_middle = jnp.exp2(middle - from_here[:, :half])
        past_middle = jnp.exp2(to_here[:, half:] - middle)
        kept = jnp.exp2(end[:, :depth])

        pltpu.make_async_copy(tables[0].at[0], ups.at[g], table_sems.at[g]).wait()
        extended[8:, :] = base[...].astype(f32) + lax.dot_general(
            shrunk[0], ups[g], TN, preferred_element_type=f32
        )
        pltpu.make_async_copy(curs.at[g], curs.at[g], chunk_sems.at[g]).wait()
        before = jnp.where(present, curs[g, width:, :].astype(f32), 0.0)
        for k in range(few):
            for part in range(parts):
                extended[8 - few + k:9 - few + k, part * 128:(part + 1) * 128] = (
                    before[k * parts + part:k * parts + part + 1, :]
                )
        from_state = lax.dot_general(curs[g, :width, :], read, NT, preferred_element_type=f32)
        carried[...] = jnp.where(present, from_state, 0.0)

        corner = jnp.zeros((half, half), bf16)
        for pair in range(heads // 2):
            lo, hi = pair * 2 * size, (pair + 1) * 2 * size
            v = channel[taps:taps + 1, lo:hi]
            for k in range(taps):
                first = 8 - few + k
                v = v + channel[k:k + 1, lo:hi] * extended[first:first + length, lo:hi]
            activated = v * (0.5 + 0.5 * jnp.tanh(0.5 * v))
            act = activated.astype(bf16).T
            wide = act.astype(f32)
            sums, early = [], []
            for i in range(2):
                h = 2 * pair + i
                a = act[i * size:(i + 1) * size, :]
                a32 = wide[i * size:(i + 1) * size, :]
                ds = jnp.broadcast_to(column[0, :, h:h + 1], (length, half))
                dt0, dt1 = to_here[h:h + 1, :half], to_here[h:h + 1, half:]
                m0 = jnp.exp2(jnp.minimum(dt0 - ds[:half], 126.0)) * scores[:half]
                m1 = jnp.exp2(jnp.minimum(dt1 - ds[half:], 126.0)) * scores[half:]
                mixing = jnp.concatenate(
                    [
                        jnp.concatenate([m0.astype(bf16), corner], axis=1),
                        jnp.concatenate([corner, m1.astype(bf16)], axis=1),
                    ],
                    axis=0,
                )
                total = jnp.dot(a, mixing, preferred_element_type=f32)
                sums.append(total + carried[h * size:(h + 1) * size, :] * grown[h:h + 1, :])
                weighted[h * size:(h + 1) * size, :] = (a32 * to_end[h:h + 1, :]).astype(bf16)
                early.append((a32[:, :half] * to_middle[h:h + 1, :]).astype(bf16))
            passed = jnp.dot(
                jnp.concatenate(early, axis=0), late_scores, preferred_element_type=f32
            )
            for i in range(2):
                h = 2 * pair + i
                late = passed[i * size:(i + 1) * size, :] * past_middle[h:h + 1, :]
                sums[i] = jnp.concatenate([sums[i][:, :half], sums[i][:, half:] + late], axis=1)
            skipped = channel[taps + 1:taps + 2, lo:hi] * activated
            out[:, lo:hi] = (jnp.concatenate(sums, axis=0).T + skipped).astype(out.dtype)
        fresh = jnp.dot(weighted[...], write, preferred_element_type=f32)
        for h in range(heads):
            rows = slice(h * size, (h + 1) * size)
            old = curs[g, rows, :].astype(f32) * kept[h:h + 1, :]
            old = jnp.where(present, old, 0.0)
            final[0, rows, :] = (fresh[rows, :] + old).astype(final.dtype)


def chunk_shape(cache, conv, width):
    conv_rows = conv.shape[0] * (width // 128)
    return (cache.shape[3] + -(-conv_rows // 16) * 16, cache.shape[4])


def body(
    hidden, base_in_projection, state_input_matrix, state_output_matrix, head_step_size,
    head_decay_rate, head_skip_scale, convolution_weight, convolution_bias, adapter_down_weight,
    adapter_up_weight, adapter_home_group, adapter_group_index, state_space_cache,
    convolution_cache, prefix_holder_device, prefix_cache_slot, prefix_block_count,
):
    groups, devices = lax.axis_size("group"), lax.axis_size("dev")
    tokens, width = base_in_projection.shape
    per_group = tokens // T_REQ
    assert per_group == devices and devices & (devices - 1) == 0 == groups & (groups - 1)
    heads = head_step_size.shape[0]
    size, depth = state_space_cache.shape[2:]
    rank = adapter_down_weight.shape[1]
    taps = convolution_weight.shape[0]
    bf16, f32 = jnp.bfloat16, jnp.float32
    limit = per_group // 2
    lines = devices // 2

    cache = state_space_cache.reshape(
        state_space_cache.shape[0], lines, 2, heads * size, depth
    )
    conv = convolution_cache.transpose(1, 0, 2)
    shape = chunk_shape(cache, conv, width)
    picks = [
        jax.ShapeDtypeStruct((ACAP,) + adapter_down_weight.shape[1:], bf16)
        for _ in range(groups - 1)
    ]
    packed = pl.pallas_call(
        functools.partial(pack_kernel, groups, devices, per_group, width),
        out_shape=(
            jax.ShapeDtypeStruct(META_SHAPE, jnp.int32),
            jax.ShapeDtypeStruct((state_input_matrix.shape[0], 2 * depth), bf16),
            jax.ShapeDtypeStruct((groups, ACAP) + adapter_down_weight.shape[1:], bf16),
            *picks,
            *[jax.ShapeDtypeStruct(shape, bf16) for _ in range(devices)],
            *[jax.ShapeDtypeStruct((lines,) + shape, bf16) for _ in range(2)],
        ),
        in_specs=smem(5) + pinned(3) + vmem(3),
        out_specs=tuple(smem(1) + vmem(2 + len(picks) + devices + 2)),
        scratch_shapes=[
            pltpu.SemaphoreType.DMA((groups * ACAP,)),
            pltpu.SemaphoreType.DMA((groups * ACAP,)),
            pltpu.SemaphoreType.DMA((devices,)),
            pltpu.SemaphoreType.DMA((2,)),
        ],
        cost_estimate=cost(),
        compiler_params=params(),
        name="pack",
    )(
        adapter_home_group.reshape(-1), adapter_group_index, prefix_holder_device.reshape(-1),
        prefix_cache_slot, prefix_block_count, adapter_down_weight, adapter_up_weight, cache,
        state_input_matrix, state_output_matrix, conv,
    )
    meta, rows_mine, packed = packed[0], packed[1], packed[2:]
    down_got = lax.all_to_all(packed[0], "group", split_axis=0, concat_axis=0, tiled=True)
    chunks = packed[groups:-2]
    rows_all = lax.all_gather(rows_mine, "dev", axis=0, tiled=True)
    zero = jnp.zeros((1,), jnp.int32)
    got = [chunks[0]] + [
        lax.ppermute(chunks[d], "dev", [(s, s ^ d) for s in range(devices)])
        for d in range(1, devices)
    ]

    spread_others = spread_rest(meta, cache, conv, devices, width, limit)

    up_send, _ = lax.optimization_barrier((packed[1:groups], got[lines]))
    up_got = swap(up_send, groups)

    rows_decay, column_decay, channel = pl.pallas_call(
        functools.partial(prep_kernel, per_group),
        out_shape=(
            jax.ShapeDtypeStruct((2 * heads, tokens), f32),
            jax.ShapeDtypeStruct((per_group, T_REQ, heads), f32),
            jax.ShapeDtypeStruct((8, width), f32),
        ),
        in_specs=smem(2) + vmem(3) + anywhere(1),
        out_specs=tuple(pl.BlockSpec(memory_space=pltpu.VMEM) for _ in range(3)),
        cost_estimate=cost(),
        compiler_params=params(),
        name="prep",
    )(
        head_decay_rate, head_skip_scale, head_step_size, convolution_weight,
        convolution_bias.reshape(1, width), meta,
    )

    each = per_group // 2
    partial_down = pl.pallas_call(
        functools.partial(shrink_kernel, per_group),
        grid_spec=pltpu.PrefetchScalarGridSpec(
            num_scalar_prefetch=1,
            grid=(per_group // each,),
            in_specs=[pl.BlockSpec((each * T_REQ, hidden.shape[1]), lambda g, meta: (g, 0))]
            + anywhere(4),
            out_specs=pl.BlockSpec((each, rank, T_REQ), lambda g, meta: (g, 0, 0)),
            scratch_shapes=[
                pltpu.VMEM((per_group,) + adapter_down_weight.shape[1:], bf16),
                pltpu.SemaphoreType.DMA((per_group,)),
            ],
        ),
        out_shape=jax.ShapeDtypeStruct((per_group, rank, T_REQ), bf16),
        cost_estimate=cost(),
        compiler_params=params(),
        name="shrink",
    )(meta, hidden, down_got, channel, got[lines], spread_others)

    parts = lax.all_to_all(partial_down, "dev", split_axis=0, concat_axis=0, tiled=True)
    summed = pl.pallas_call(
        sum_kernel,
        out_shape=jax.ShapeDtypeStruct((devices, 1, rank, T_REQ), bf16),
        in_specs=vmem(1),
        out_specs=vmem(1)[0],
        cost_estimate=cost(),
        compiler_params=params(),
        name="sum_parts",
    )(parts.reshape(devices, 1, rank, T_REQ))
    shrunk = lax.all_to_all(summed, "dev", split_axis=0, concat_axis=0, tiled=True)
    shrunk = shrunk.reshape(per_group, rank, T_REQ)

    befores = [[partial_down, got[lines + 1]], [summed, up_got[groups // 2 - 1]], [rows_all, up_got[-1]]]
    spread = spread_steps(zero, meta, packed[-2:], devices)
    next(spread)
    for step in range(1, lines):
        sent = spread.send(befores.pop(0) if befores else [])
    spread = spread.send([])

    outs = None
    for begin, steps in ((0, lines), (lines, devices - lines + limit)):
        if begin == 0:
            chunks, after = got[:lines], [sent, got[lines + 2], got[lines + 3]]
        else:
            chunks, after = [*got[lines:], *spread, spread_others], []

        def request(g, meta, begin=begin):
            return meta[POS_REQ, begin + g]

        in_specs = [
            pl.BlockSpec((T_REQ, width), lambda g, meta: (request(g, meta), 0)),
            pl.BlockSpec((1, rank, T_REQ), lambda g, meta: (request(g, meta), 0, 0)),
            pl.BlockSpec((8, width), lambda g, meta: (0, 0)),
            pl.BlockSpec((2 * heads, T_REQ), lambda g, meta: (0, request(g, meta))),
            pl.BlockSpec((1, T_REQ, heads), lambda g, meta: (request(g, meta), 0, 0)),
            pl.BlockSpec((T_REQ, 2 * depth), lambda g, meta: (request(g, meta), 0)),
        ] + anywhere(groups + len(chunks) + len(after))
        operands = [
            meta, base_in_projection, shrunk, channel, rows_decay, column_decay, rows_all,
            adapter_up_weight, *up_got, *chunks, *after,
        ]
        aliases = {}
        if outs is not None:
            aliases = {len(operands): 0, len(operands) + 1: 1}
            operands += list(outs)
            in_specs += anywhere(2)
        outs = pl.pallas_call(
            functools.partial(mix_kernel, groups, taps, begin, steps, lines, size),
            grid_spec=pltpu.PrefetchScalarGridSpec(
                num_scalar_prefetch=1,
                grid=(steps,),
                in_specs=in_specs,
                out_specs=(
                    pl.BlockSpec((T_REQ, width), lambda g, meta: (request(g, meta), 0)),
                    pl.BlockSpec(
                        (1, heads * size, depth), lambda g, meta: (request(g, meta), 0, 0)
                    ),
                ),
                scratch_shapes=[
                    pltpu.VMEM((T_REQ + 8, width), f32),
                    pltpu.VMEM((T_REQ, T_REQ // 2), f32),
                    pltpu.VMEM((width, T_REQ), f32),
                    pltpu.VMEM((width, T_REQ), bf16),
                    pltpu.VMEM((steps,) + adapter_up_weight.shape[1:], bf16),
                    pltpu.VMEM((steps,) + shape, bf16),
                    pltpu.SemaphoreType.DMA((steps,)),
                    pltpu.SemaphoreType.DMA((steps,)),
                ],
            ),
            out_shape=(
                jax.ShapeDtypeStruct((tokens, width), bf16),
                jax.ShapeDtypeStruct((per_group, heads * size, depth), bf16),
            ),
            input_output_aliases=aliases,
            cost_estimate=cost(),
            compiler_params=params(),
            name=f"mix_{begin}",
        )(*operands)
    return outs[0], outs[1].reshape(per_group, heads, size, depth)


def solution(mesh):
    placed = (
        P("group", "dev"),
        P("group", "dev"),
        P(("group", "dev"), None),
        P(("group", "dev"), None),
        P("dev", "group"),
        P("dev"),
        P("dev"),
        P(None, "dev"),
        P("dev"),
        P("group", None, "dev"),
        P("group", None, "dev"),
        P(),
        P(),
        P(("group", "dev"), None, None, None),
        P(("group", "dev"), None, None),
        P(),
        P(),
        P(),
    )
    return jax.shard_map(
        body,
        mesh=mesh,
        in_specs=placed,
        out_specs=(P("group", "dev"), P("group", "dev", None, None)),
        check_vma=False,
    )
```
